128 devices in a mesh: gx: 8 (over y, core), gy: 16 (over x, z).
Axes of the slice: x: 4, y: 4, z: 4, core: 2. Of those that a mesh axis runs over, the one named last changes fastest.
Arguments:
- source_blocks: bfloat16 [4096, 128, 128], P(('gx', 'gy')), may hold values from -8 to 8
- block_scale: float32 [4096], P(('gx', 'gy')), may hold values from 0.5 to 4
- block_list: int32 [128, 36], replicated, may hold values from 0 to 4095, as said below
- block_count: int32 [128], replicated, may hold values from 27 to 36, as said below
- row_weights: bfloat16 [4608, 128, 128], P(('gx', 'gy')), may hold values from -1 to 1.2
- col_weights: bfloat16 [4608, 128, 128], P(('gx', 'gy')), may hold values from -1 to 1.2
Outputs:
- relief: float32 [12288, 6144], P('gy', 'gx')
- slope_factor: float32 [12288, 6144], P('gy', 'gx')
- flow: bfloat16 [8, 12288, 6144], P(None, 'gy', 'gx')
The draws below stay inside these ranges and needn't reach their ends.
Inputs may be any that keep to these rules, and one draw needn't show every extreme that they name: `block_list`: every block named in row t is held by a tile of the same gx index as t (holder of b is b // 32). Among the first block_count[t] entries of row t, at most 4 name blocks of one holder; every row reaches 4 for some holder. Entries past the count are valid block numbers and are ignored. `block_count`: some output tile has exactly 36 live windows.
All inputs are finite; a program needn't handle non-finite values.
Results may differ from the reference program's by a relative error of at most 0.03.
Values may be sent and summed in bfloat16 or wider, within the bound.
No kernel may reach another device: no remote copies, remote signals or barrier semaphores. Data moves between devices by JAX's collectives and lax.ppermute only.
A program may use at most 128 MiB of HBM per device.

```python
import math
import jax
import jax.numpy as jnp
from jax import lax

BS = 128
W = 6
NB = 32
K = 36
R = 768
C = 768
CAP = 4
NR = 12288
NC = 6144
N_GX = 8
N_GY = 16
DEVICES = 128


def keys_weight(dist):
    inner = (1.5 * dist - 2.5) * dist * dist + 1.0
    outer = ((-0.5 * dist + 2.5) * dist - 4.0) * dist + 2.0
    return jnp.where(dist < 1.0, inner, jnp.where(dist < 2.0, outer, 0.0))


def routing(key):
    first, second, third = jax.random.split(key, 3)
    perms = jax.vmap(lambda sub: jax.random.permutation(sub, N_GY))(jax.random.split(first, DEVICES))
    groups = (K + CAP - 1) // CAP
    slot = jnp.arange(K)
    column = jnp.arange(DEVICES) // N_GY
    holder = column[:, None] * N_GY + perms[:, slot // CAP]
    base = jax.random.randint(second, (DEVICES, groups), 0, NB)
    local_index = (base[:, slot // CAP] + slot % CAP) % NB
    ids = (holder * NB + local_index).astype(jnp.int32)
    short = jax.random.randint(third, (DEVICES,), 0, K // 4 + 1)
    counts = K - short
    chosen = jax.random.randint(jax.random.fold_in(key, 7), (), 0, DEVICES)
    counts = jnp.where(jnp.arange(DEVICES) == chosen, K, counts).astype(jnp.int32)
    return (ids, counts)


def draw_block_list(key, part):
    return routing(key)[0]


def draw_block_count(key, part):
    return routing(key)[1]


def draw_source_blocks(key, part):
    key = jax.random.fold_in(key, 13)
    first, second = jax.random.split(key)
    total = NB * DEVICES
    phase = jax.random.uniform(second, (total, 1, 1), jnp.float32, 0.0, 2.0 * math.pi)
    rows = jnp.arange(BS).astype(jnp.float32)[None, :, None]
    cols = jnp.arange(BS).astype(jnp.float32)[None, None, :]
    smooth_part = 1.5 * jnp.sin(2.0 * math.pi * (rows + cols) / (2.0 * BS) + phase)
    noise = jnp.clip(jax.random.normal(first, (total, BS, BS), jnp.float32), -5.0, 5.0)
    values = noise + smooth_part
    return values.astype(jnp.bfloat16)


def cubic_rows(key, spread):
    first, second = jax.random.split(key)
    total = K * DEVICES
    shared = jax.random.uniform(first, (total, 1, 1), jnp.float32, -spread, spread)
    own = jax.random.uniform(second, (total, BS, 1), jnp.float32, -0.45, 0.45)
    centre = jnp.arange(BS).astype(jnp.float32)[None, :, None] + shared + own
    taps = jnp.arange(BS).astype(jnp.float32)[None, None, :]
    values = keys_weight(jnp.abs(taps - centre))
    return values / jnp.sum(values, axis=2, keepdims=True)


def draw_row_weights(key, part):
    key = jax.random.fold_in(key, 11)
    values = cubic_rows(key, 0.0)
    return values.astype(jnp.bfloat16)


def draw_col_weights(key, part):
    key = jax.random.fold_in(key, 17)
    values = cubic_rows(key, 0.0)
    return jnp.transpose(values, (0, 2, 1)).astype(jnp.bfloat16)


def shard_levels(key, shape, cuts, least, largest):
    factor_of = 1.0
    for axis_at, blocks in cuts:
        heights = jax.random.uniform(jax.random.fold_in(jax.random.fold_in(key, 6), axis_at), (blocks,), jnp.float32, least / len(cuts), largest / len(cuts))
        factor_of = factor_of * jnp.repeat(jnp.exp(heights), shape[axis_at] // blocks).reshape((-1,) + (1,) * (len(shape) - 1 - axis_at))
    return factor_of


def setup_inputs(seed: int = 0) -> dict:
    keys = jax.random.split(jax.random.key(seed), 7)
    return {
        "source_blocks": draw_source_blocks(jax.random.fold_in(keys[6], 71), 0),
        "block_scale": jnp.clip(jnp.exp(math.log(4.0) - 2.0794415 * jax.random.uniform(keys[1], (NB * DEVICES,), jnp.float32) ** shard_levels(keys[1], (NB * DEVICES,), ((0, 128),), -0.2, 0.2)), 0.5, 4.0),
        "block_list": draw_block_list(jax.random.fold_in(keys[6], 71), 0),
        "block_count": draw_block_count(jax.random.fold_in(keys[6], 71), 0),
        "row_weights": draw_row_weights(jax.random.fold_in(keys[6], 71), 0),
        "col_weights": draw_col_weights(jax.random.fold_in(keys[6], 71), 0),
    }


rim_width = 24
sigma_cells = 10.0
flat_drop = 0.05

def surface(padded, rows, cols):

    def near(di, dj):
        return padded[1 + di:1 + di + rows, 1 + dj:1 + dj + cols]
    grad_x = (near(-1, 1) + 2.0 * near(0, 1) + near(1, 1) - (near(-1, -1) + 2.0 * near(0, -1) + near(1, -1))) / 8.0
    grad_y = (near(1, -1) + 2.0 * near(1, 0) + near(1, 1) - (near(-1, -1) + 2.0 * near(-1, 0) + near(-1, 1))) / 8.0
    slope = jnp.sqrt(1.0 + grad_x * grad_x + grad_y * grad_y)
    centre = near(0, 0)
    parts = []
    for di, dj in ((-1, -1), (-1, 0), (-1, 1), (0, -1), (0, 1), (1, -1), (1, 0), (1, 1)):
        reach = (di * di + dj * dj) ** 0.5
        parts.append(jnp.maximum((centre - near(di, dj)) / reach, 0.0) + flat_drop)
    weights = jnp.stack(parts, axis=0)
    flow = (weights / lax.optimization_barrier(jnp.sum(weights, axis=0, keepdims=True))).astype(jnp.bfloat16)
    return (slope, flow)

def reference(source_blocks, block_scale, block_list, block_count, row_weights, col_weights):
    rows_w = row_weights.reshape(DEVICES, K, BS, BS)
    cols_w = col_weights.reshape(DEVICES, K, BS, BS)

    def one_tile(packed):
        wy_tile, wx_tile, ids, count = packed
        living = (jnp.arange(K) < count).astype(jnp.float32)
        blocks = source_blocks[ids].astype(jnp.float32)
        factor = block_scale[ids] * living
        partial_value = jnp.einsum('kri,kic->krc', wy_tile.astype(jnp.float32), blocks)
        partial_value = (partial_value * factor[:, None, None]).astype(jnp.bfloat16)
        window = jnp.einsum('kri,kic->krc', partial_value.astype(jnp.float32), wx_tile.astype(jnp.float32))
        return window.reshape(W, W, BS, BS).transpose(0, 2, 1, 3).reshape(R, C)
    tiles = lax.map(one_tile, (rows_w, cols_w, block_list, block_count))
    elevation = tiles.reshape(N_GX, N_GY, R, C).transpose(1, 2, 0, 3).reshape(NR, NC)
    taps = jnp.arange(-rim_width, rim_width + 1).astype(jnp.float32)
    kernel = jnp.exp(-taps * taps / (2.0 * sigma_cells * sigma_cells))
    kernel = kernel / jnp.sum(kernel)
    padded = jnp.pad(elevation, rim_width)
    row_pass = jnp.zeros((NR, NC + 2 * rim_width), jnp.float32)
    for step in range(2 * rim_width + 1):
        row_pass = row_pass + kernel[step] * padded[step:step + NR, :]
    smoothed = jnp.zeros((NR, NC), jnp.float32)
    for step in range(2 * rim_width + 1):
        smoothed = smoothed + kernel[step] * row_pass[:, step:step + NC]
    relief = elevation - smoothed
    slope, flow = surface(jnp.pad(elevation, 1), NR, NC)
    return (relief, slope, flow)
```

```python
import jax
import jax.numpy as jnp
import ml_dtypes
import numpy as np
from jax import lax
from jax.experimental import pallas as pl
from jax.experimental.pallas import tpu as pltpu
from jax.sharding import PartitionSpec as P

W = 6
CAP = 4
RIM = 24
PAD = 32
SIGMA = 10.0
FLAT = 0.05
DIAG = 0.5**0.5
F32 = jnp.float32
BF16 = jnp.bfloat16
MIB = 1 << 20

SMEM = pl.BlockSpec(memory_space=pltpu.SMEM)
VMEM = pl.BlockSpec(memory_space=pltpu.VMEM)
ANY = pl.BlockSpec(memory_space=pl.ANY)


def gather_kernel(
    list_hbm, count_hbm, scale_hbm, blocks_hbm, out_hbm,
    listed, counted, scale, blocks, found, table, staged, sems, out_sems,
):
    holders = lax.axis_size("gy")
    first = lax.axis_index("gx") * holders
    held = blocks.shape[0]
    base = (first + lax.axis_index("gy")) * held
    slots = listed.shape[0]
    copies = [
        pltpu.make_async_copy(list_hbm, listed, sems.at[0]),
        pltpu.make_async_copy(count_hbm, counted, sems.at[1]),
        pltpu.make_async_copy(scale_hbm, scale, sems.at[2]),
        pltpu.make_async_copy(blocks_hbm, blocks, sems.at[3]),
    ]
    for copy in copies:
        copy.start()
    copies[0].wait()
    copies[1].wait()
    shape = found.shape
    row = lax.broadcasted_iota(jnp.int32, shape, 0)
    live = jnp.broadcast_to(counted[...], shape)
    rank = jnp.zeros(shape, jnp.int32)
    chosen = jnp.zeros(shape, jnp.int32)
    for k in range(slots):
        block = jnp.broadcast_to(listed[k : k + 1, :], shape) - base
        hit = (block >= 0) & (block < held) & (k < live)
        chosen = jnp.where(hit & (rank == row), block, chosen)
        rank = rank + hit.astype(jnp.int32)
    found[...] = chosen
    handed = pltpu.make_async_copy(found, table, sems.at[4])
    handed.start()
    handed.wait()
    copies[2].wait()
    copies[3].wait()

    def one_tile(t, carry):
        for j in range(CAP):
            block = table[j, first + t]
            value = blocks[block].astype(F32) * scale[block]
            staged[t, j] = value.astype(BF16)
        pltpu.make_async_copy(staged.at[t], out_hbm.at[t], out_sems.at[t]).start()
        return carry

    lax.fori_loop(0, holders, one_tile, 0)
    for t in range(out_hbm.shape[0]):
        pltpu.make_async_copy(staged.at[t], out_hbm.at[t], out_sems.at[t]).wait()


def gather(block_list, block_count, block_scale, source_blocks):
    held, edge, _ = source_blocks.shape
    holders = lax.axis_size("gy")
    slots, tiles = block_list.shape
    return pl.pallas_call(
        gather_kernel,
        out_shape=jax.ShapeDtypeStruct((holders, CAP, edge, edge), BF16),
        in_specs=[ANY] * 4,
        out_specs=ANY,
        scratch_shapes=[
            pltpu.VMEM((slots, tiles), jnp.int32),
            pltpu.VMEM((1, tiles), jnp.int32),
            pltpu.SMEM((held,), F32),
            pltpu.VMEM((held, edge, edge), BF16),
            pltpu.VMEM((8, tiles), jnp.int32),
            pltpu.SMEM((8, tiles), jnp.int32),
            pltpu.VMEM((holders, CAP, edge, edge), BF16),
            pltpu.SemaphoreType.DMA((5,)),
            pltpu.SemaphoreType.DMA((holders,)),
        ],
        compiler_params=pltpu.CompilerParams(vmem_limit_bytes=56 * MIB),
        name="gather_blocks",
    )(block_list, block_count.reshape(1, tiles), block_scale, source_blocks)


def resample_kernel(
    list_ref, count_ref, arrived_ref, row_ref, col_ref,
    elev_ref, band_ref, left_ref, right_ref, source, seen,
):
    holders = lax.axis_size("gy")
    first = lax.axis_index("gx") * holders
    tile = first + lax.axis_index("gy")
    held = 32
    slots = list_ref.shape[0]
    edge = row_ref.shape[1]
    live = count_ref[tile]
    for h in range(holders):
        seen[h] = 0
    for k in range(slots):
        owner = (list_ref[k, tile] - first * held) // held
        owner = jnp.clip(owner, 0, holders - 1)
        rank = seen[owner]
        source[k] = owner * CAP + jnp.minimum(rank, CAP - 1)
        seen[owner] = rank + (k < live).astype(jnp.int32)

    def one_row(i, carry):
        for j in range(W):
            k = i * W + j
            part = jnp.dot(row_ref[k], arrived_ref[source[k]], preferred_element_type=F32)
            part = jnp.where(k < live, part, 0.0).astype(BF16)
            window = jnp.dot(part, col_ref[k], preferred_element_type=F32)
            span = pl.ds(pl.multiple_of(i * edge, edge), edge)
            elev_ref[j, span, :] = window
            band_ref[span, j * edge : (j + 1) * edge] = window.astype(BF16)
        return carry

    lax.fori_loop(0, W, one_row, 0)

    rows = elev_ref.shape[1]
    chunk = rows // 4
    lane = lax.broadcasted_iota(jnp.int32, (chunk, 128), 1)
    left = jnp.zeros((chunk, 128), F32)
    right = jnp.zeros((chunk, 128), F32)
    for q in range(4):
        mine = (lane >= PAD * q) & (lane < PAD * (q + 1))
        part = elev_ref[0, q * chunk : (q + 1) * chunk, :]
        if q:
            part = pltpu.roll(part, PAD * q, 1)
        left = jnp.where(mine, part, left)
        part = elev_ref[W - 1, q * chunk : (q + 1) * chunk, :]
        if q != 3:
            part = pltpu.roll(part, PAD * (q + 1), 1)
        right = jnp.where(mine, part, right)
    left_ref[...] = left.astype(BF16)
    right_ref[...] = right.astype(BF16)


def resample(block_list, block_count, arrived, row_weights, col_weights):
    slots, edge, _ = row_weights.shape
    side = W * edge
    shapes = [
        ((W, side, edge), F32),
        ((side, side), BF16),
        ((side // 4, 128), BF16),
        ((side // 4, 128), BF16),
    ]
    return pl.pallas_call(
        resample_kernel,
        out_shape=[jax.ShapeDtypeStruct(s, d) for s, d in shapes],
        in_specs=[SMEM, SMEM, VMEM, VMEM, VMEM],
        out_specs=[VMEM] * len(shapes),
        scratch_shapes=[
            pltpu.SMEM((slots,), jnp.int32),
            pltpu.SMEM((lax.axis_size("gy"),), jnp.int32),
        ],
        compiler_params=pltpu.CompilerParams(vmem_limit_bytes=24 * MIB),
        name="resample",
    )(block_list, block_count, arrived, row_weights, col_weights)


def tap(offset):
    value = np.exp(-(offset * offset).astype(np.float32) / np.float32(2.0 * SIGMA * SIGMA))
    return np.where(np.abs(offset) <= RIM, value, 0.0).astype(ml_dtypes.bfloat16)


def tap_total():
    return float(np.sum(tap(np.arange(-RIM, RIM + 1)).astype(np.float64)))


def across_taps(wide, out):
    return jnp.asarray(tap(np.arange(wide)[:, None] - np.arange(out)[None, :] - 128))


def down_taps(step):
    return jnp.asarray(tap(np.arange(step + 2 * PAD)[None, :] - np.arange(step)[:, None] - PAD))


def cells(mid, low, high):
    centre = mid(0)
    ul, uc, ur = low(-1), mid(-1), high(-1)
    cl, cr = low(0), high(0)
    dl, dc, dr = low(1), mid(1), high(1)
    one = dr - ul
    two = ur - dl
    grad_x = one + two + 2.0 * (cr - cl)
    grad_y = one - two + 2.0 * (dc - uc)
    square = 1.0 + (grad_x * grad_x + grad_y * grad_y) * (1.0 / 64.0)
    slope = square * lax.rsqrt(square)
    raised = centre + FLAT
    slant = centre * DIAG + FLAT
    flows = []
    for value, diagonal in (
        (ul, True), (uc, False), (ur, True), (cl, False),
        (cr, False), (dl, True), (dc, False), (dr, True),
    ):
        drop = slant - value * DIAG if diagonal else raised - value
        flows.append(jnp.maximum(drop, FLAT))
    total = (
        ((flows[0] + flows[1]) + (flows[2] + flows[3]))
        + ((flows[4] + flows[5]) + (flows[6] + flows[7]))
    )
    share = pl.reciprocal(total, approx=True)
    return slope, [(flow * share).astype(BF16) for flow in flows]


def sideways(centre, before, after):
    lane = lax.broadcasted_iota(jnp.int32, centre.shape, 1)
    low = jnp.where(lane == 0, pltpu.roll(before, 1, 1), pltpu.roll(centre, 1, 1))
    high = jnp.where(lane == 127, pltpu.roll(after, 127, 1), pltpu.roll(centre, 127, 1))
    return low, high


def dot(a, b):
    return jnp.dot(a, b, preferred_element_type=F32)


STEP = 176


def inner_kernel(
    elev_ref, band_ref, across, down, relief_hbm, slope_hbm, flow_hbm,
    relief, slope, flow, low_ref, high_ref, sems,
):
    lanes, rows, _ = elev_ref.shape
    steps = (rows - 2 * PAD) // STEP
    count = lanes - 2
    inverse = 1.0 / (tap_total() ** 2)

    def copies(i):
        slot = lax.rem(i, 2)
        at = pl.multiple_of(PAD + i * STEP, 16)
        place = (pl.ds(at, STEP), pl.ds(128, count * 128))
        return (
            pltpu.make_async_copy(relief.at[slot], relief_hbm.at[place], sems.at[slot, 0]),
            pltpu.make_async_copy(slope.at[slot], slope_hbm.at[place], sems.at[slot, 1]),
            pltpu.make_async_copy(
                flow.at[slot], flow_hbm.at[(slice(None),) + place], sems.at[slot, 2]
            ),
        )

    def one_step(i, carry):
        slot = lax.rem(i, 2)
        base = pl.multiple_of(i * STEP, 16)

        @pl.when(i >= 2)
        def drain():
            for copy in copies(i - 2):
                copy.wait()

        smooth = dot(down[...], band_ref[pl.ds(base, STEP + 2 * PAD), :]).astype(BF16)
        for j in range(count // 2):
            value = dot(smooth[:, j * 256 : j * 256 + 512], across[...])
            for h in range(2):
                at = j * 256 + h * 128
                centre = elev_ref[j * 2 + h + 1, pl.ds(base + PAD, STEP), :]
                relief[slot, :, at : at + 128] = (
                    centre - value[:, h * 128 : h * 128 + 128] * inverse
                )
        span = pl.ds(base + PAD - 8, STEP + 16)
        for j in range(count):
            low, high = sideways(elev_ref[j + 1, span, :], elev_ref[j, span, :], elev_ref[j + 2, span, :])
            low_ref[j] = low
            high_ref[j] = high

        for at in range(0, STEP, 16):
            for j in range(count):
                value, parts = cells(
                    lambda d: elev_ref[j + 1, pl.ds(base + at + PAD + d, 16), :],
                    lambda d: low_ref[j, pl.ds(at + 8 + d, 16), :],
                    lambda d: high_ref[j, pl.ds(at + 8 + d, 16), :],
                )
                place = (pl.ds(at, 16), slice(j * 128, (j + 1) * 128))
                slope[(slot,) + place] = value
                for n, part in enumerate(parts):
                    flow[(slot, n) + place] = part
        for copy in copies(i):
            copy.start()
        return carry

    lax.fori_loop(0, steps, one_step, 0)
    for i in (steps - 2, steps - 1):
        for copy in copies(i):
            copy.wait()


def out_shapes(rows, cols):
    return [
        jax.ShapeDtypeStruct((rows, cols), F32),
        jax.ShapeDtypeStruct((rows, cols), F32),
        jax.ShapeDtypeStruct((8, rows, cols), BF16),
    ]


def cost(cells_done):
    return pl.CostEstimate(
        flops=cells_done * 4000, bytes_accessed=cells_done * 24, transcendentals=cells_done * 2
    )


def inner(elevation, band):
    lanes, rows, _ = elevation.shape
    cols = lanes * 128
    wide = (lanes - 2) * 128
    return pl.pallas_call(
        inner_kernel,
        out_shape=out_shapes(rows, cols),
        in_specs=[VMEM] * 4,
        out_specs=[ANY] * 3,
        scratch_shapes=[
            pltpu.VMEM((2, STEP, wide), F32),
            pltpu.VMEM((2, STEP, wide), F32),
            pltpu.VMEM((2, 8, STEP, wide), BF16),
            pltpu.VMEM((lanes - 2, STEP + 16, 128), F32),
            pltpu.VMEM((lanes - 2, STEP + 16, 128), F32),
            pltpu.SemaphoreType.DMA((2, 3)),
        ],
        cost_estimate=cost((rows - 2 * PAD) * wide),
        compiler_params=pltpu.CompilerParams(vmem_limit_bytes=16 * MIB),
        name="inner_cells",
    )(elevation, band, across_taps(512, 256), down_taps(STEP))


def unpack_left(value, q):
    value = value.astype(F32)
    return value if q == 3 else pltpu.roll(value, 96 - PAD * q, 1)


def unpack_right(value, q):
    value = value.astype(F32)
    return value if q == 0 else pltpu.roll(value, 128 - PAD * q, 1)


def sides_kernel(
    elev_ref, band_ref, left_ref, right_ref, across, down, relief_in, slope_in, flow_in,
    relief_hbm, slope_hbm, flow_hbm,
    relief, slope, flow, halo, halo_band, low_ref, high_ref, sems,
):
    lanes, rows, _ = elev_ref.shape
    steps = (rows - 2 * PAD) // STEP
    chunk = rows // 4
    inverse = 1.0 / (tap_total() ** 2)
    for q in range(4):
        span = slice(q * chunk, (q + 1) * chunk)
        for s, value in enumerate((unpack_left(left_ref[...], q), unpack_right(right_ref[...], q))):
            halo[s, span, :] = value
            halo_band[s, span, :] = value.astype(BF16)

    def copies(i, s):
        slot = lax.rem(i, 2)
        at = pl.multiple_of(PAD + i * STEP, 16)
        place = (pl.ds(at, STEP), pl.ds(s * (lanes - 1) * 128, 128))
        return (
            pltpu.make_async_copy(relief.at[slot, s], relief_hbm.at[place], sems.at[slot, s, 0]),
            pltpu.make_async_copy(slope.at[slot, s], slope_hbm.at[place], sems.at[slot, s, 1]),
            pltpu.make_async_copy(
                flow.at[slot, s], flow_hbm.at[(slice(None),) + place], sems.at[slot, s, 2]
            ),
        )

    def one_step(i, carry):
        slot = lax.rem(i, 2)
        base = pl.multiple_of(i * STEP, 16)

        @pl.when(i >= 2)
        def drain():
            for s in range(2):
                for copy in copies(i - 2, s):
                    copy.wait()

        tall = pl.ds(base, STEP + 2 * PAD)
        span = pl.ds(base + PAD - 8, STEP + 16)
        for s in range(2):
            own = dot(down[...], band_ref[tall, s * (lanes - 2) * 128 : s * (lanes - 2) * 128 + 256])
            far = dot(down[...], halo_band[s, tall, :])
            smooth = jnp.concatenate([own, far] if s else [far, own], axis=1).astype(BF16)
            value = dot(smooth, across[...])
            j = s * (lanes - 1)
            relief[slot, s] = elev_ref[j, pl.ds(base + PAD, STEP), :] - value * inverse
            before = elev_ref[j - 1, span, :] if s else halo[0, span, :]
            after = halo[1, span, :] if s else elev_ref[1, span, :]
            low, high = sideways(elev_ref[j, span, :], before, after)
            low_ref[s] = low
            high_ref[s] = high

        for at in range(0, STEP, 16):
            for s in range(2):
                value, parts = cells(
                    lambda d: elev_ref[s * (lanes - 1), pl.ds(base + at + PAD + d, 16), :],
                    lambda d: low_ref[s, pl.ds(at + 8 + d, 16), :],
                    lambda d: high_ref[s, pl.ds(at + 8 + d, 16), :],
                )
                slope[slot, s, pl.ds(at, 16), :] = value
                for n, part in enumerate(parts):
                    flow[slot, s, n, pl.ds(at, 16), :] = part
        for s in range(2):
            for copy in copies(i, s):
                copy.start()
        return carry

    lax.fori_loop(0, steps, one_step, 0)
    for i in (steps - 2, steps - 1):
        for s in range(2):
            for copy in copies(i, s):
                copy.wait()


def sides(elevation, band, left, right, outs):
    lanes, rows, _ = elevation.shape
    return pl.pallas_call(
        sides_kernel,
        out_shape=out_shapes(rows, lanes * 128),
        in_specs=[VMEM] * 6 + [ANY] * 3,
        out_specs=[ANY] * 3,
        input_output_aliases={6: 0, 7: 1, 8: 2},
        scratch_shapes=[
            pltpu.VMEM((2, 2, STEP, 128), F32),
            pltpu.VMEM((2, 2, STEP, 128), F32),
            pltpu.VMEM((2, 2, 8, STEP, 128), BF16),
            pltpu.VMEM((2, rows, 128), F32),
            pltpu.VMEM((2, rows, 128), BF16),
            pltpu.VMEM((2, STEP + 16, 128), F32),
            pltpu.VMEM((2, STEP + 16, 128), F32),
            pltpu.SemaphoreType.DMA((2, 2, 3)),
        ],
        cost_estimate=cost((rows - 2 * PAD) * 256),
        compiler_params=pltpu.CompilerParams(vmem_limit_bytes=16 * MIB),
        name="side_cells",
    )(elevation, band, left, right, across_taps(384, 128), down_taps(STEP), *outs)


def ends_kernel(
    elev_ref, band_ref, left_ref, right_ref, up_ref, down_ref, across, down,
    relief_in, slope_in, flow_in, relief_hbm, slope_hbm, flow_hbm,
    relief, slope, flow, wide, band, low_ref, high_ref, sems,
):
    lanes, rows, _ = elev_ref.shape
    cols = lanes * 128
    near = 2 * PAD
    inverse = 1.0 / (tap_total() ** 2)
    packed = left_ref.shape[0]
    for e in range(2):
        here = slice(PAD, PAD + near) if e == 0 else slice(0, near)
        there = slice(0, PAD) if e == 0 else slice(near, near + PAD)
        other = down_ref if e else up_ref
        own_rows = slice(rows - near, rows) if e else slice(0, near)
        pack_rows = slice(packed - near, packed) if e else slice(0, near)
        band[e, here, 128 : 128 + cols] = band_ref[own_rows, :]
        band[e, there, 128 : 128 + cols] = other[:, 0:cols]
        far_left = unpack_left(left_ref[pack_rows, :], 3 * e)
        far_right = unpack_right(right_ref[pack_rows, :], 3 * e)
        corner_left = unpack_left(other[:, cols : cols + 128], 0 if e else 3)
        corner_right = unpack_right(other[:, cols + 128 : cols + 256], 0 if e else 3)
        band[e, here, 0:128] = far_left.astype(BF16)
        band[e, there, 0:128] = corner_left.astype(BF16)
        band[e, here, 128 + cols :] = far_right.astype(BF16)
        band[e, there, 128 + cols :] = corner_right.astype(BF16)
        if e == 0:
            wide[e, 0, 0:8, :] = corner_left[PAD - 8 : PAD]
            wide[e, 0, 8:48, :] = far_left[0:40]
            wide[e, lanes + 1, 0:8, :] = corner_right[PAD - 8 : PAD]
            wide[e, lanes + 1, 8:48, :] = far_right[0:40]
        else:
            wide[e, 0, 0:40, :] = far_left[near - 40 : near]
            wide[e, 0, 40:48, :] = corner_left[0:8]
            wide[e, lanes + 1, 0:40, :] = far_right[near - 40 : near]
            wide[e, lanes + 1, 40:48, :] = corner_right[0:8]
        for j in range(lanes):
            part = other[:, j * 128 : (j + 1) * 128].astype(F32)
            if e == 0:
                wide[e, j + 1, 0:8, :] = part[PAD - 8 : PAD]
                wide[e, j + 1, 8:48, :] = elev_ref[j, 0:40, :]
            else:
                wide[e, j + 1, 0:40, :] = elev_ref[j, rows - 40 : rows, :]
                wide[e, j + 1, 40:48, :] = part[0:8]

    for e in range(2):
        smooth = dot(down[...], band[e]).astype(BF16)
        for j in range(lanes // 2):
            value = dot(smooth[:, j * 256 : j * 256 + 512], across[...])
            for h in range(2):
                at = j * 256 + h * 128
                relief[e, :, at : at + 128] = (
                    wide[e, j * 2 + h + 1, 8 : 8 + PAD, :] - value[:, h * 128 : h * 128 + 128] * inverse
                )
        for j in range(lanes):
            low, high = sideways(wide[e, j + 1], wide[e, j], wide[e, j + 2])
            low_ref[e, j] = low
            high_ref[e, j] = high
            column = slice(j * 128, (j + 1) * 128)
            for at in range(0, PAD, 16):
                value, parts = cells(
                    lambda d: wide[e, j + 1, at + 8 + d : at + 24 + d, :],
                    lambda d: low_ref[e, j, at + 8 + d : at + 24 + d, :],
                    lambda d: high_ref[e, j, at + 8 + d : at + 24 + d, :],
                )
                slope[e, at : at + 16, column] = value
                for n, part in enumerate(parts):
                    flow[e, n, at : at + 16, column] = part
        place = pl.ds(e * (rows - PAD), PAD)
        pltpu.make_async_copy(relief.at[e], relief_hbm.at[place], sems.at[e, 0]).start()
        pltpu.make_async_copy(slope.at[e], slope_hbm.at[place], sems.at[e, 1]).start()
        pltpu.make_async_copy(flow.at[e], flow_hbm.at[:, place], sems.at[e, 2]).start()
    for e in range(2):
        place = pl.ds(e * (rows - PAD), PAD)
        pltpu.make_async_copy(relief.at[e], relief_hbm.at[place], sems.at[e, 0]).wait()
        pltpu.make_async_copy(slope.at[e], slope_hbm.at[place], sems.at[e, 1]).wait()
        pltpu.make_async_copy(flow.at[e], flow_hbm.at[:, place], sems.at[e, 2]).wait()


def ends(elevation, band, left, right, up, down, outs):
    lanes, rows, _ = elevation.shape
    cols = lanes * 128
    return pl.pallas_call(
        ends_kernel,
        out_shape=out_shapes(rows, cols),
        in_specs=[VMEM] * 8 + [ANY] * 3,
        out_specs=[ANY] * 3,
        input_output_aliases={8: 0, 9: 1, 10: 2},
        scratch_shapes=[
            pltpu.VMEM((2, PAD, cols), F32),
            pltpu.VMEM((2, PAD, cols), F32),
            pltpu.VMEM((2, 8, PAD, cols), BF16),
            pltpu.VMEM((2, lanes + 2, PAD + 16, 128), F32),
            pltpu.VMEM((2, 3 * PAD, cols + 256), BF16),
            pltpu.VMEM((2, lanes, PAD + 16, 128), F32),
            pltpu.VMEM((2, lanes, PAD + 16, 128), F32),
            pltpu.SemaphoreType.DMA((2, 3)),
        ],
        cost_estimate=cost(2 * PAD * cols),
        compiler_params=pltpu.CompilerParams(vmem_limit_bytes=16 * MIB),
        name="end_cells",
    )(elevation, band, left, right, up, down, across_taps(512, 256), down_taps(PAD), *outs)


def exchange(low, high, axis):
    devices = lax.axis_size(axis)
    up = [(i, i + 1) for i in range(devices - 1)]
    down = [(j, i) for i, j in up]
    return lax.ppermute(high, axis, up), lax.ppermute(low, axis, down)


def local(source_blocks, block_scale, block_list, block_count, row_weights, col_weights):
    holders = lax.axis_size("gy")
    edge = source_blocks.shape[1]
    block_list = block_list.T
    outgoing = gather(block_list, block_count, block_scale, source_blocks)
    arrived = lax.all_to_all(
        outgoing, "gy", split_axis=0, concat_axis=0, tiled=True
    ).reshape(holders * CAP, edge, edge)
    elevation, band, left, right = resample(
        block_list, block_count, arrived, row_weights, col_weights
    )
    before, after = exchange(left, right, "gx")
    outs = inner(elevation, band)
    top = jnp.concatenate([band[:PAD], before[:PAD], after[:PAD]], axis=1)
    bottom = jnp.concatenate([band[-PAD:], before[-PAD:], after[-PAD:]], axis=1)
    above, below = exchange(top, bottom, "gy")
    outs = sides(elevation, band, before, after, outs)
    return tuple(ends(elevation, band, before, after, above, below, outs))


def solution(mesh):
    in_specs = (
        P(("gx", "gy"), None, None),
        P(("gx", "gy")),
        P(),
        P(),
        P(("gx", "gy"), None, None),
        P(("gx", "gy"), None, None),
    )
    out_specs = (P("gy", "gx"), P("gy", "gx"), P(None, "gy", "gx"))
    return jax.shard_map(local, mesh=mesh, in_specs=in_specs, out_specs=out_specs, check_vma=False)
```

```python
import jax
import jax.numpy as jnp
import ml_dtypes
import numpy as np
from jax import lax
from jax.experimental import pallas as pl
from jax.experimental.pallas import tpu as pltpu
from jax.sharding import PartitionSpec as P

W = 6
CAP = 4
RIM = 24
PAD = 32
SIGMA = 10.0
FLAT = 0.05
DIAG = 0.5**0.5
F32 = jnp.float32
BF16 = jnp.bfloat16
MIB = 1 << 20

SMEM = pl.BlockSpec(memory_space=pltpu.SMEM)
VMEM = pl.BlockSpec(memory_space=pltpu.VMEM)
ANY = pl.BlockSpec(memory_space=pl.ANY)


def gather_kernel(
    list_hbm, count_hbm, scale_hbm, blocks_hbm, out_hbm,
    listed, counted, scale, blocks, found, table, staged, sems, out_sems,
):
    holders = lax.axis_size("gy")
    first = lax.axis_index("gx") * holders
    held = blocks.shape[0]
    base = (first + lax.axis_index("gy")) * held
    slots = listed.shape[0]
    copies = [
        pltpu.make_async_copy(list_hbm, listed, sems.at[0]),
        pltpu.make_async_copy(count_hbm, counted, sems.at[1]),
        pltpu.make_async_copy(scale_hbm, scale, sems.at[2]),
        pltpu.make_async_copy(blocks_hbm, blocks, sems.at[3]),
    ]
    for copy in copies:
        copy.start()
    copies[0].wait()
    copies[1].wait()
    shape = found.shape
    row = lax.broadcasted_iota(jnp.int32, shape, 0)
    live = jnp.broadcast_to(counted[...], shape)
    rank = jnp.zeros(shape, jnp.int32)
    chosen = jnp.zeros(shape, jnp.int32)
    for k in range(slots):
        block = jnp.broadcast_to(listed[k : k + 1, :], shape) - base
        hit = (block >= 0) & (block < held) & (k < live)
        chosen = jnp.where(hit & (rank == row), block, chosen)
        rank = rank + hit.astype(jnp.int32)
    found[...] = chosen
    handed = pltpu.make_async_copy(found, table, sems.at[4])
    handed.start()
    handed.wait()
    copies[2].wait()
    copies[3].wait()

    def one_tile(t, carry):
        for j in range(CAP):
            block = table[j, first + t]
            value = blocks[block].astype(F32) * scale[block]
            staged[t, j] = value.astype(BF16)
        pltpu.make_async_copy(staged.at[t], out_hbm.at[t], out_sems.at[t]).start()
        return carry

    lax.fori_loop(0, holders, one_tile, 0)
    for t in range(out_hbm.shape[0]):
        pltpu.make_async_copy(staged.at[t], out_hbm.at[t], out_sems.at[t]).wait()


def gather(block_list, block_count, block_scale, source_blocks):
    held, edge, _ = source_blocks.shape
    holders = lax.axis_size("gy")
    slots, tiles = block_list.shape
    return pl.pallas_call(
        gather_kernel,
        out_shape=jax.ShapeDtypeStruct((holders, CAP, edge, edge), BF16),
        in_specs=[ANY] * 4,
        out_specs=ANY,
        scratch_shapes=[
            pltpu.VMEM((slots, tiles), jnp.int32),
            pltpu.VMEM((1, tiles), jnp.int32),
            pltpu.SMEM((held,), F32),
            pltpu.VMEM((held, edge, edge), BF16),
            pltpu.VMEM((8, tiles), jnp.int32),
            pltpu.SMEM((8, tiles), jnp.int32),
            pltpu.VMEM((holders, CAP, edge, edge), BF16),
            pltpu.SemaphoreType.DMA((5,)),
            pltpu.SemaphoreType.DMA((holders,)),
        ],
        compiler_params=pltpu.CompilerParams(vmem_limit_bytes=56 * MIB),
        name="gather_blocks",
    )(block_list, block_count.reshape(1, tiles), block_scale, source_blocks)


def find_sources(list_ref, count_ref, source, seen):
    holders = lax.axis_size("gy")
    first = lax.axis_index("gx") * holders
    tile = first + lax.axis_index("gy")
    held = 32
    live = count_ref[tile]
    for h in range(holders):
        seen[h] = 0
    for k in range(list_ref.shape[0]):
        owner = (list_ref[k, tile] - first * held) // held
        owner = jnp.clip(owner, 0, holders - 1)
        rank = seen[owner]
        source[k] = owner * CAP + jnp.minimum(rank, CAP - 1)
        seen[owner] = rank + (k < live).astype(jnp.int32)
    return live


def window(k, live, source, arrived_ref, row_ref, col_ref):
    part = dot(row_ref[k], arrived_ref[source[k]])
    part = jnp.where(k < live, part, 0.0).astype(BF16)
    return dot(part, col_ref[k])


def edges_kernel(
    list_ref, count_ref, arrived_ref, row_ref, col_ref, edge_ref, left_ref, right_ref, source, seen
):
    edge = row_ref.shape[1]
    live = find_sources(list_ref, count_ref, source, seen)
    for i in range(W):
        for s in range(2):
            k = i * W + s * (W - 1)
            edge_ref[s, i * edge : (i + 1) * edge, :] = window(
                k, live, source, arrived_ref, row_ref, col_ref
            )
    rows = edge_ref.shape[1]
    chunk = rows // 4
    lane = lax.broadcasted_iota(jnp.int32, (chunk, 128), 1)
    left = jnp.zeros((chunk, 128), F32)
    right = jnp.zeros((chunk, 128), F32)
    for q in range(4):
        mine = (lane >= PAD * q) & (lane < PAD * (q + 1))
        part = edge_ref[0, q * chunk : (q + 1) * chunk, :]
        if q:
            part = pltpu.roll(part, PAD * q, 1)
        left = jnp.where(mine, part, left)
        part = edge_ref[1, q * chunk : (q + 1) * chunk, :]
        if q != 3:
            part = pltpu.roll(part, PAD * (q + 1), 1)
        right = jnp.where(mine, part, right)
    left_ref[...] = left.astype(BF16)
    right_ref[...] = right.astype(BF16)


def edges(block_list, block_count, arrived, row_weights, col_weights):
    slots, edge, _ = row_weights.shape
    side = W * edge
    shapes = [((2, side, edge), F32), ((side // 4, 128), BF16), ((side // 4, 128), BF16)]
    return pl.pallas_call(
        edges_kernel,
        out_shape=[jax.ShapeDtypeStruct(s, d) for s, d in shapes],
        in_specs=[SMEM, SMEM, VMEM, VMEM, VMEM],
        out_specs=[VMEM] * len(shapes),
        scratch_shapes=[
            pltpu.SMEM((slots,), jnp.int32),
            pltpu.SMEM((lax.axis_size("gy"),), jnp.int32),
        ],
        cost_estimate=cost(side * 256),
        compiler_params=pltpu.CompilerParams(vmem_limit_bytes=16 * MIB),
        name="edge_windows",
    )(block_list, block_count, arrived, row_weights, col_weights)


def middle_kernel(
    list_ref, count_ref, arrived_ref, row_ref, col_ref, edge_ref, down,
    inner_ref, low_ref, high_ref, band_ref, fall_ref, source, seen,
):
    edge = row_ref.shape[1]
    rows = band_ref.shape[0]
    live = find_sources(list_ref, count_ref, source, seen)
    for s in range(2):
        band_ref[:, s * (W - 1) * edge : (s * (W - 1) + 1) * edge] = edge_ref[s].astype(BF16)

    for i in range(W):
        span = slice(i * edge, (i + 1) * edge)
        for j in range(1, W - 1):
            value = window(i * W + j, live, source, arrived_ref, row_ref, col_ref)
            inner_ref[j - 1, span, :] = value
            band_ref[span, j * edge : (j + 1) * edge] = value.astype(BF16)
    for i in range((rows - 2 * PAD) // STEP):
        value = dot(down[...], band_ref[i * STEP : (i + 1) * STEP + 2 * PAD, :])
        fall_ref[i * STEP : (i + 1) * STEP, :] = value.astype(BF16)

    def one_span(q, carry):
        span = pl.ds(pl.multiple_of(q * edge, edge), edge)
        pieces = [edge_ref[0, span, :]]
        pieces += [inner_ref[j, span, :] for j in range(W - 2)] + [edge_ref[1, span, :]]
        lane = lax.broadcasted_iota(jnp.int32, pieces[0].shape, 1)
        lows = [pltpu.roll(piece, 1, 1) for piece in pieces]
        highs = [pltpu.roll(piece, 127, 1) for piece in pieces]
        for j in range(W):
            low_ref[j, span, :] = jnp.where(lane == 0, lows[j - 1], lows[j]) if j else lows[j]
            high_ref[j, span, :] = (
                jnp.where(lane == 127, highs[j + 1], highs[j]) if j < W - 1 else highs[j]
            )
        return carry

    lax.fori_loop(0, W, one_span, 0)


def middle(block_list, block_count, arrived, row_weights, col_weights, edge_values):
    slots, edge, _ = row_weights.shape
    side = W * edge
    shapes = [
        ((W - 2, side, edge), F32),
        ((W, side, edge), F32),
        ((W, side, edge), F32),
        ((side, side), BF16),
        ((side - 2 * PAD, side), BF16),
    ]
    return pl.pallas_call(
        middle_kernel,
        out_shape=[jax.ShapeDtypeStruct(s, d) for s, d in shapes],
        in_specs=[SMEM, SMEM] + [VMEM] * 5,
        out_specs=[VMEM] * len(shapes),
        scratch_shapes=[
            pltpu.SMEM((slots,), jnp.int32),
            pltpu.SMEM((lax.axis_size("gy"),), jnp.int32),
        ],
        cost_estimate=cost(side * side),
        compiler_params=pltpu.CompilerParams(vmem_limit_bytes=24 * MIB),
        name="middle_windows",
    )(block_list, block_count, arrived, row_weights, col_weights, edge_values, down_taps(STEP))


def tap(offset):
    value = np.exp(-(offset * offset).astype(np.float32) / np.float32(2.0 * SIGMA * SIGMA))
    return np.where(np.abs(offset) <= RIM, value, 0.0).astype(ml_dtypes.bfloat16)


def tap_total():
    return float(np.sum(tap(np.arange(-RIM, RIM + 1)).astype(np.float64)))


def across_taps(wide, out):
    return jnp.asarray(tap(np.arange(wide)[:, None] - np.arange(out)[None, :] - 128))


def down_taps(step):
    return jnp.asarray(tap(np.arange(step + 2 * PAD)[None, :] - np.arange(step)[:, None] - PAD))


def cells(mid, low, high):
    centre = mid(0)
    ul, uc, ur = low(-1), mid(-1), high(-1)
    cl, cr = low(0), high(0)
    dl, dc, dr = low(1), mid(1), high(1)
    one = dr - ul
    two = ur - dl
    grad_x = one + two + 2.0 * (cr - cl)
    grad_y = one - two + 2.0 * (dc - uc)
    square = 1.0 + (grad_x * grad_x + grad_y * grad_y) * (1.0 / 64.0)
    slope = square * lax.rsqrt(square)
    raised = centre + FLAT
    slant = centre * DIAG + FLAT
    flows = []
    for value, diagonal in (
        (ul, True), (uc, False), (ur, True), (cl, False),
        (cr, False), (dl, True), (dc, False), (dr, True),
    ):
        drop = slant - value * DIAG if diagonal else raised - value
        flows.append(jnp.maximum(drop, FLAT))
    total = (
        ((flows[0] + flows[1]) + (flows[2] + flows[3]))
        + ((flows[4] + flows[5]) + (flows[6] + flows[7]))
    )
    share = pl.reciprocal(total, approx=True)
    return slope, [(flow * share).astype(BF16) for flow in flows]


def sideways(centre, before, after):
    lane = lax.broadcasted_iota(jnp.int32, centre.shape, 1)
    low = jnp.where(lane == 0, pltpu.roll(before, 1, 1), pltpu.roll(centre, 1, 1))
    high = jnp.where(lane == 127, pltpu.roll(after, 127, 1), pltpu.roll(centre, 127, 1))
    return low, high


def dot(a, b):
    return jnp.dot(a, b, preferred_element_type=F32)


STEP = 176


def main_kernel(
    edge_ref, inner_ref, low_ref, high_ref, fall_ref, left_ref, right_ref, across, down,
    relief_hbm, slope_hbm, flow_hbm, relief, slope, flow, far, patched, sems,
):
    rows, cols = low_ref.shape[1], relief.shape[1]
    lanes = cols // 128
    steps = (rows - 2 * PAD) // STEP
    chunk = rows // 4
    inverse = 1.0 / (tap_total() ** 2)
    lane = lax.broadcasted_iota(jnp.int32, (chunk, 128), 1)
    for q in range(4):
        span = slice(q * chunk, (q + 1) * chunk)
        value = unpack_left(left_ref[...], q)
        far[0, span, :] = value.astype(BF16)
        patched[0, span, :] = jnp.where(lane == 0, pltpu.roll(value, 1, 1), low_ref[0, span, :])
        value = unpack_right(right_ref[...], q)
        far[1, span, :] = value.astype(BF16)
        patched[1, span, :] = jnp.where(
            lane == 127, pltpu.roll(value, 127, 1), high_ref[lanes - 1, span, :]
        )

    def copies(i):
        span = pl.ds(pl.multiple_of(i * STEP, 16), STEP)
        place = pl.ds(pl.multiple_of(PAD + i * STEP, 16), STEP)
        return (
            pltpu.make_async_copy(relief.at[span], relief_hbm.at[place], sems.at[i, 0]),
            pltpu.make_async_copy(slope.at[span], slope_hbm.at[place], sems.at[i, 1]),
            pltpu.make_async_copy(flow.at[:, span], flow_hbm.at[:, place], sems.at[i, 2]),
        )

    def mid(j, span):
        if j in (0, lanes - 1):
            return edge_ref[int(j > 0), span, :]
        return inner_ref[j - 1, span, :]

    def low(j, span):
        return low_ref[j, span, :] if j else patched[0, span, :]

    def high(j, span):
        return high_ref[j, span, :] if j < lanes - 1 else patched[1, span, :]

    def one_step(i, carry):
        base = pl.multiple_of(i * STEP, 16)
        tall = pl.ds(base, STEP + 2 * PAD)
        span = pl.ds(base, STEP)
        sides = [dot(down[...], far[s, tall, :]).astype(BF16) for s in range(2)]
        for j in range(lanes // 2):
            at = j * 256
            if j == 0:
                wide = jnp.concatenate([sides[0], fall_ref[span, 0:384]], axis=1)
            elif j == lanes // 2 - 1:
                wide = jnp.concatenate([fall_ref[span, at - 128 :], sides[1]], axis=1)
            else:
                wide = fall_ref[span, at - 128 : at + 384]
            value = dot(wide, across[...])
            for h in range(2):
                centre = mid(j * 2 + h, pl.ds(base + PAD, STEP))
                relief[span, at + h * 128 : at + h * 128 + 128] = (
                    centre - value[:, h * 128 : h * 128 + 128] * inverse
                )
        for q in range(STEP // 16):
            at = pl.multiple_of(base + q * 16, 16)
            for j in range(lanes):
                value, parts = cells(
                    lambda d: mid(j, pl.ds(at + PAD + d, 16)),
                    lambda d: low(j, pl.ds(at + PAD + d, 16)),
                    lambda d: high(j, pl.ds(at + PAD + d, 16)),
                )
                place = (pl.ds(at, 16), slice(j * 128, (j + 1) * 128))
                slope[place] = value
                for n, part in enumerate(parts):
                    flow[(n,) + place] = part
        for copy in copies(i):
            copy.start()
        return carry

    lax.fori_loop(0, steps, one_step, 0)
    for i in range(steps):
        for copy in copies(i):
            copy.wait()


def main(edge_values, inner, low, high, fall, left, right):
    lanes, rows, _ = low.shape
    cols = lanes * 128
    tall = rows - 2 * PAD
    return pl.pallas_call(
        main_kernel,
        out_shape=out_shapes(rows, cols),
        in_specs=[VMEM] * 9,
        out_specs=[ANY] * 3,
        scratch_shapes=[
            pltpu.VMEM((tall, cols), F32),
            pltpu.VMEM((tall, cols), F32),
            pltpu.VMEM((8, tall, cols), BF16),
            pltpu.VMEM((2, rows, 128), BF16),
            pltpu.VMEM((2, rows, 128), F32),
            pltpu.SemaphoreType.DMA((tall // STEP, 3)),
        ],
        cost_estimate=cost(tall * cols),
        compiler_params=pltpu.CompilerParams(vmem_limit_bytes=32 * MIB),
        name="main_cells",
    )(edge_values, inner, low, high, fall, left, right, across_taps(512, 256), down_taps(STEP))


def out_shapes(rows, cols):
    return [
        jax.ShapeDtypeStruct((rows, cols), F32),
        jax.ShapeDtypeStruct((rows, cols), F32),
        jax.ShapeDtypeStruct((8, rows, cols), BF16),
    ]


def cost(cells_done):
    return pl.CostEstimate(
        flops=cells_done * 4000, bytes_accessed=cells_done * 24, transcendentals=cells_done * 2
    )


def unpack_left(value, q):
    value = value.astype(F32)
    return value if q == 3 else pltpu.roll(value, 96 - PAD * q, 1)


def unpack_right(value, q):
    value = value.astype(F32)
    return value if q == 0 else pltpu.roll(value, 128 - PAD * q, 1)


def ends_kernel(
    edge_ref, inner_ref, band_ref, left_ref, right_ref, up_ref, down_ref, across, down,
    relief_in, slope_in, flow_in, relief_hbm, slope_hbm, flow_hbm,
    relief, slope, flow, wide, band, low_ref, high_ref, sems,
):
    rows, cols = band_ref.shape
    lanes = cols // 128
    near = 2 * PAD
    tall = PAD + 16
    inverse = 1.0 / (tap_total() ** 2)
    packed = left_ref.shape[0]
    for e in range(2):
        here = slice(PAD, PAD + near) if e == 0 else slice(0, near)
        there = slice(0, PAD) if e == 0 else slice(near, near + PAD)
        other = down_ref if e else up_ref
        top = e * tall
        own_rows = slice(rows - near, rows) if e else slice(0, near)
        pack_rows = slice(packed - near, packed) if e else slice(0, near)
        band[e, here, 128 : 128 + cols] = band_ref[own_rows, :]
        band[e, there, 128 : 128 + cols] = other[:, 0:cols]
        far_left = unpack_left(left_ref[pack_rows, :], 3 * e)
        far_right = unpack_right(right_ref[pack_rows, :], 3 * e)
        corner_left = unpack_left(other[:, cols : cols + 128], 0 if e else 3)
        corner_right = unpack_right(other[:, cols + 128 : cols + 256], 0 if e else 3)
        band[e, here, 0:128] = far_left.astype(BF16)
        band[e, there, 0:128] = corner_left.astype(BF16)
        band[e, here, 128 + cols :] = far_right.astype(BF16)
        band[e, there, 128 + cols :] = corner_right.astype(BF16)
        if e == 0:
            wide[0, top : top + 8, :] = corner_left[PAD - 8 : PAD]
            wide[0, top + 8 : top + 48, :] = far_left[0:40]
            wide[lanes + 1, top : top + 8, :] = corner_right[PAD - 8 : PAD]
            wide[lanes + 1, top + 8 : top + 48, :] = far_right[0:40]
        else:
            wide[0, top : top + 40, :] = far_left[near - 40 : near]
            wide[0, top + 40 : top + 48, :] = corner_left[0:8]
            wide[lanes + 1, top : top + 40, :] = far_right[near - 40 : near]
            wide[lanes + 1, top + 40 : top + 48, :] = corner_right[0:8]
        for j in range(lanes):
            part = other[:, j * 128 : (j + 1) * 128].astype(F32)
            own = edge_ref.at[int(j > 0)] if j in (0, lanes - 1) else inner_ref.at[j - 1]
            if e == 0:
                wide[j + 1, top : top + 8, :] = part[PAD - 8 : PAD]
                wide[j + 1, top + 8 : top + 48, :] = own[0:40, :]
            else:
                wide[j + 1, top : top + 40, :] = own[rows - 40 : rows, :]
                wide[j + 1, top + 40 : top + 48, :] = part[0:8]

    for e in range(2):
        smooth = dot(down[...], band[e]).astype(BF16)
        for j in range(lanes // 2):
            value = dot(smooth[:, j * 256 : j * 256 + 512], across[...])
            for h in range(2):
                at = j * 256 + h * 128
                relief[e, :, at : at + 128] = (
                    wide[j * 2 + h + 1, e * tall + 8 : e * tall + 8 + PAD, :] - value[:, h * 128 : h * 128 + 128] * inverse
                )
    for j in range(lanes):
        low, high = sideways(wide[j + 1], wide[j], wide[j + 2])
        low_ref[j] = low
        high_ref[j] = high

    def one_end(e, carry):
        for at in range(0, PAD, 16):
            top = pl.multiple_of(e * tall + 8 + at, 8)
            for j in range(lanes):
                value, parts = cells(
                    lambda d: wide[j + 1, pl.ds(top + d, 16), :],
                    lambda d: low_ref[j, pl.ds(top + d, 16), :],
                    lambda d: high_ref[j, pl.ds(top + d, 16), :],
                )
                place = (slice(at, at + 16), slice(j * 128, (j + 1) * 128))
                slope[(e,) + place] = value
                for n, part in enumerate(parts):
                    flow[(e, n) + place] = part
        place = pl.ds(pl.multiple_of(e * (rows - PAD), PAD), PAD)
        pltpu.make_async_copy(relief.at[e], relief_hbm.at[place], sems.at[e, 0]).start()
        pltpu.make_async_copy(slope.at[e], slope_hbm.at[place], sems.at[e, 1]).start()
        pltpu.make_async_copy(flow.at[e], flow_hbm.at[:, place], sems.at[e, 2]).start()
        return carry

    lax.fori_loop(0, 2, one_end, 0)
    for e in range(2):
        place = pl.ds(e * (rows - PAD), PAD)
        pltpu.make_async_copy(relief.at[e], relief_hbm.at[place], sems.at[e, 0]).wait()
        pltpu.make_async_copy(slope.at[e], slope_hbm.at[place], sems.at[e, 1]).wait()
        pltpu.make_async_copy(flow.at[e], flow_hbm.at[:, place], sems.at[e, 2]).wait()


def ends(edge_values, inner, band, left, right, up, down, outs):
    rows, cols = band.shape
    lanes = cols // 128
    return pl.pallas_call(
        ends_kernel,
        out_shape=out_shapes(rows, cols),
        in_specs=[VMEM] * 9 + [ANY] * 3,
        out_specs=[ANY] * 3,
        input_output_aliases={9: 0, 10: 1, 11: 2},
        scratch_shapes=[
            pltpu.VMEM((2, PAD, cols), F32),
            pltpu.VMEM((2, PAD, cols), F32),
            pltpu.VMEM((2, 8, PAD, cols), BF16),
            pltpu.VMEM((lanes + 2, 2 * (PAD + 16), 128), F32),
            pltpu.VMEM((2, 3 * PAD, cols + 256), BF16),
            pltpu.VMEM((lanes, 2 * (PAD + 16), 128), F32),
            pltpu.VMEM((lanes, 2 * (PAD + 16), 128), F32),
            pltpu.SemaphoreType.DMA((2, 3)),
        ],
        cost_estimate=cost(2 * PAD * cols),
        compiler_params=pltpu.CompilerParams(vmem_limit_bytes=16 * MIB),
        name="end_cells",
    )(
        edge_values, inner, band, left, right, up, down,
        across_taps(512, 256), down_taps(PAD), *outs,
    )


def exchange(low, high, axis):
    devices = lax.axis_size(axis)
    up = [(i, i + 1) for i in range(devices - 1)]
    down = [(j, i) for i, j in up]
    return lax.ppermute(high, axis, up), lax.ppermute(low, axis, down)


def local(source_blocks, block_scale, block_list, block_count, row_weights, col_weights):
    holders = lax.axis_size("gy")
    edge = source_blocks.shape[1]
    block_list = block_list.T
    outgoing = gather(block_list, block_count, block_scale, source_blocks)
    arrived = lax.all_to_all(
        outgoing, "gy", split_axis=0, concat_axis=0, tiled=True
    ).reshape(holders * CAP, edge, edge)
    weights = (row_weights, col_weights)
    edge_values, left, right = edges(block_list, block_count, arrived, *weights)
    before, after = exchange(left, right, "gx")
    inner, low, high, band, fall = middle(block_list, block_count, arrived, *weights, edge_values)
    top = jnp.concatenate([band[:PAD], before[:PAD], after[:PAD]], axis=1)
    bottom = jnp.concatenate([band[-PAD:], before[-PAD:], after[-PAD:]], axis=1)
    above, below = exchange(top, bottom, "gy")
    outs = main(edge_values, inner, low, high, fall, before, after)
    return tuple(ends(edge_values, inner, band, before, after, above, below, outs))


def solution(mesh):
    in_specs = (
        P(("gx", "gy"), None, None),
        P(("gx", "gy")),
        P(),
        P(),
        P(("gx", "gy"), None, None),
        P(("gx", "gy"), None, None),
    )
    out_specs = (P("gy", "gx"), P("gy", "gx"), P(None, "gy", "gx"))
    return jax.shard_map(local, mesh=mesh, in_specs=in_specs, out_specs=out_specs, check_vma=False)
```

```python
import jax
import jax.numpy as jnp
import ml_dtypes
import numpy as np
from jax import lax
from jax.experimental import pallas as pl
from jax.experimental.pallas import tpu as pltpu
from jax.sharding import PartitionSpec as P

W = 6
CAP = 4
RIM = 24
PAD = 32
SIGMA = 10.0
FLAT = 0.05
DIAG = 0.5**0.5
F32 = jnp.float32
BF16 = jnp.bfloat16
MIB = 1 << 20

SMEM = pl.BlockSpec(memory_space=pltpu.SMEM)
VMEM = pl.BlockSpec(memory_space=pltpu.VMEM)
ANY = pl.BlockSpec(memory_space=pl.ANY)


def gather_kernel(
    list_hbm, count_hbm, scale_hbm, blocks_hbm, out_hbm,
    listed, counted, scale, blocks, found, table, staged, sems, out_sems,
):
    holders = lax.axis_size("gy")
    first = lax.axis_index("gx") * holders
    held = blocks.shape[0]
    base = (first + lax.axis_index("gy")) * held
    slots = listed.shape[0]
    copies = [
        pltpu.make_async_copy(list_hbm, listed, sems.at[0]),
        pltpu.make_async_copy(count_hbm, counted, sems.at[1]),
        pltpu.make_async_copy(scale_hbm, scale, sems.at[2]),
        pltpu.make_async_copy(blocks_hbm, blocks, sems.at[3]),
    ]
    for copy in copies:
        copy.start()
    copies[0].wait()
    copies[1].wait()
    shape = found.shape
    row = lax.broadcasted_iota(jnp.int32, shape, 0)
    live = jnp.broadcast_to(counted[...], shape)
    rank = jnp.zeros(shape, jnp.int32)
    chosen = jnp.zeros(shape, jnp.int32)
    for k in range(slots):
        block = jnp.broadcast_to(listed[k : k + 1, :], shape) - base
        hit = (block >= 0) & (block < held) & (k < live)
        chosen = jnp.where(hit & (rank == row), block, chosen)
        rank = rank + hit.astype(jnp.int32)
    found[...] = chosen
    handed = pltpu.make_async_copy(found, table, sems.at[4])
    handed.start()
    handed.wait()
    copies[2].wait()
    copies[3].wait()

    def one_tile(t, carry):
        for j in range(CAP):
            block = table[j, first + t]
            value = blocks[block].astype(F32) * scale[block]
            staged[t, j] = value.astype(BF16)
        pltpu.make_async_copy(staged.at[t], out_hbm.at[t], out_sems.at[t]).start()
        return carry

    lax.fori_loop(0, holders, one_tile, 0)
    for t in range(out_hbm.shape[0]):
        pltpu.make_async_copy(staged.at[t], out_hbm.at[t], out_sems.at[t]).wait()


def gather(block_list, block_count, block_scale, source_blocks):
    held, edge, _ = source_blocks.shape
    holders = lax.axis_size("gy")
    slots, tiles = block_list.shape
    return pl.pallas_call(
        gather_kernel,
        out_shape=jax.ShapeDtypeStruct((holders, CAP, edge, edge), BF16),
        in_specs=[ANY] * 4,
        out_specs=ANY,
        scratch_shapes=[
            pltpu.VMEM((slots, tiles), jnp.int32),
            pltpu.VMEM((1, tiles), jnp.int32),
            pltpu.SMEM((held,), F32),
            pltpu.VMEM((held, edge, edge), BF16),
            pltpu.VMEM((8, tiles), jnp.int32),
            pltpu.SMEM((8, tiles), jnp.int32),
            pltpu.VMEM((holders, CAP, edge, edge), BF16),
            pltpu.SemaphoreType.DMA((5,)),
            pltpu.SemaphoreType.DMA((holders,)),
        ],
        compiler_params=pltpu.CompilerParams(vmem_limit_bytes=56 * MIB),
        name="gather_blocks",
    )(block_list, block_count.reshape(1, tiles), block_scale, source_blocks)


def find_sources(list_ref, count_ref, source, seen):
    holders = lax.axis_size("gy")
    first = lax.axis_index("gx") * holders
    tile = first + lax.axis_index("gy")
    held = 32
    live = count_ref[tile]
    for h in range(holders):
        seen[h] = 0
    for k in range(list_ref.shape[0]):
        owner = (list_ref[k, tile] - first * held) // held
        owner = jnp.clip(owner, 0, holders - 1)
        rank = seen[owner]
        source[k] = owner * CAP + jnp.minimum(rank, CAP - 1)
        seen[owner] = rank + (k < live).astype(jnp.int32)
    return live


def window(k, live, source, arrived_ref, row_ref, col_ref):
    part = dot(row_ref[k], arrived_ref[source[k]])
    part = jnp.where(k < live, part, 0.0).astype(BF16)
    return dot(part, col_ref[k])


def edges_kernel(
    list_ref, count_ref, arrived_ref, row_ref, col_ref, edge_ref, left_ref, right_ref, source, seen
):
    edge = row_ref.shape[1]
    live = find_sources(list_ref, count_ref, source, seen)
    for i in range(W):
        for s in range(2):
            k = i * W + s * (W - 1)
            edge_ref[s, i * edge : (i + 1) * edge, :] = window(
                k, live, source, arrived_ref, row_ref, col_ref
            )
    rows = edge_ref.shape[1]
    chunk = rows // 4
    lane = lax.broadcasted_iota(jnp.int32, (chunk, 128), 1)
    left = jnp.zeros((chunk, 128), F32)
    right = jnp.zeros((chunk, 128), F32)
    for q in range(4):
        mine = (lane >= PAD * q) & (lane < PAD * (q + 1))
        part = edge_ref[0, q * chunk : (q + 1) * chunk, :]
        if q:
            part = pltpu.roll(part, PAD * q, 1)
        left = jnp.where(mine, part, left)
        part = edge_ref[1, q * chunk : (q + 1) * chunk, :]
        if q != 3:
            part = pltpu.roll(part, PAD * (q + 1), 1)
        right = jnp.where(mine, part, right)
    left_ref[...] = left.astype(BF16)
    right_ref[...] = right.astype(BF16)


def edges(block_list, block_count, arrived, row_weights, col_weights):
    slots, edge, _ = row_weights.shape
    side = W * edge
    shapes = [((2, side, edge), F32), ((side // 4, 128), BF16), ((side // 4, 128), BF16)]
    return pl.pallas_call(
        edges_kernel,
        out_shape=[jax.ShapeDtypeStruct(s, d) for s, d in shapes],
        in_specs=[SMEM, SMEM, VMEM, VMEM, VMEM],
        out_specs=[VMEM] * len(shapes),
        scratch_shapes=[
            pltpu.SMEM((slots,), jnp.int32),
            pltpu.SMEM((lax.axis_size("gy"),), jnp.int32),
        ],
        cost_estimate=cost(side * 256),
        compiler_params=pltpu.CompilerParams(vmem_limit_bytes=16 * MIB),
        name="edge_windows",
    )(block_list, block_count, arrived, row_weights, col_weights)


def middle_kernel(
    list_ref, count_ref, arrived_ref, row_ref, col_ref, edge_ref, down,
    inner_ref, low_ref, high_ref, band_ref, fall_ref, source, seen,
):
    edge = row_ref.shape[1]
    rows = band_ref.shape[0]
    live = find_sources(list_ref, count_ref, source, seen)
    for s in range(2):
        band_ref[:, s * (W - 1) * edge : (s * (W - 1) + 1) * edge] = edge_ref[s].astype(BF16)

    for i in range(W):
        span = slice(i * edge, (i + 1) * edge)
        for j in range(1, W - 1):
            value = window(i * W + j, live, source, arrived_ref, row_ref, col_ref)
            inner_ref[j - 1, span, :] = value
            band_ref[span, j * edge : (j + 1) * edge] = value.astype(BF16)
    for i in range((rows - 2 * PAD) // STEP):
        value = dot(down[...], band_ref[i * STEP : (i + 1) * STEP + 2 * PAD, :])
        fall_ref[i * STEP : (i + 1) * STEP, :] = value.astype(BF16)

    def one_span(q, carry):
        span = pl.ds(pl.multiple_of(q * edge, edge), edge)
        pieces = [edge_ref[0, span, :]]
        pieces += [inner_ref[j, span, :] for j in range(W - 2)] + [edge_ref[1, span, :]]
        lane = lax.broadcasted_iota(jnp.int32, pieces[0].shape, 1)
        lows = [pltpu.roll(piece, 1, 1) for piece in pieces]
        highs = [pltpu.roll(piece, 127, 1) for piece in pieces]
        for j in range(W):
            low_ref[j, span, :] = jnp.where(lane == 0, lows[j - 1], lows[j]) if j else lows[j]
            high_ref[j, span, :] = (
                jnp.where(lane == 127, highs[j + 1], highs[j]) if j < W - 1 else highs[j]
            )
        return carry

    lax.fori_loop(0, W, one_span, 0)


def middle(block_list, block_count, arrived, row_weights, col_weights, edge_values):
    slots, edge, _ = row_weights.shape
    side = W * edge
    shapes = [
        ((W - 2, side, edge), F32),
        ((W, side, edge), F32),
        ((W, side, edge), F32),
        ((side, side), BF16),
        ((side - 2 * PAD, side), BF16),
    ]
    return pl.pallas_call(
        middle_kernel,
        out_shape=[jax.ShapeDtypeStruct(s, d) for s, d in shapes],
        in_specs=[SMEM, SMEM] + [VMEM] * 5,
        out_specs=[VMEM] * len(shapes),
        scratch_shapes=[
            pltpu.SMEM((slots,), jnp.int32),
            pltpu.SMEM((lax.axis_size("gy"),), jnp.int32),
        ],
        cost_estimate=cost(side * side),
        compiler_params=pltpu.CompilerParams(vmem_limit_bytes=24 * MIB),
        name="middle_windows",
    )(block_list, block_count, arrived, row_weights, col_weights, edge_values, down_taps(STEP))


def tap(offset):
    value = np.exp(-(offset * offset).astype(np.float32) / np.float32(2.0 * SIGMA * SIGMA))
    return np.where(np.abs(offset) <= RIM, value, 0.0).astype(ml_dtypes.bfloat16)


def tap_total():
    return float(np.sum(tap(np.arange(-RIM, RIM + 1)).astype(np.float64)))


def across_taps(wide, out):
    return jnp.asarray(tap(np.arange(wide)[:, None] - np.arange(out)[None, :] - 128))


def down_taps(step):
    return jnp.asarray(tap(np.arange(step + 2 * PAD)[None, :] - np.arange(step)[:, None] - PAD))


def cells(mid, low, high):
    centre = mid(0)
    ul, uc, ur = low(-1), mid(-1), high(-1)
    cl, cr = low(0), high(0)
    dl, dc, dr = low(1), mid(1), high(1)
    one = dr - ul
    two = ur - dl
    grad_x = one + two + 2.0 * (cr - cl)
    grad_y = one - two + 2.0 * (dc - uc)
    square = 1.0 + (grad_x * grad_x + grad_y * grad_y) * (1.0 / 64.0)
    slope = square * lax.rsqrt(square)
    flows = []
    own = centre.astype(BF16)
    for value, diagonal in (
        (ul, True), (uc, False), (ur, True), (cl, False),
        (cr, False), (dl, True), (dc, False), (dr, True),
    ):
        drop = jnp.maximum(own - value.astype(BF16), 0)
        flows.append((drop * BF16(DIAG) if diagonal else drop) + BF16(FLAT))
    total = (
        ((flows[0] + flows[1]) + (flows[2] + flows[3]))
        + ((flows[4] + flows[5]) + (flows[6] + flows[7]))
    )
    share = pl.reciprocal(total.astype(F32), approx=True).astype(BF16)
    return slope, [flow * share for flow in flows]


def sideways(centre, before, after):
    lane = lax.broadcasted_iota(jnp.int32, centre.shape, 1)
    low = jnp.where(lane == 0, pltpu.roll(before, 1, 1), pltpu.roll(centre, 1, 1))
    high = jnp.where(lane == 127, pltpu.roll(after, 127, 1), pltpu.roll(centre, 127, 1))
    return low, high


def dot(a, b):
    return jnp.dot(a, b, preferred_element_type=F32)


STEP = 176


def main_kernel(
    edge_ref, inner_ref, low_ref, high_ref, fall_ref, left_ref, right_ref, across, down,
    relief_hbm, slope_hbm, flow_hbm, relief, slope, flow, far, patched, sems,
):
    rows, cols = low_ref.shape[1], relief.shape[1]
    lanes = cols // 128
    steps = (rows - 2 * PAD) // STEP
    chunk = rows // 4
    inverse = 1.0 / (tap_total() ** 2)
    lane = lax.broadcasted_iota(jnp.int32, (chunk, 128), 1)
    for q in range(4):
        span = slice(q * chunk, (q + 1) * chunk)
        value = unpack_left(left_ref[...], q)
        far[0, span, :] = value.astype(BF16)
        patched[0, span, :] = jnp.where(lane == 0, pltpu.roll(value, 1, 1), low_ref[0, span, :])
        value = unpack_right(right_ref[...], q)
        far[1, span, :] = value.astype(BF16)
        patched[1, span, :] = jnp.where(
            lane == 127, pltpu.roll(value, 127, 1), high_ref[lanes - 1, span, :]
        )

    def copies(i):
        span = pl.ds(pl.multiple_of(i * STEP, 16), STEP)
        place = pl.ds(pl.multiple_of(PAD + i * STEP, 16), STEP)
        return (
            pltpu.make_async_copy(relief.at[span], relief_hbm.at[place], sems.at[i, 0]),
            pltpu.make_async_copy(slope.at[span], slope_hbm.at[place], sems.at[i, 1]),
            pltpu.make_async_copy(flow.at[:, span], flow_hbm.at[:, place], sems.at[i, 2]),
        )

    def mid(j, span):
        if j in (0, lanes - 1):
            return edge_ref[int(j > 0), span, :]
        return inner_ref[j - 1, span, :]

    def low(j, span):
        return low_ref[j, span, :] if j else patched[0, span, :]

    def high(j, span):
        return high_ref[j, span, :] if j < lanes - 1 else patched[1, span, :]

    def one_step(i, carry):
        base = pl.multiple_of(i * STEP, 16)
        tall = pl.ds(base, STEP + 2 * PAD)
        span = pl.ds(base, STEP)
        sides = [dot(down[...], far[s, tall, :]).astype(BF16) for s in range(2)]
        for j in range(lanes // 2):
            at = j * 256
            if j == 0:
                wide = jnp.concatenate([sides[0], fall_ref[span, 0:384]], axis=1)
            elif j == lanes // 2 - 1:
                wide = jnp.concatenate([fall_ref[span, at - 128 :], sides[1]], axis=1)
            else:
                wide = fall_ref[span, at - 128 : at + 384]
            value = dot(wide, across[...])
            for h in range(2):
                centre = mid(j * 2 + h, pl.ds(base + PAD, STEP))
                relief[span, at + h * 128 : at + h * 128 + 128] = (
                    centre - value[:, h * 128 : h * 128 + 128] * inverse
                )
        for q in range(STEP // 16):
            at = pl.multiple_of(base + q * 16, 16)
            for j in range(lanes):
                value, parts = cells(
                    lambda d: mid(j, pl.ds(at + PAD + d, 16)),
                    lambda d: low(j, pl.ds(at + PAD + d, 16)),
                    lambda d: high(j, pl.ds(at + PAD + d, 16)),
                )
                place = (pl.ds(at, 16), slice(j * 128, (j + 1) * 128))
                slope[place] = value
                for n, part in enumerate(parts):
                    flow[(n,) + place] = part
        for copy in copies(i):
            copy.start()
        return carry

    lax.fori_loop(0, steps, one_step, 0)
    for i in range(steps):
        for copy in copies(i):
            copy.wait()


def main(edge_values, inner, low, high, fall, left, right):
    lanes, rows, _ = low.shape
    cols = lanes * 128
    tall = rows - 2 * PAD
    return pl.pallas_call(
        main_kernel,
        out_shape=out_shapes(rows, cols),
        in_specs=[VMEM] * 9,
        out_specs=[ANY] * 3,
        scratch_shapes=[
            pltpu.VMEM((tall, cols), F32),
            pltpu.VMEM((tall, cols), F32),
            pltpu.VMEM((8, tall, cols), BF16),
            pltpu.VMEM((2, rows, 128), BF16),
            pltpu.VMEM((2, rows, 128), F32),
            pltpu.SemaphoreType.DMA((tall // STEP, 3)),
        ],
        cost_estimate=cost(tall * cols),
        compiler_params=pltpu.CompilerParams(vmem_limit_bytes=32 * MIB),
        name="main_cells",
    )(edge_values, inner, low, high, fall, left, right, across_taps(512, 256), down_taps(STEP))


def out_shapes(rows, cols):
    return [
        jax.ShapeDtypeStruct((rows, cols), F32),
        jax.ShapeDtypeStruct((rows, cols), F32),
        jax.ShapeDtypeStruct((8, rows, cols), BF16),
    ]


def cost(cells_done):
    return pl.CostEstimate(
        flops=cells_done * 4000, bytes_accessed=cells_done * 24, transcendentals=cells_done * 2
    )


def unpack_left(value, q):
    value = value.astype(F32)
    return value if q == 3 else pltpu.roll(value, 96 - PAD * q, 1)


def unpack_right(value, q):
    value = value.astype(F32)
    return value if q == 0 else pltpu.roll(value, 128 - PAD * q, 1)


def ends_kernel(
    edge_ref, inner_ref, band_ref, left_ref, right_ref, up_ref, down_ref, across, down,
    relief_in, slope_in, flow_in, relief_hbm, slope_hbm, flow_hbm,
    relief, slope, flow, wide, band, low_ref, high_ref, sems,
):
    rows, cols = band_ref.shape
    lanes = cols // 128
    near = 2 * PAD
    tall = PAD + 16
    inverse = 1.0 / (tap_total() ** 2)
    packed = left_ref.shape[0]
    for e in range(2):
        here = slice(PAD, PAD + near) if e == 0 else slice(0, near)
        there = slice(0, PAD) if e == 0 else slice(near, near + PAD)
        other = down_ref if e else up_ref
        top = e * tall
        own_rows = slice(rows - near, rows) if e else slice(0, near)
        pack_rows = slice(packed - near, packed) if e else slice(0, near)
        band[e, here, 128 : 128 + cols] = band_ref[own_rows, :]
        band[e, there, 128 : 128 + cols] = other[:, 0:cols]
        far_left = unpack_left(left_ref[pack_rows, :], 3 * e)
        far_right = unpack_right(right_ref[pack_rows, :], 3 * e)
        corner_left = unpack_left(other[:, cols : cols + 128], 0 if e else 3)
        corner_right = unpack_right(other[:, cols + 128 : cols + 256], 0 if e else 3)
        band[e, here, 0:128] = far_left.astype(BF16)
        band[e, there, 0:128] = corner_left.astype(BF16)
        band[e, here, 128 + cols :] = far_right.astype(BF16)
        band[e, there, 128 + cols :] = corner_right.astype(BF16)
        if e == 0:
            wide[0, top : top + 8, :] = corner_left[PAD - 8 : PAD]
            wide[0, top + 8 : top + 48, :] = far_left[0:40]
            wide[lanes + 1, top : top + 8, :] = corner_right[PAD - 8 : PAD]
            wide[lanes + 1, top + 8 : top + 48, :] = far_right[0:40]
        else:
            wide[0, top : top + 40, :] = far_left[near - 40 : near]
            wide[0, top + 40 : top + 48, :] = corner_left[0:8]
            wide[lanes + 1, top : top + 40, :] = far_right[near - 40 : near]
            wide[lanes + 1, top + 40 : top + 48, :] = corner_right[0:8]
        for j in range(lanes):
            part = other[:, j * 128 : (j + 1) * 128].astype(F32)
            own = edge_ref.at[int(j > 0)] if j in (0, lanes - 1) else inner_ref.at[j - 1]
            if e == 0:
                wide[j + 1, top : top + 8, :] = part[PAD - 8 : PAD]
                wide[j + 1, top + 8 : top + 48, :] = own[0:40, :]
            else:
                wide[j + 1, top : top + 40, :] = own[rows - 40 : rows, :]
                wide[j + 1, top + 40 : top + 48, :] = part[0:8]

    for e in range(2):
        smooth = dot(down[...], band[e]).astype(BF16)
        for j in range(lanes // 2):
            value = dot(smooth[:, j * 256 : j * 256 + 512], across[...])
            for h in range(2):
                at = j * 256 + h * 128
                relief[e, :, at : at + 128] = (
                    wide[j * 2 + h + 1, e * tall + 8 : e * tall + 8 + PAD, :] - value[:, h * 128 : h * 128 + 128] * inverse
                )
    for j in range(lanes):
        low, high = sideways(wide[j + 1], wide[j], wide[j + 2])
        low_ref[j] = low
        high_ref[j] = high

    def one_end(e, carry):
        for at in range(0, PAD, 16):
            top = pl.multiple_of(e * tall + 8 + at, 8)
            for j in range(lanes):
                value, parts = cells(
                    lambda d: wide[j + 1, pl.ds(top + d, 16), :],
                    lambda d: low_ref[j, pl.ds(top + d, 16), :],
                    lambda d: high_ref[j, pl.ds(top + d, 16), :],
                )
                place = (slice(at, at + 16), slice(j * 128, (j + 1) * 128))
                slope[(e,) + place] = value
                for n, part in enumerate(parts):
                    flow[(e, n) + place] = part
        place = pl.ds(pl.multiple_of(e * (rows - PAD), PAD), PAD)
        pltpu.make_async_copy(relief.at[e], relief_hbm.at[place], sems.at[e, 0]).start()
        pltpu.make_async_copy(slope.at[e], slope_hbm.at[place], sems.at[e, 1]).start()
        pltpu.make_async_copy(flow.at[e], flow_hbm.at[:, place], sems.at[e, 2]).start()
        return carry

    lax.fori_loop(0, 2, one_end, 0)
    for e in range(2):
        place = pl.ds(e * (rows - PAD), PAD)
        pltpu.make_async_copy(relief.at[e], relief_hbm.at[place], sems.at[e, 0]).wait()
        pltpu.make_async_copy(slope.at[e], slope_hbm.at[place], sems.at[e, 1]).wait()
        pltpu.make_async_copy(flow.at[e], flow_hbm.at[:, place], sems.at[e, 2]).wait()


def ends(edge_values, inner, band, left, right, up, down, outs):
    rows, cols = band.shape
    lanes = cols // 128
    return pl.pallas_call(
        ends_kernel,
        out_shape=out_shapes(rows, cols),
        in_specs=[VMEM] * 9 + [ANY] * 3,
        out_specs=[ANY] * 3,
        input_output_aliases={9: 0, 10: 1, 11: 2},
        scratch_shapes=[
            pltpu.VMEM((2, PAD, cols), F32),
            pltpu.VMEM((2, PAD, cols), F32),
            pltpu.VMEM((2, 8, PAD, cols), BF16),
            pltpu.VMEM((lanes + 2, 2 * (PAD + 16), 128), F32),
            pltpu.VMEM((2, 3 * PAD, cols + 256), BF16),
            pltpu.VMEM((lanes, 2 * (PAD + 16), 128), F32),
            pltpu.VMEM((lanes, 2 * (PAD + 16), 128), F32),
            pltpu.SemaphoreType.DMA((2, 3)),
        ],
        cost_estimate=cost(2 * PAD * cols),
        compiler_params=pltpu.CompilerParams(vmem_limit_bytes=16 * MIB),
        name="end_cells",
    )(
        edge_values, inner, band, left, right, up, down,
        across_taps(512, 256), down_taps(PAD), *outs,
    )


def exchange(low, high, axis):
    devices = lax.axis_size(axis)
    up = [(i, i + 1) for i in range(devices - 1)]
    down = [(j, i) for i, j in up]
    return lax.ppermute(high, axis, up), lax.ppermute(low, axis, down)


def local(source_blocks, block_scale, block_list, block_count, row_weights, col_weights):
    holders = lax.axis_size("gy")
    edge = source_blocks.shape[1]
    block_list = block_list.T
    outgoing = gather(block_list, block_count, block_scale, source_blocks)
    arrived = lax.all_to_all(
        outgoing, "gy", split_axis=0, concat_axis=0, tiled=True
    ).reshape(holders * CAP, edge, edge)
    weights = (row_weights, col_weights)
    edge_values, left, right = edges(block_list, block_count, arrived, *weights)
    before, after = exchange(left, right, "gx")
    inner, low, high, band, fall = middle(block_list, block_count, arrived, *weights, edge_values)
    top = jnp.concatenate([band[:PAD], before[:PAD], after[:PAD]], axis=1)
    bottom = jnp.concatenate([band[-PAD:], before[-PAD:], after[-PAD:]], axis=1)
    above, below = exchange(top, bottom, "gy")
    outs = main(edge_values, inner, low, high, fall, before, after)
    return tuple(ends(edge_values, inner, band, before, after, above, below, outs))


def solution(mesh):
    in_specs = (
        P(("gx", "gy"), None, None),
        P(("gx", "gy")),
        P(),
        P(),
        P(("gx", "gy"), None, None),
        P(("gx", "gy"), None, None),
    )
    out_specs = (P("gy", "gx"), P("gy", "gx"), P(None, "gy", "gx"))
    return jax.shard_map(local, mesh=mesh, in_specs=in_specs, out_specs=out_specs, check_vma=False)
```

```python
import jax
import jax.numpy as jnp
import ml_dtypes
import numpy as np
from jax import lax
from jax.experimental import pallas as pl
from jax.experimental.pallas import tpu as pltpu
from jax.sharding import PartitionSpec as P

W = 6
CAP = 4
RIM = 24
PAD = 32
SIGMA = 10.0
FLAT = 0.05
DIAG = 0.5**0.5
F32 = jnp.float32
BF16 = jnp.bfloat16
MIB = 1 << 20

SMEM = pl.BlockSpec(memory_space=pltpu.SMEM)
VMEM = pl.BlockSpec(memory_space=pltpu.VMEM)
ANY = pl.BlockSpec(memory_space=pl.ANY)


def gather_kernel(
    list_hbm, count_hbm, scale_hbm, blocks_hbm, out_hbm, source_hbm,
    listed, counted, scale, blocks, found, table, staged,
    named, numbered, seen, source, sems, out_sems,
):
    holders = lax.axis_size("gy")
    first = lax.axis_index("gx") * holders
    held = blocks.shape[0]
    base = (first + lax.axis_index("gy")) * held
    slots = listed.shape[0]
    copies = [
        pltpu.make_async_copy(list_hbm, listed, sems.at[0]),
        pltpu.make_async_copy(count_hbm, counted, sems.at[1]),
        pltpu.make_async_copy(scale_hbm, scale, sems.at[2]),
        pltpu.make_async_copy(blocks_hbm, blocks, sems.at[3]),
        pltpu.make_async_copy(list_hbm, named, sems.at[5]),
        pltpu.make_async_copy(count_hbm, numbered, sems.at[6]),
    ]
    for copy in copies:
        copy.start()
    copies[0].wait()
    copies[1].wait()
    shape = found.shape
    row = lax.broadcasted_iota(jnp.int32, shape, 0)
    live = jnp.broadcast_to(counted[...], shape)
    rank = jnp.zeros(shape, jnp.int32)
    chosen = jnp.zeros(shape, jnp.int32)
    for k in range(slots):
        block = jnp.broadcast_to(listed[k : k + 1, :], shape) - base
        hit = (block >= 0) & (block < held) & (k < live)
        chosen = jnp.where(hit & (rank == row), block, chosen)
        rank = rank + hit.astype(jnp.int32)
    found[...] = chosen
    handed = pltpu.make_async_copy(found, table, sems.at[4])
    handed.start()
    copies[4].wait()
    copies[5].wait()
    tile = first + lax.axis_index("gy")
    count = numbered[0, tile]
    for h in range(out_hbm.shape[0]):
        seen[h] = 0
    for k in range(slots):
        block = jnp.clip(named[k, tile] - first * held, 0, out_hbm.shape[0] * held - 1)
        owner = lax.shift_right_logical(block, jnp.int32(held.bit_length() - 1))
        rank = seen[owner]
        source[0, k] = owner * CAP + jnp.minimum(rank, CAP - 1)
        seen[owner] = rank + (k < count).astype(jnp.int32)
    source[0, slots] = count
    told = pltpu.make_async_copy(source, source_hbm, sems.at[7])
    told.start()
    handed.wait()
    copies[2].wait()
    copies[3].wait()

    def one_tile(t, carry):
        for j in range(CAP):
            block = table[j, first + t]
            value = blocks[block].astype(F32) * scale[block]
            staged[t, j] = value.astype(BF16)
        pltpu.make_async_copy(staged.at[t], out_hbm.at[t], out_sems.at[t]).start()
        return carry

    lax.fori_loop(0, holders, one_tile, 0)
    for t in range(out_hbm.shape[0]):
        pltpu.make_async_copy(staged.at[t], out_hbm.at[t], out_sems.at[t]).wait()
    told.wait()


def gather(block_list, block_count, block_scale, source_blocks):
    held, edge, _ = source_blocks.shape
    holders = lax.axis_size("gy")
    slots, tiles = block_list.shape
    return pl.pallas_call(
        gather_kernel,
        out_shape=[
            jax.ShapeDtypeStruct((holders, CAP, edge, edge), BF16),
            jax.ShapeDtypeStruct((1, tiles), jnp.int32),
        ],
        in_specs=[ANY] * 4,
        out_specs=[ANY] * 2,
        scratch_shapes=[
            pltpu.VMEM((slots, tiles), jnp.int32),
            pltpu.VMEM((1, tiles), jnp.int32),
            pltpu.SMEM((held,), F32),
            pltpu.VMEM((held, edge, edge), BF16),
            pltpu.VMEM((8, tiles), jnp.int32),
            pltpu.SMEM((8, tiles), jnp.int32),
            pltpu.VMEM((holders, CAP, edge, edge), BF16),
            pltpu.SMEM((slots, tiles), jnp.int32),
            pltpu.SMEM((1, tiles), jnp.int32),
            pltpu.SMEM((holders,), jnp.int32),
            pltpu.SMEM((1, tiles), jnp.int32),
            pltpu.SemaphoreType.DMA((8,)),
            pltpu.SemaphoreType.DMA((holders,)),
        ],
        compiler_params=pltpu.CompilerParams(vmem_limit_bytes=56 * MIB),
        name="gather_blocks",
    )(block_list, block_count.reshape(1, tiles), block_scale, source_blocks)


def window(k, source_ref, arrived_ref, row_ref, col_ref):
    live = source_ref[0, row_ref.shape[0]]
    part = dot(row_ref[k], arrived_ref[source_ref[0, k]])
    part = jnp.where(k < live, part, 0.0).astype(BF16)
    return dot(part, col_ref[k])


def edges_kernel(
    source_ref, arrived_ref, row_ref, col_ref, edge_ref, left_ref, right_ref
):
    edge = row_ref.shape[1]
    for i in range(W):
        for s in range(2):
            k = i * W + s * (W - 1)
            edge_ref[s, i * edge : (i + 1) * edge, :] = window(
                k, source_ref, arrived_ref, row_ref, col_ref
            )
    rows = edge_ref.shape[1]
    chunk = rows // 4
    lane = lax.broadcasted_iota(jnp.int32, (chunk, 128), 1)
    left = jnp.zeros((chunk, 128), F32)
    right = jnp.zeros((chunk, 128), F32)
    for q in range(4):
        mine = (lane >= PAD * q) & (lane < PAD * (q + 1))
        part = edge_ref[0, q * chunk : (q + 1) * chunk, :]
        if q:
            part = pltpu.roll(part, PAD * q, 1)
        left = jnp.where(mine, part, left)
        part = edge_ref[1, q * chunk : (q + 1) * chunk, :]
        if q != 3:
            part = pltpu.roll(part, PAD * (q + 1), 1)
        right = jnp.where(mine, part, right)
    left_ref[...] = left.astype(BF16)
    right_ref[...] = right.astype(BF16)


def edges(source, arrived, row_weights, col_weights):
    edge = row_weights.shape[1]
    side = W * edge
    shapes = [((2, side, edge), F32), ((side // 4, 128), BF16), ((side // 4, 128), BF16)]
    return pl.pallas_call(
        edges_kernel,
        out_shape=[jax.ShapeDtypeStruct(s, d) for s, d in shapes],
        in_specs=[SMEM, VMEM, VMEM, VMEM],
        out_specs=[VMEM] * len(shapes),
        cost_estimate=cost(side * 256),
        compiler_params=pltpu.CompilerParams(vmem_limit_bytes=16 * MIB),
        name="edge_windows",
    )(source, arrived, row_weights, col_weights)


def middle_kernel(
    source_ref, arrived_ref, row_ref, col_ref, edge_ref, down,
    inner_ref, low_ref, high_ref, band_ref, fall_ref,
):
    edge = row_ref.shape[1]
    rows = band_ref.shape[0]
    for s in range(2):
        band_ref[:, s * (W - 1) * edge : (s * (W - 1) + 1) * edge] = edge_ref[s].astype(BF16)

    for i in range(W):
        span = slice(i * edge, (i + 1) * edge)
        for j in range(1, W - 1):
            value = window(i * W + j, source_ref, arrived_ref, row_ref, col_ref)
            inner_ref[j - 1, span, :] = value
            band_ref[span, j * edge : (j + 1) * edge] = value.astype(BF16)
    for i in range((rows - 2 * PAD) // STEP):
        value = dot(down[...], band_ref[i * STEP : (i + 1) * STEP + 2 * PAD, :])
        fall_ref[i * STEP : (i + 1) * STEP, :] = value.astype(BF16)

    def one_span(q, carry):
        span = pl.ds(pl.multiple_of(q * edge, edge), edge)
        pieces = [edge_ref[0, span, :]]
        pieces += [inner_ref[j, span, :] for j in range(W - 2)] + [edge_ref[1, span, :]]
        lane = lax.broadcasted_iota(jnp.int32, pieces[0].shape, 1)
        lows = [pltpu.roll(piece, 1, 1) for piece in pieces]
        highs = [pltpu.roll(piece, 127, 1) for piece in pieces]
        for j in range(W):
            low_ref[j, span, :] = jnp.where(lane == 0, lows[j - 1], lows[j]) if j else lows[j]
            high_ref[j, span, :] = (
                jnp.where(lane == 127, highs[j + 1], highs[j]) if j < W - 1 else highs[j]
            )
        return carry

    lax.fori_loop(0, W, one_span, 0)


def middle(source, arrived, row_weights, col_weights, edge_values):
    edge = row_weights.shape[1]
    side = W * edge
    shapes = [
        ((W - 2, side, edge), F32),
        ((W, side, edge), F32),
        ((W, side, edge), F32),
        ((side, side), BF16),
        ((side - 2 * PAD, side), BF16),
    ]
    return pl.pallas_call(
        middle_kernel,
        out_shape=[jax.ShapeDtypeStruct(s, d) for s, d in shapes],
        in_specs=[SMEM] + [VMEM] * 5,
        out_specs=[VMEM] * len(shapes),
        cost_estimate=cost(side * side),
        compiler_params=pltpu.CompilerParams(vmem_limit_bytes=24 * MIB),
        name="middle_windows",
    )(source, arrived, row_weights, col_weights, edge_values, down_taps(STEP))


def tap(offset):
    value = np.exp(-(offset * offset).astype(np.float32) / np.float32(2.0 * SIGMA * SIGMA))
    return np.where(np.abs(offset) <= RIM, value, 0.0).astype(ml_dtypes.bfloat16)


def tap_total():
    return float(np.sum(tap(np.arange(-RIM, RIM + 1)).astype(np.float64)))


def across_taps(wide, out):
    return jnp.asarray(tap(np.arange(wide)[:, None] - np.arange(out)[None, :] - 128))


def down_taps(step):
    return jnp.asarray(tap(np.arange(step + 2 * PAD)[None, :] - np.arange(step)[:, None] - PAD))


def cells(mid, low, high):
    centre, cl, cr = [load(0).astype(BF16) for load in (mid, low, high)]
    uc, ul, ur = [load(-1).astype(BF16) for load in (mid, low, high)]
    dc, dl, dr = [load(1).astype(BF16) for load in (mid, low, high)]
    one = dr - ul
    two = ur - dl
    across = cr - cl
    along = dc - uc
    grad_x = (one + two) + (across + across)
    grad_y = (one - two) + (along + along)
    steep = (grad_x * grad_x + grad_y * grad_y).astype(F32)
    square = 1.0 + steep * (1.0 / 64.0)
    slope = square * lax.rsqrt(square)
    flows = []
    for value, diagonal in (
        (ul, True), (uc, False), (ur, True), (cl, False),
        (cr, False), (dl, True), (dc, False), (dr, True),
    ):
        drop = jnp.maximum(centre - value, 0)
        flows.append((drop * BF16(DIAG) if diagonal else drop) + BF16(FLAT))
    total = (
        ((flows[0] + flows[1]) + (flows[2] + flows[3]))
        + ((flows[4] + flows[5]) + (flows[6] + flows[7]))
    )
    share = pl.reciprocal(total.astype(F32), approx=True).astype(BF16)
    return slope, [flow * share for flow in flows]


def sideways(centre, before, after):
    lane = lax.broadcasted_iota(jnp.int32, centre.shape, 1)
    low = jnp.where(lane == 0, pltpu.roll(before, 1, 1), pltpu.roll(centre, 1, 1))
    high = jnp.where(lane == 127, pltpu.roll(after, 127, 1), pltpu.roll(centre, 127, 1))
    return low, high


def dot(a, b):
    return jnp.dot(a, b, preferred_element_type=F32)


STEP = 176


def main_kernel(
    edge_ref, inner_ref, low_ref, high_ref, fall_ref, left_ref, right_ref, across, down,
    relief_hbm, slope_hbm, flow_hbm, relief, slope, flow, far, patched, sems,
):
    rows, cols = low_ref.shape[1], relief.shape[1]
    lanes = cols // 128
    steps = (rows - 2 * PAD) // STEP
    chunk = rows // 4
    inverse = 1.0 / (tap_total() ** 2)
    lane = lax.broadcasted_iota(jnp.int32, (chunk, 128), 1)
    for q in range(4):
        span = slice(q * chunk, (q + 1) * chunk)
        value = unpack_left(left_ref[...], q)
        far[0, span, :] = value.astype(BF16)
        patched[0, span, :] = jnp.where(lane == 0, pltpu.roll(value, 1, 1), low_ref[0, span, :])
        value = unpack_right(right_ref[...], q)
        far[1, span, :] = value.astype(BF16)
        patched[1, span, :] = jnp.where(
            lane == 127, pltpu.roll(value, 127, 1), high_ref[lanes - 1, span, :]
        )

    def copies(i):
        span = pl.ds(pl.multiple_of(i * STEP, 16), STEP)
        place = pl.ds(pl.multiple_of(PAD + i * STEP, 16), STEP)
        return (
            pltpu.make_async_copy(relief.at[span], relief_hbm.at[place], sems.at[i, 0]),
            pltpu.make_async_copy(slope.at[span], slope_hbm.at[place], sems.at[i, 1]),
            pltpu.make_async_copy(flow.at[:, span], flow_hbm.at[:, place], sems.at[i, 2]),
        )

    def mid(j, span):
        if j in (0, lanes - 1):
            return edge_ref[int(j > 0), span, :]
        return inner_ref[j - 1, span, :]

    def low(j, span):
        return low_ref[j, span, :] if j else patched[0, span, :]

    def high(j, span):
        return high_ref[j, span, :] if j < lanes - 1 else patched[1, span, :]

    def one_step(i, carry):
        base = pl.multiple_of(i * STEP, 16)
        tall = pl.ds(base, STEP + 2 * PAD)
        span = pl.ds(base, STEP)
        sides = [dot(down[...], far[s, tall, :]).astype(BF16) for s in range(2)]
        for j in range(lanes // 2):
            at = j * 256
            if j == 0:
                wide = jnp.concatenate([sides[0], fall_ref[span, 0:384]], axis=1)
            elif j == lanes // 2 - 1:
                wide = jnp.concatenate([fall_ref[span, at - 128 :], sides[1]], axis=1)
            else:
                wide = fall_ref[span, at - 128 : at + 384]
            value = dot(wide, across[...])
            for h in range(2):
                centre = mid(j * 2 + h, pl.ds(base + PAD, STEP))
                relief[span, at + h * 128 : at + h * 128 + 128] = (
                    centre - value[:, h * 128 : h * 128 + 128] * inverse
                )
        for q in range(STEP // 16):
            at = pl.multiple_of(base + q * 16, 16)
            for j in range(lanes):
                value, parts = cells(
                    lambda d: mid(j, pl.ds(at + PAD + d, 16)),
                    lambda d: low(j, pl.ds(at + PAD + d, 16)),
                    lambda d: high(j, pl.ds(at + PAD + d, 16)),
                )
                place = (pl.ds(at, 16), slice(j * 128, (j + 1) * 128))
                slope[place] = value
                for n, part in enumerate(parts):
                    flow[(n,) + place] = part
        for copy in copies(i):
            copy.start()
        return carry

    lax.fori_loop(0, steps, one_step, 0)
    for i in range(steps):
        for copy in copies(i):
            copy.wait()


def main(edge_values, inner, low, high, fall, left, right):
    lanes, rows, _ = low.shape
    cols = lanes * 128
    tall = rows - 2 * PAD
    return pl.pallas_call(
        main_kernel,
        out_shape=out_shapes(rows, cols),
        in_specs=[VMEM] * 9,
        out_specs=[ANY] * 3,
        scratch_shapes=[
            pltpu.VMEM((tall, cols), F32),
            pltpu.VMEM((tall, cols), F32),
            pltpu.VMEM((8, tall, cols), BF16),
            pltpu.VMEM((2, rows, 128), BF16),
            pltpu.VMEM((2, rows, 128), F32),
            pltpu.SemaphoreType.DMA((tall // STEP, 3)),
        ],
        cost_estimate=cost(tall * cols),
        compiler_params=pltpu.CompilerParams(vmem_limit_bytes=32 * MIB),
        name="main_cells",
    )(edge_values, inner, low, high, fall, left, right, across_taps(512, 256), down_taps(STEP))


def out_shapes(rows, cols):
    return [
        jax.ShapeDtypeStruct((rows, cols), F32),
        jax.ShapeDtypeStruct((rows, cols), F32),
        jax.ShapeDtypeStruct((8, rows, cols), BF16),
    ]


def cost(cells_done):
    return pl.CostEstimate(
        flops=cells_done * 4000, bytes_accessed=cells_done * 24, transcendentals=cells_done * 2
    )


def unpack_left(value, q):
    value = value.astype(F32)
    return value if q == 3 else pltpu.roll(value, 96 - PAD * q, 1)


def unpack_right(value, q):
    value = value.astype(F32)
    return value if q == 0 else pltpu.roll(value, 128 - PAD * q, 1)


def ends_kernel(
    edge_ref, inner_ref, band_ref, left_ref, right_ref, up_ref, down_ref, across, down,
    relief_in, slope_in, flow_in, relief_hbm, slope_hbm, flow_hbm,
    relief, slope, flow, wide, band, low_ref, high_ref, sems,
):
    rows, cols = band_ref.shape
    lanes = cols // 128
    near = 2 * PAD
    tall = PAD + 16
    inverse = 1.0 / (tap_total() ** 2)
    packed = left_ref.shape[0]
    for e in range(2):
        here = slice(PAD, PAD + near) if e == 0 else slice(0, near)
        there = slice(0, PAD) if e == 0 else slice(near, near + PAD)
        other = down_ref if e else up_ref
        top = e * tall
        own_rows = slice(rows - near, rows) if e else slice(0, near)
        pack_rows = slice(packed - near, packed) if e else slice(0, near)
        band[e, here, 128 : 128 + cols] = band_ref[own_rows, :]
        band[e, there, 128 : 128 + cols] = other[:, 0:cols]
        far_left = unpack_left(left_ref[pack_rows, :], 3 * e)
        far_right = unpack_right(right_ref[pack_rows, :], 3 * e)
        corner_left = unpack_left(other[:, cols : cols + 128], 0 if e else 3)
        corner_right = unpack_right(other[:, cols + 128 : cols + 256], 0 if e else 3)
        band[e, here, 0:128] = far_left.astype(BF16)
        band[e, there, 0:128] = corner_left.astype(BF16)
        band[e, here, 128 + cols :] = far_right.astype(BF16)
        band[e, there, 128 + cols :] = corner_right.astype(BF16)
        if e == 0:
            wide[0, top : top + 8, :] = corner_left[PAD - 8 : PAD]
            wide[0, top + 8 : top + 48, :] = far_left[0:40]
            wide[lanes + 1, top : top + 8, :] = corner_right[PAD - 8 : PAD]
            wide[lanes + 1, top + 8 : top + 48, :] = far_right[0:40]
        else:
            wide[0, top : top + 40, :] = far_left[near - 40 : near]
            wide[0, top + 40 : top + 48, :] = corner_left[0:8]
            wide[lanes + 1, top : top + 40, :] = far_right[near - 40 : near]
            wide[lanes + 1, top + 40 : top + 48, :] = corner_right[0:8]
        for j in range(lanes):
            part = other[:, j * 128 : (j + 1) * 128].astype(F32)
            own = edge_ref.at[int(j > 0)] if j in (0, lanes - 1) else inner_ref.at[j - 1]
            if e == 0:
                wide[j + 1, top : top + 8, :] = part[PAD - 8 : PAD]
                wide[j + 1, top + 8 : top + 48, :] = own[0:40, :]
            else:
                wide[j + 1, top : top + 40, :] = own[rows - 40 : rows, :]
                wide[j + 1, top + 40 : top + 48, :] = part[0:8]

    for e in range(2):
        smooth = dot(down[...], band[e]).astype(BF16)
        for j in range(lanes // 2):
            value = dot(smooth[:, j * 256 : j * 256 + 512], across[...])
            for h in range(2):
                at = j * 256 + h * 128
                relief[e, :, at : at + 128] = (
                    wide[j * 2 + h + 1, e * tall + 8 : e * tall + 8 + PAD, :] - value[:, h * 128 : h * 128 + 128] * inverse
                )
    for j in range(lanes):
        low, high = sideways(wide[j + 1], wide[j], wide[j + 2])
        low_ref[j] = low
        high_ref[j] = high

    def one_end(e, carry):
        for at in range(0, PAD, 16):
            top = pl.multiple_of(e * tall + 8 + at, 8)
            for j in range(lanes):
                value, parts = cells(
                    lambda d: wide[j + 1, pl.ds(top + d, 16), :],
                    lambda d: low_ref[j, pl.ds(top + d, 16), :],
                    lambda d: high_ref[j, pl.ds(top + d, 16), :],
                )
                place = (slice(at, at + 16), slice(j * 128, (j + 1) * 128))
                slope[(e,) + place] = value
                for n, part in enumerate(parts):
                    flow[(e, n) + place] = part
        place = pl.ds(pl.multiple_of(e * (rows - PAD), PAD), PAD)
        pltpu.make_async_copy(relief.at[e], relief_hbm.at[place], sems.at[e, 0]).start()
        pltpu.make_async_copy(slope.at[e], slope_hbm.at[place], sems.at[e, 1]).start()
        pltpu.make_async_copy(flow.at[e], flow_hbm.at[:, place], sems.at[e, 2]).start()
        return carry

    lax.fori_loop(0, 2, one_end, 0)
    for e in range(2):
        place = pl.ds(e * (rows - PAD), PAD)
        pltpu.make_async_copy(relief.at[e], relief_hbm.at[place], sems.at[e, 0]).wait()
        pltpu.make_async_copy(slope.at[e], slope_hbm.at[place], sems.at[e, 1]).wait()
        pltpu.make_async_copy(flow.at[e], flow_hbm.at[:, place], sems.at[e, 2]).wait()


def ends(edge_values, inner, band, left, right, up, down, outs):
    rows, cols = band.shape
    lanes = cols // 128
    return pl.pallas_call(
        ends_kernel,
        out_shape=out_shapes(rows, cols),
        in_specs=[VMEM] * 9 + [ANY] * 3,
        out_specs=[ANY] * 3,
        input_output_aliases={9: 0, 10: 1, 11: 2},
        scratch_shapes=[
            pltpu.VMEM((2, PAD, cols), F32),
            pltpu.VMEM((2, PAD, cols), F32),
            pltpu.VMEM((2, 8, PAD, cols), BF16),
            pltpu.VMEM((lanes + 2, 2 * (PAD + 16), 128), F32),
            pltpu.VMEM((2, 3 * PAD, cols + 256), BF16),
            pltpu.VMEM((lanes, 2 * (PAD + 16), 128), F32),
            pltpu.VMEM((lanes, 2 * (PAD + 16), 128), F32),
            pltpu.SemaphoreType.DMA((2, 3)),
        ],
        cost_estimate=cost(2 * PAD * cols),
        compiler_params=pltpu.CompilerParams(vmem_limit_bytes=16 * MIB),
        name="end_cells",
    )(
        edge_values, inner, band, left, right, up, down,
        across_taps(512, 256), down_taps(PAD), *outs,
    )


def exchange(low, high, axis):
    devices = lax.axis_size(axis)
    even = lax.rem(lax.axis_index(axis), 2) == 0
    swaps = []
    for start in range(2):
        pairs = [(i, i + 1) for i in range(start, devices - 1, 2)]
        swaps.append(pairs + [(j, i) for i, j in pairs])
    first = lax.ppermute(jnp.where(even, high, low), axis, swaps[0])
    second = lax.ppermute(jnp.where(even, low, high), axis, swaps[1])
    return jnp.where(even, second, first), jnp.where(even, first, second)


def local(source_blocks, block_scale, block_list, block_count, row_weights, col_weights):
    holders = lax.axis_size("gy")
    edge = source_blocks.shape[1]
    block_list = block_list.T
    outgoing, source = gather(block_list, block_count, block_scale, source_blocks)
    arrived = lax.all_to_all(
        outgoing, "gy", split_axis=0, concat_axis=0, tiled=True
    ).reshape(holders * CAP, edge, edge)
    weights = (row_weights, col_weights)
    edge_values, left, right = edges(source, arrived, *weights)
    before, after = exchange(left, right, "gx")
    inner, low, high, band, fall = middle(source, arrived, *weights, edge_values)
    top = jnp.concatenate([band[:PAD], before[:PAD], after[:PAD]], axis=1)
    bottom = jnp.concatenate([band[-PAD:], before[-PAD:], after[-PAD:]], axis=1)
    above, below = exchange(top, bottom, "gy")
    outs = main(edge_values, inner, low, high, fall, before, after)
    return tuple(ends(edge_values, inner, band, before, after, above, below, outs))


def solution(mesh):
    in_specs = (
        P(("gx", "gy"), None, None),
        P(("gx", "gy")),
        P(),
        P(),
        P(("gx", "gy"), None, None),
        P(("gx", "gy"), None, None),
    )
    out_specs = (P("gy", "gx"), P("gy", "gx"), P(None, "gy", "gx"))
    return jax.shard_map(local, mesh=mesh, in_specs=in_specs, out_specs=out_specs, check_vma=False)
```

```python
import jax
import jax.numpy as jnp
import ml_dtypes
import numpy as np
from jax import lax
from jax.experimental import pallas as pl
from jax.experimental.pallas import tpu as pltpu
from jax.sharding import PartitionSpec as P

W = 6
CAP = 4
RIM = 24
PAD = 32
SIGMA = 10.0
FLAT = 0.05
DIAG = 0.5**0.5
F32 = jnp.float32
BF16 = jnp.bfloat16
MIB = 1 << 20

SMEM = pl.BlockSpec(memory_space=pltpu.SMEM)
VMEM = pl.BlockSpec(memory_space=pltpu.VMEM)
ANY = pl.BlockSpec(memory_space=pl.ANY)


def gather_kernel(
    list_hbm, count_hbm, scale_hbm, blocks_hbm, out_hbm, source_hbm,
    listed, counted, scale, blocks, found, table, staged,
    named, numbered, seen, source, sems, out_sems,
):
    holders = lax.axis_size("gy")
    first = lax.axis_index("gx") * holders
    held = blocks.shape[0]
    base = (first + lax.axis_index("gy")) * held
    slots = listed.shape[0]
    copies = [
        pltpu.make_async_copy(list_hbm, listed, sems.at[0]),
        pltpu.make_async_copy(count_hbm, counted, sems.at[1]),
        pltpu.make_async_copy(scale_hbm, scale, sems.at[2]),
        pltpu.make_async_copy(blocks_hbm, blocks, sems.at[3]),
        pltpu.make_async_copy(list_hbm, named, sems.at[5]),
        pltpu.make_async_copy(count_hbm, numbered, sems.at[6]),
    ]
    for copy in copies:
        copy.start()
    copies[0].wait()
    copies[1].wait()
    shape = found.shape
    row = lax.broadcasted_iota(jnp.int32, shape, 0)
    live = jnp.broadcast_to(counted[...], shape)
    rank = jnp.zeros(shape, jnp.int32)
    chosen = jnp.zeros(shape, jnp.int32)
    for k in range(slots):
        block = jnp.broadcast_to(listed[k : k + 1, :], shape) - base
        hit = (block >= 0) & (block < held) & (k < live)
        chosen = jnp.where(hit & (rank == row), block, chosen)
        rank = rank + hit.astype(jnp.int32)
    found[...] = chosen
    handed = pltpu.make_async_copy(found, table, sems.at[4])
    handed.start()
    copies[4].wait()
    copies[5].wait()
    tile = first + lax.axis_index("gy")
    count = numbered[0, tile]
    for h in range(out_hbm.shape[0]):
        seen[h] = 0
    for k in range(slots):
        block = jnp.clip(named[k, tile] - first * held, 0, out_hbm.shape[0] * held - 1)
        owner = lax.shift_right_logical(block, jnp.int32(held.bit_length() - 1))
        rank = seen[owner]
        source[0, k] = owner * CAP + jnp.minimum(rank, CAP - 1)
        seen[owner] = rank + (k < count).astype(jnp.int32)
    source[0, slots] = count
    told = pltpu.make_async_copy(source, source_hbm, sems.at[7])
    told.start()
    handed.wait()
    copies[2].wait()
    copies[3].wait()

    def one_tile(t, carry):
        for j in range(CAP):
            block = table[j, first + t]
            value = blocks[block].astype(F32) * scale[block]
            staged[t, j] = value.astype(BF16)
        pltpu.make_async_copy(staged.at[t], out_hbm.at[t], out_sems.at[t]).start()
        return carry

    lax.fori_loop(0, holders, one_tile, 0)
    for t in range(out_hbm.shape[0]):
        pltpu.make_async_copy(staged.at[t], out_hbm.at[t], out_sems.at[t]).wait()
    told.wait()


def gather(block_list, block_count, block_scale, source_blocks):
    held, edge, _ = source_blocks.shape
    holders = lax.axis_size("gy")
    slots, tiles = block_list.shape
    return pl.pallas_call(
        gather_kernel,
        out_shape=[
            jax.ShapeDtypeStruct((holders, CAP, edge, edge), BF16),
            jax.ShapeDtypeStruct((1, tiles), jnp.int32),
        ],
        in_specs=[ANY] * 4,
        out_specs=[ANY] * 2,
        scratch_shapes=[
            pltpu.VMEM((slots, tiles), jnp.int32),
            pltpu.VMEM((1, tiles), jnp.int32),
            pltpu.SMEM((held,), F32),
            pltpu.VMEM((held, edge, edge), BF16),
            pltpu.VMEM((8, tiles), jnp.int32),
            pltpu.SMEM((8, tiles), jnp.int32),
            pltpu.VMEM((holders, CAP, edge, edge), BF16),
            pltpu.SMEM((slots, tiles), jnp.int32),
            pltpu.SMEM((1, tiles), jnp.int32),
            pltpu.SMEM((holders,), jnp.int32),
            pltpu.SMEM((1, tiles), jnp.int32),
            pltpu.SemaphoreType.DMA((8,)),
            pltpu.SemaphoreType.DMA((holders,)),
        ],
        compiler_params=pltpu.CompilerParams(vmem_limit_bytes=56 * MIB),
        name="gather_blocks",
    )(block_list, block_count.reshape(1, tiles), block_scale, source_blocks)


def is_even(axis):
    return lax.rem(lax.axis_index(axis), 2) == 0


def before_and_after(first, second, axis):
    even = is_even(axis)
    first, second = first.astype(F32), second.astype(F32)
    return jnp.where(even, second, first), jnp.where(even, first, second)


def window(k, source_ref, arrived_ref, row_ref, col_ref):
    live = source_ref[0, row_ref.shape[0]]
    part = dot(row_ref[k], arrived_ref[source_ref[0, k]])
    part = jnp.where(k < live, part, 0.0).astype(BF16)
    return dot(part, col_ref[k])


def edges_kernel(
    source_ref, arrived_ref, row_ref, col_ref, edge_ref, first_ref, second_ref
):
    edge = row_ref.shape[1]
    for i in range(W):
        for s in range(2):
            k = i * W + s * (W - 1)
            edge_ref[s, i * edge : (i + 1) * edge, :] = window(
                k, source_ref, arrived_ref, row_ref, col_ref
            )
    rows = edge_ref.shape[1]
    chunk = rows // 4
    lane = lax.broadcasted_iota(jnp.int32, (chunk, 128), 1)
    left = jnp.zeros((chunk, 128), F32)
    right = jnp.zeros((chunk, 128), F32)
    for q in range(4):
        mine = (lane >= PAD * q) & (lane < PAD * (q + 1))
        part = edge_ref[0, q * chunk : (q + 1) * chunk, :]
        if q:
            part = pltpu.roll(part, PAD * q, 1)
        left = jnp.where(mine, part, left)
        part = edge_ref[1, q * chunk : (q + 1) * chunk, :]
        if q != 3:
            part = pltpu.roll(part, PAD * (q + 1), 1)
        right = jnp.where(mine, part, right)
    even = is_even("gx")
    first_ref[...] = jnp.where(even, right, left).astype(BF16)
    second_ref[...] = jnp.where(even, left, right).astype(BF16)


def edges(source, arrived, row_weights, col_weights):
    edge = row_weights.shape[1]
    side = W * edge
    shapes = [((2, side, edge), F32), ((side // 4, 128), BF16), ((side // 4, 128), BF16)]
    return pl.pallas_call(
        edges_kernel,
        out_shape=[jax.ShapeDtypeStruct(s, d) for s, d in shapes],
        in_specs=[SMEM, VMEM, VMEM, VMEM],
        out_specs=[VMEM] * len(shapes),
        cost_estimate=cost(side * 256),
        compiler_params=pltpu.CompilerParams(vmem_limit_bytes=16 * MIB),
        name="edge_windows",
    )(source, arrived, row_weights, col_weights)


def middle_kernel(
    source_ref, arrived_ref, row_ref, col_ref, edge_ref, down,
    inner_ref, low_ref, high_ref, band_ref, fall_ref, strips_ref, odd_ref,
):
    edge = row_ref.shape[1]
    rows = band_ref.shape[0]
    odd = lax.rem(lax.axis_index("gy"), 2)
    odd_ref[...] = jnp.full(odd_ref.shape, odd, jnp.int32)
    for s in range(2):
        band_ref[:, s * (W - 1) * edge : (s * (W - 1) + 1) * edge] = edge_ref[s].astype(BF16)

    for i in range(W):
        span = slice(i * edge, (i + 1) * edge)
        for j in range(1, W - 1):
            value = window(i * W + j, source_ref, arrived_ref, row_ref, col_ref)
            inner_ref[j - 1, span, :] = value
            band_ref[span, j * edge : (j + 1) * edge] = value.astype(BF16)
    for n in range(2):
        at = pl.multiple_of(jnp.where(odd == n, rows - PAD, 0), PAD)
        strips_ref[n] = band_ref[pl.ds(at, PAD), :]
    for i in range((rows - 2 * PAD) // STEP):
        value = dot(down[...], band_ref[i * STEP : (i + 1) * STEP + 2 * PAD, :])
        fall_ref[i * STEP : (i + 1) * STEP, :] = value.astype(BF16)

    def one_span(q, carry):
        span = pl.ds(pl.multiple_of(q * edge, edge), edge)
        pieces = [edge_ref[0, span, :]]
        pieces += [inner_ref[j, span, :] for j in range(W - 2)] + [edge_ref[1, span, :]]
        lane = lax.broadcasted_iota(jnp.int32, pieces[0].shape, 1)
        lows = [pltpu.roll(piece, 1, 1) for piece in pieces]
        highs = [pltpu.roll(piece, 127, 1) for piece in pieces]
        for j in range(W):
            low_ref[j, span, :] = jnp.where(lane == 0, lows[j - 1], lows[j]) if j else lows[j]
            high_ref[j, span, :] = (
                jnp.where(lane == 127, highs[j + 1], highs[j]) if j < W - 1 else highs[j]
            )
        return carry

    lax.fori_loop(0, W, one_span, 0)


def middle(source, arrived, row_weights, col_weights, edge_values):
    edge = row_weights.shape[1]
    side = W * edge
    shapes = [
        ((W - 2, side, edge), F32),
        ((W, side, edge), F32),
        ((W, side, edge), F32),
        ((side, side), BF16),
        ((side - 2 * PAD, side), BF16),
        ((2, PAD, side), BF16),
        ((8, 128), jnp.int32),
    ]
    return pl.pallas_call(
        middle_kernel,
        out_shape=[jax.ShapeDtypeStruct(s, d) for s, d in shapes],
        in_specs=[SMEM] + [VMEM] * 5,
        out_specs=[VMEM] * len(shapes),
        cost_estimate=cost(side * side),
        compiler_params=pltpu.CompilerParams(vmem_limit_bytes=24 * MIB),
        name="middle_windows",
    )(source, arrived, row_weights, col_weights, edge_values, down_taps(STEP))


def tap(offset):
    value = np.exp(-(offset * offset).astype(np.float32) / np.float32(2.0 * SIGMA * SIGMA))
    return np.where(np.abs(offset) <= RIM, value, 0.0).astype(ml_dtypes.bfloat16)


def tap_total():
    return float(np.sum(tap(np.arange(-RIM, RIM + 1)).astype(np.float64)))


def across_taps(wide, out):
    return jnp.asarray(tap(np.arange(wide)[:, None] - np.arange(out)[None, :] - 128))


def down_taps(step):
    return jnp.asarray(tap(np.arange(step + 2 * PAD)[None, :] - np.arange(step)[:, None] - PAD))


def cells(mid, low, high):
    centre, cl, cr = [load(0).astype(BF16) for load in (mid, low, high)]
    uc, ul, ur = [load(-1).astype(BF16) for load in (mid, low, high)]
    dc, dl, dr = [load(1).astype(BF16) for load in (mid, low, high)]
    one = dr - ul
    two = ur - dl
    across = cr - cl
    along = dc - uc
    grad_x = (one + two) + (across + across)
    grad_y = (one - two) + (along + along)
    steep = (grad_x * grad_x + grad_y * grad_y).astype(F32)
    square = 1.0 + steep * (1.0 / 64.0)
    slope = square * lax.rsqrt(square)
    flows = []
    for value, diagonal in (
        (ul, True), (uc, False), (ur, True), (cl, False),
        (cr, False), (dl, True), (dc, False), (dr, True),
    ):
        drop = jnp.maximum(centre - value, 0)
        flows.append((drop * BF16(DIAG) if diagonal else drop) + BF16(FLAT))
    total = (
        ((flows[0] + flows[1]) + (flows[2] + flows[3]))
        + ((flows[4] + flows[5]) + (flows[6] + flows[7]))
    )
    share = pl.reciprocal(total.astype(F32), approx=True).astype(BF16)
    return slope, [flow * share for flow in flows]


def sideways(centre, before, after):
    lane = lax.broadcasted_iota(jnp.int32, centre.shape, 1)
    low = jnp.where(lane == 0, pltpu.roll(before, 1, 1), pltpu.roll(centre, 1, 1))
    high = jnp.where(lane == 127, pltpu.roll(after, 127, 1), pltpu.roll(centre, 127, 1))
    return low, high


def dot(a, b):
    return jnp.dot(a, b, preferred_element_type=F32)


STEP = 176


def main_kernel(
    edge_ref, inner_ref, low_ref, high_ref, fall_ref, first_ref, second_ref, across, down,
    relief_hbm, slope_hbm, flow_hbm, relief, slope, flow, far, patched, sems,
):
    rows, cols = low_ref.shape[1], relief.shape[1]
    lanes = cols // 128
    steps = (rows - 2 * PAD) // STEP
    chunk = rows // 4
    inverse = 1.0 / (tap_total() ** 2)
    lane = lax.broadcasted_iota(jnp.int32, (chunk, 128), 1)
    left, right = before_and_after(first_ref[...], second_ref[...], "gx")
    for q in range(4):
        span = slice(q * chunk, (q + 1) * chunk)
        value = unpack_left(left, q)
        far[0, span, :] = value.astype(BF16)
        patched[0, span, :] = jnp.where(lane == 0, pltpu.roll(value, 1, 1), low_ref[0, span, :])
        value = unpack_right(right, q)
        far[1, span, :] = value.astype(BF16)
        patched[1, span, :] = jnp.where(
            lane == 127, pltpu.roll(value, 127, 1), high_ref[lanes - 1, span, :]
        )

    def copies(i):
        span = pl.ds(pl.multiple_of(i * STEP, 16), STEP)
        place = pl.ds(pl.multiple_of(PAD + i * STEP, 16), STEP)
        return (
            pltpu.make_async_copy(relief.at[span], relief_hbm.at[place], sems.at[i, 0]),
            pltpu.make_async_copy(slope.at[span], slope_hbm.at[place], sems.at[i, 1]),
            pltpu.make_async_copy(flow.at[:, span], flow_hbm.at[:, place], sems.at[i, 2]),
        )

    def mid(j, span):
        if j in (0, lanes - 1):
            return edge_ref[int(j > 0), span, :]
        return inner_ref[j - 1, span, :]

    def low(j, span):
        return low_ref[j, span, :] if j else patched[0, span, :]

    def high(j, span):
        return high_ref[j, span, :] if j < lanes - 1 else patched[1, span, :]

    def one_step(i, carry):
        base = pl.multiple_of(i * STEP, 16)
        tall = pl.ds(base, STEP + 2 * PAD)
        span = pl.ds(base, STEP)
        sides = [dot(down[...], far[s, tall, :]).astype(BF16) for s in range(2)]
        for j in range(lanes // 2):
            at = j * 256
            if j == 0:
                wide = jnp.concatenate([sides[0], fall_ref[span, 0:384]], axis=1)
            elif j == lanes // 2 - 1:
                wide = jnp.concatenate([fall_ref[span, at - 128 :], sides[1]], axis=1)
            else:
                wide = fall_ref[span, at - 128 : at + 384]
            value = dot(wide, across[...])
            for h in range(2):
                centre = mid(j * 2 + h, pl.ds(base + PAD, STEP))
                relief[span, at + h * 128 : at + h * 128 + 128] = (
                    centre - value[:, h * 128 : h * 128 + 128] * inverse
                )
        for q in range(STEP // 16):
            at = pl.multiple_of(base + q * 16, 16)
            for j in range(lanes):
                value, parts = cells(
                    lambda d: mid(j, pl.ds(at + PAD + d, 16)),
                    lambda d: low(j, pl.ds(at + PAD + d, 16)),
                    lambda d: high(j, pl.ds(at + PAD + d, 16)),
                )
                place = (pl.ds(at, 16), slice(j * 128, (j + 1) * 128))
                slope[place] = value
                for n, part in enumerate(parts):
                    flow[(n,) + place] = part
        for copy in copies(i):
            copy.start()
        return carry

    lax.fori_loop(0, steps, one_step, 0)
    for i in range(steps):
        for copy in copies(i):
            copy.wait()


def main(edge_values, inner, low, high, fall, left, right):
    lanes, rows, _ = low.shape
    cols = lanes * 128
    tall = rows - 2 * PAD
    return pl.pallas_call(
        main_kernel,
        out_shape=out_shapes(rows, cols),
        in_specs=[VMEM] * 9,
        out_specs=[ANY] * 3,
        scratch_shapes=[
            pltpu.VMEM((tall, cols), F32),
            pltpu.VMEM((tall, cols), F32),
            pltpu.VMEM((8, tall, cols), BF16),
            pltpu.VMEM((2, rows, 128), BF16),
            pltpu.VMEM((2, rows, 128), F32),
            pltpu.SemaphoreType.DMA((tall // STEP, 3)),
        ],
        cost_estimate=cost(tall * cols),
        compiler_params=pltpu.CompilerParams(vmem_limit_bytes=32 * MIB),
        name="main_cells",
    )(edge_values, inner, low, high, fall, left, right, across_taps(512, 256), down_taps(STEP))


def out_shapes(rows, cols):
    return [
        jax.ShapeDtypeStruct((rows, cols), F32),
        jax.ShapeDtypeStruct((rows, cols), F32),
        jax.ShapeDtypeStruct((8, rows, cols), BF16),
    ]


def cost(cells_done):
    return pl.CostEstimate(
        flops=cells_done * 4000, bytes_accessed=cells_done * 24, transcendentals=cells_done * 2
    )


def unpack_left(value, q):
    return value if q == 3 else pltpu.roll(value, 96 - PAD * q, 1)


def unpack_right(value, q):
    return value if q == 0 else pltpu.roll(value, 128 - PAD * q, 1)


def ends_kernel(
    edge_ref, inner_ref, band_ref, first_ref, second_ref, near_ref, next_ref, across, down,
    relief_in, slope_in, flow_in, relief_hbm, slope_hbm, flow_hbm,
    relief, slope, flow, wide, band, low_ref, high_ref, sems,
):
    rows, cols = band_ref.shape
    lanes = cols // 128
    near = 2 * PAD
    tall = PAD + 16
    inverse = 1.0 / (tap_total() ** 2)
    packed = first_ref.shape[0]
    others = before_and_after(near_ref[...], next_ref[...], "gy")
    for e in range(2):
        here = slice(PAD, PAD + near) if e == 0 else slice(0, near)
        there = slice(0, PAD) if e == 0 else slice(near, near + PAD)
        other = others[e]
        top = e * tall
        own_rows = slice(rows - near, rows) if e else slice(0, near)
        pack_rows = slice(packed - near, packed) if e else slice(0, near)
        band[e, here, 128 : 128 + cols] = band_ref[own_rows, :]
        band[e, there, 128 : 128 + cols] = other[:, 0:cols].astype(BF16)
        left, right = before_and_after(first_ref[pack_rows, :], second_ref[pack_rows, :], "gx")
        far_left = unpack_left(left, 3 * e)
        far_right = unpack_right(right, 3 * e)
        left, right = before_and_after(
            other[:, cols : cols + 128], other[:, cols + 128 : cols + 256], "gx"
        )
        corner_left = unpack_left(left, 0 if e else 3)
        corner_right = unpack_right(right, 0 if e else 3)
        band[e, here, 0:128] = far_left.astype(BF16)
        band[e, there, 0:128] = corner_left.astype(BF16)
        band[e, here, 128 + cols :] = far_right.astype(BF16)
        band[e, there, 128 + cols :] = corner_right.astype(BF16)
        if e == 0:
            wide[0, top : top + 8, :] = corner_left[PAD - 8 : PAD]
            wide[0, top + 8 : top + 48, :] = far_left[0:40]
            wide[lanes + 1, top : top + 8, :] = corner_right[PAD - 8 : PAD]
            wide[lanes + 1, top + 8 : top + 48, :] = far_right[0:40]
        else:
            wide[0, top : top + 40, :] = far_left[near - 40 : near]
            wide[0, top + 40 : top + 48, :] = corner_left[0:8]
            wide[lanes + 1, top : top + 40, :] = far_right[near - 40 : near]
            wide[lanes + 1, top + 40 : top + 48, :] = corner_right[0:8]
        for j in range(lanes):
            part = other[:, j * 128 : (j + 1) * 128]
            own = edge_ref.at[int(j > 0)] if j in (0, lanes - 1) else inner_ref.at[j - 1]
            if e == 0:
                wide[j + 1, top : top + 8, :] = part[PAD - 8 : PAD]
                wide[j + 1, top + 8 : top + 48, :] = own[0:40, :]
            else:
                wide[j + 1, top : top + 40, :] = own[rows - 40 : rows, :]
                wide[j + 1, top + 40 : top + 48, :] = part[0:8]

    for e in range(2):
        smooth = dot(down[...], band[e]).astype(BF16)
        for j in range(lanes // 2):
            value = dot(smooth[:, j * 256 : j * 256 + 512], across[...])
            for h in range(2):
                at = j * 256 + h * 128
                relief[e, :, at : at + 128] = (
                    wide[j * 2 + h + 1, e * tall + 8 : e * tall + 8 + PAD, :] - value[:, h * 128 : h * 128 + 128] * inverse
                )
    for j in range(lanes):
        low, high = sideways(wide[j + 1], wide[j], wide[j + 2])
        low_ref[j] = low
        high_ref[j] = high

    def one_end(e, carry):
        for at in range(0, PAD, 16):
            top = pl.multiple_of(e * tall + 8 + at, 8)
            for j in range(lanes):
                value, parts = cells(
                    lambda d: wide[j + 1, pl.ds(top + d, 16), :],
                    lambda d: low_ref[j, pl.ds(top + d, 16), :],
                    lambda d: high_ref[j, pl.ds(top + d, 16), :],
                )
                place = (slice(at, at + 16), slice(j * 128, (j + 1) * 128))
                slope[(e,) + place] = value
                for n, part in enumerate(parts):
                    flow[(e, n) + place] = part
        place = pl.ds(pl.multiple_of(e * (rows - PAD), PAD), PAD)
        pltpu.make_async_copy(relief.at[e], relief_hbm.at[place], sems.at[e, 0]).start()
        pltpu.make_async_copy(slope.at[e], slope_hbm.at[place], sems.at[e, 1]).start()
        pltpu.make_async_copy(flow.at[e], flow_hbm.at[:, place], sems.at[e, 2]).start()
        return carry

    lax.fori_loop(0, 2, one_end, 0)
    for e in range(2):
        place = pl.ds(e * (rows - PAD), PAD)
        pltpu.make_async_copy(relief.at[e], relief_hbm.at[place], sems.at[e, 0]).wait()
        pltpu.make_async_copy(slope.at[e], slope_hbm.at[place], sems.at[e, 1]).wait()
        pltpu.make_async_copy(flow.at[e], flow_hbm.at[:, place], sems.at[e, 2]).wait()


def ends(edge_values, inner, band, left, right, up, down, outs):
    rows, cols = band.shape
    lanes = cols // 128
    return pl.pallas_call(
        ends_kernel,
        out_shape=out_shapes(rows, cols),
        in_specs=[VMEM] * 9 + [ANY] * 3,
        out_specs=[ANY] * 3,
        input_output_aliases={9: 0, 10: 1, 11: 2},
        scratch_shapes=[
            pltpu.VMEM((2, PAD, cols), F32),
            pltpu.VMEM((2, PAD, cols), F32),
            pltpu.VMEM((2, 8, PAD, cols), BF16),
            pltpu.VMEM((lanes + 2, 2 * (PAD + 16), 128), F32),
            pltpu.VMEM((2, 3 * PAD, cols + 256), BF16),
            pltpu.VMEM((lanes, 2 * (PAD + 16), 128), F32),
            pltpu.VMEM((lanes, 2 * (PAD + 16), 128), F32),
            pltpu.SemaphoreType.DMA((2, 3)),
        ],
        cost_estimate=cost(2 * PAD * cols),
        compiler_params=pltpu.CompilerParams(vmem_limit_bytes=16 * MIB),
        name="end_cells",
    )(
        edge_values, inner, band, left, right, up, down,
        across_taps(512, 256), down_taps(PAD), *outs,
    )


def swap(first, second, axis):
    devices = lax.axis_size(axis)
    received = []
    for start, value in enumerate((first, second)):
        pairs = [(i, i + 1) for i in range(start, devices - 1, 2)]
        received.append(lax.ppermute(value, axis, pairs + [(j, i) for i, j in pairs]))
    return received


def local(source_blocks, block_scale, block_list, block_count, row_weights, col_weights):
    block_list = block_list.T
    outgoing, source = gather(block_list, block_count, block_scale, source_blocks)
    edge = source_blocks.shape[1]
    arrived = lax.all_to_all(outgoing, "gy", split_axis=0, concat_axis=0, tiled=True)
    arrived = arrived.reshape(-1, edge, edge)
    weights = (row_weights, col_weights)
    edge_values, *messages = edges(source, arrived, *weights)
    beside = swap(*messages, "gx")
    inner, low, high, band, fall, strips, odd = middle(source, arrived, *weights, edge_values)
    messages = []
    for n in range(2):
        corners = [jnp.where(odd[:1] == n, side[-PAD:], side[:PAD]) for side in beside]
        messages.append(jnp.concatenate([strips[n], *corners], axis=1))
    ahead = swap(*messages, "gy")
    outs = main(edge_values, inner, low, high, fall, *beside)
    return tuple(ends(edge_values, inner, band, *beside, *ahead, outs))


def solution(mesh):
    in_specs = (
        P(("gx", "gy"), None, None),
        P(("gx", "gy")),
        P(),
        P(),
        P(("gx", "gy"), None, None),
        P(("gx", "gy"), None, None),
    )
    out_specs = (P("gy", "gx"), P("gy", "gx"), P(None, "gy", "gx"))
    return jax.shard_map(local, mesh=mesh, in_specs=in_specs, out_specs=out_specs, check_vma=False)
```

```python
import jax
import jax.numpy as jnp
import ml_dtypes
import numpy as np
from jax import lax
from jax.experimental import pallas as pl
from jax.experimental.pallas import tpu as pltpu
from jax.sharding import PartitionSpec as P

W = 6
CAP = 4
RIM = 24
PAD = 32
SIGMA = 10.0
FLAT = 0.05
DIAG = 0.5**0.5
F32 = jnp.float32
BF16 = jnp.bfloat16
MIB = 1 << 20

SMEM = pl.BlockSpec(memory_space=pltpu.SMEM)
VMEM = pl.BlockSpec(memory_space=pltpu.VMEM)
ANY = pl.BlockSpec(memory_space=pl.ANY)


def gather_kernel(
    list_hbm, count_hbm, scale_hbm, blocks_hbm, out_hbm, source_hbm,
    listed, counted, scale, blocks, found, table, staged,
    named, numbered, seen, source, sems, out_sems,
):
    holders = lax.axis_size("gy")
    first = lax.axis_index("gx") * holders
    held = blocks.shape[0]
    base = (first + lax.axis_index("gy")) * held
    slots = listed.shape[0]
    copies = [
        pltpu.make_async_copy(list_hbm, listed, sems.at[0]),
        pltpu.make_async_copy(count_hbm, counted, sems.at[1]),
        pltpu.make_async_copy(scale_hbm, scale, sems.at[2]),
        pltpu.make_async_copy(blocks_hbm, blocks, sems.at[3]),
        pltpu.make_async_copy(list_hbm, named, sems.at[5]),
        pltpu.make_async_copy(count_hbm, numbered, sems.at[6]),
    ]
    for copy in copies:
        copy.start()
    copies[0].wait()
    copies[1].wait()
    shape = found.shape
    row = lax.broadcasted_iota(jnp.int32, shape, 0)
    live = jnp.broadcast_to(counted[...], shape)
    rank = jnp.zeros(shape, jnp.int32)
    chosen = jnp.zeros(shape, jnp.int32)
    for k in range(slots):
        block = jnp.broadcast_to(listed[k : k + 1, :], shape) - base
        hit = (block >= 0) & (block < held) & (k < live)
        chosen = jnp.where(hit & (rank == row), block, chosen)
        rank = rank + hit.astype(jnp.int32)
    found[...] = jnp.where(row < CAP, chosen, rank)
    handed = pltpu.make_async_copy(found, table, sems.at[4])
    handed.start()
    copies[4].wait()
    copies[5].wait()
    tile = first + lax.axis_index("gy")
    count = numbered[0, tile]
    for h in range(out_hbm.shape[0]):
        seen[h] = 0
    for k in range(slots):
        block = jnp.clip(named[k, tile] - first * held, 0, out_hbm.shape[0] * held - 1)
        owner = lax.shift_right_logical(block, jnp.int32(held.bit_length() - 1))
        rank = seen[owner]
        source[0, k] = owner * CAP + jnp.minimum(rank, CAP - 1)
        seen[owner] = rank + (k < count).astype(jnp.int32)
    source[0, slots] = count
    told = pltpu.make_async_copy(source, source_hbm, sems.at[7])
    told.start()
    handed.wait()
    copies[2].wait()
    copies[3].wait()

    def one_tile(t, carry):
        @pl.when(table[CAP, first + t] > 0)
        def fill():
            for j in range(CAP):
                block = table[j, first + t]
                value = blocks[block].astype(F32) * scale[block]
                staged[t, j] = value.astype(BF16)
            pltpu.make_async_copy(staged.at[t], out_hbm.at[t], out_sems.at[t]).start()

        return carry

    lax.fori_loop(0, holders, one_tile, 0)

    def one_wait(t, carry):
        @pl.when(table[CAP, first + t] > 0)
        def drain():
            pltpu.make_async_copy(staged.at[t], out_hbm.at[t], out_sems.at[t]).wait()

        return carry

    lax.fori_loop(0, holders, one_wait, 0)
    told.wait()


def gather(block_list, block_count, block_scale, source_blocks):
    held, edge, _ = source_blocks.shape
    holders = lax.axis_size("gy")
    slots, tiles = block_list.shape
    return pl.pallas_call(
        gather_kernel,
        out_shape=[
            jax.ShapeDtypeStruct((holders, CAP, edge, edge), BF16),
            jax.ShapeDtypeStruct((1, tiles), jnp.int32),
        ],
        in_specs=[ANY] * 4,
        out_specs=[ANY] * 2,
        scratch_shapes=[
            pltpu.VMEM((slots, tiles), jnp.int32),
            pltpu.VMEM((1, tiles), jnp.int32),
            pltpu.SMEM((held,), F32),
            pltpu.VMEM((held, edge, edge), BF16),
            pltpu.VMEM((8, tiles), jnp.int32),
            pltpu.SMEM((8, tiles), jnp.int32),
            pltpu.VMEM((holders, CAP, edge, edge), BF16),
            pltpu.SMEM((slots, tiles), jnp.int32),
            pltpu.SMEM((1, tiles), jnp.int32),
            pltpu.SMEM((holders,), jnp.int32),
            pltpu.SMEM((1, tiles), jnp.int32),
            pltpu.SemaphoreType.DMA((8,)),
            pltpu.SemaphoreType.DMA((holders,)),
        ],
        compiler_params=pltpu.CompilerParams(vmem_limit_bytes=56 * MIB),
        name="gather_blocks",
    )(block_list, block_count.reshape(1, tiles), block_scale, source_blocks)


def is_even(axis):
    return lax.rem(lax.axis_index(axis), 2) == 0


def before_and_after(first, second, axis):
    even = is_even(axis)
    first, second = first.astype(F32), second.astype(F32)
    return jnp.where(even, second, first), jnp.where(even, first, second)


def window(k, source_ref, arrived_ref, row_ref, col_ref):
    live = source_ref[0, row_ref.shape[0]]
    part = dot(row_ref[k], arrived_ref[source_ref[0, k]])
    part = jnp.where(k < live, part, 0.0).astype(BF16)
    return dot(part, col_ref[k])


def edges_kernel(
    source_ref, arrived_ref, row_ref, col_ref, edge_ref, first_ref, second_ref
):
    edge = row_ref.shape[1]
    for i in range(W):
        for s in range(2):
            k = i * W + s * (W - 1)
            edge_ref[s, i * edge : (i + 1) * edge, :] = window(
                k, source_ref, arrived_ref, row_ref, col_ref
            )
    rows = edge_ref.shape[1]
    chunk = rows // 4
    lane = lax.broadcasted_iota(jnp.int32, (chunk, 128), 1)
    left = jnp.zeros((chunk, 128), F32)
    right = jnp.zeros((chunk, 128), F32)
    for q in range(4):
        mine = (lane >= PAD * q) & (lane < PAD * (q + 1))
        part = edge_ref[0, q * chunk : (q + 1) * chunk, :]
        if q:
            part = pltpu.roll(part, PAD * q, 1)
        left = jnp.where(mine, part, left)
        part = edge_ref[1, q * chunk : (q + 1) * chunk, :]
        if q != 3:
            part = pltpu.roll(part, PAD * (q + 1), 1)
        right = jnp.where(mine, part, right)
    even = is_even("gx")
    first_ref[...] = jnp.where(even, right, left).astype(BF16)
    second_ref[...] = jnp.where(even, left, right).astype(BF16)


def edges(source, arrived, row_weights, col_weights):
    edge = row_weights.shape[1]
    side = W * edge
    shapes = [((2, side, edge), F32), ((side // 4, 128), BF16), ((side // 4, 128), BF16)]
    return pl.pallas_call(
        edges_kernel,
        out_shape=[jax.ShapeDtypeStruct(s, d) for s, d in shapes],
        in_specs=[SMEM, VMEM, VMEM, VMEM],
        out_specs=[VMEM] * len(shapes),
        cost_estimate=cost(side * 256),
        compiler_params=pltpu.CompilerParams(vmem_limit_bytes=16 * MIB),
        name="edge_windows",
    )(source, arrived, row_weights, col_weights)


def middle_kernel(
    source_ref, arrived_ref, row_ref, col_ref, edge_ref, down,
    inner_ref, low_ref, high_ref, band_ref, fall_ref, strips_ref, odd_ref,
):
    edge = row_ref.shape[1]
    rows = band_ref.shape[0]
    odd = lax.rem(lax.axis_index("gy"), 2)
    odd_ref[...] = jnp.full(odd_ref.shape, odd, jnp.int32)
    for s in range(2):
        band_ref[:, s * (W - 1) * edge : (s * (W - 1) + 1) * edge] = edge_ref[s].astype(BF16)

    for i in range(W):
        span = slice(i * edge, (i + 1) * edge)
        for j in range(1, W - 1):
            value = window(i * W + j, source_ref, arrived_ref, row_ref, col_ref)
            inner_ref[j - 1, span, :] = value
            band_ref[span, j * edge : (j + 1) * edge] = value.astype(BF16)
    for n in range(2):
        at = pl.multiple_of(jnp.where(odd == n, rows - PAD, 0), PAD)
        strips_ref[n] = band_ref[pl.ds(at, PAD), :]
    for i in range((rows - 2 * PAD) // STEP):
        value = dot(down[...], band_ref[i * STEP : (i + 1) * STEP + 2 * PAD, :])
        fall_ref[i * STEP : (i + 1) * STEP, :] = value.astype(BF16)

    def one_span(q, carry):
        span = pl.ds(pl.multiple_of(q * edge, edge), edge)
        pieces = [edge_ref[0, span, :]]
        pieces += [inner_ref[j, span, :] for j in range(W - 2)] + [edge_ref[1, span, :]]
        lane = lax.broadcasted_iota(jnp.int32, pieces[0].shape, 1)
        lows = [pltpu.roll(piece, 1, 1) for piece in pieces]
        highs = [pltpu.roll(piece, 127, 1) for piece in pieces]
        for j in range(W):
            low_ref[j, span, :] = jnp.where(lane == 0, lows[j - 1], lows[j]) if j else lows[j]
            high_ref[j, span, :] = (
                jnp.where(lane == 127, highs[j + 1], highs[j]) if j < W - 1 else highs[j]
            )
        return carry

    lax.fori_loop(0, W, one_span, 0)


def middle(source, arrived, row_weights, col_weights, edge_values):
    edge = row_weights.shape[1]
    side = W * edge
    shapes = [
        ((W - 2, side, edge), F32),
        ((W, side, edge), F32),
        ((W, side, edge), F32),
        ((side, side), BF16),
        ((side - 2 * PAD, side), BF16),
        ((2, PAD, side), BF16),
        ((8, 128), jnp.int32),
    ]
    return pl.pallas_call(
        middle_kernel,
        out_shape=[jax.ShapeDtypeStruct(s, d) for s, d in shapes],
        in_specs=[SMEM] + [VMEM] * 5,
        out_specs=[VMEM] * len(shapes),
        cost_estimate=cost(side * side),
        compiler_params=pltpu.CompilerParams(vmem_limit_bytes=24 * MIB),
        name="middle_windows",
    )(source, arrived, row_weights, col_weights, edge_values, down_taps(STEP))


def tap(offset):
    value = np.exp(-(offset * offset).astype(np.float32) / np.float32(2.0 * SIGMA * SIGMA))
    return np.where(np.abs(offset) <= RIM, value, 0.0).astype(ml_dtypes.bfloat16)


def tap_total():
    return float(np.sum(tap(np.arange(-RIM, RIM + 1)).astype(np.float64)))


def across_taps(wide, out):
    return jnp.asarray(tap(np.arange(wide)[:, None] - np.arange(out)[None, :] - 128))


def down_taps(step):
    return jnp.asarray(tap(np.arange(step + 2 * PAD)[None, :] - np.arange(step)[:, None] - PAD))


def cells(mid, low, high):
    centre, cl, cr = [load(0).astype(BF16) for load in (mid, low, high)]
    uc, ul, ur = [load(-1).astype(BF16) for load in (mid, low, high)]
    dc, dl, dr = [load(1).astype(BF16) for load in (mid, low, high)]
    one = dr - ul
    two = ur - dl
    across = cr - cl
    along = dc - uc
    grad_x = (one + two) + (across + across)
    grad_y = (one - two) + (along + along)
    steep = grad_x * grad_x + grad_y * grad_y
    square = BF16(1.0) + steep * BF16(1.0 / 64.0)
    slope = (square * lax.rsqrt(square)).astype(F32)
    flows = []
    for value, diagonal in (
        (ul, True), (uc, False), (ur, True), (cl, False),
        (cr, False), (dl, True), (dc, False), (dr, True),
    ):
        drop = jnp.maximum(centre - value, 0)
        flows.append((drop * BF16(DIAG) if diagonal else drop) + BF16(FLAT))
    total = (
        ((flows[0] + flows[1]) + (flows[2] + flows[3]))
        + ((flows[4] + flows[5]) + (flows[6] + flows[7]))
    )
    share = pl.reciprocal(total.astype(F32), approx=True).astype(BF16)
    return slope, [flow * share for flow in flows]


def sideways(centre, before, after):
    lane = lax.broadcasted_iota(jnp.int32, centre.shape, 1)
    low = jnp.where(lane == 0, pltpu.roll(before, 1, 1), pltpu.roll(centre, 1, 1))
    high = jnp.where(lane == 127, pltpu.roll(after, 127, 1), pltpu.roll(centre, 127, 1))
    return low, high


def dot(a, b):
    return jnp.dot(a, b, preferred_element_type=F32)


STEP = 176


def main_kernel(
    edge_ref, inner_ref, low_ref, high_ref, fall_ref, first_ref, second_ref, across, down,
    relief_hbm, slope_hbm, flow_hbm, relief, slope, flow, far, patched, sems,
):
    rows, cols = low_ref.shape[1], relief.shape[1]
    lanes = cols // 128
    steps = (rows - 2 * PAD) // STEP
    chunk = rows // 4
    inverse = 1.0 / (tap_total() ** 2)
    lane = lax.broadcasted_iota(jnp.int32, (chunk, 128), 1)
    left, right = before_and_after(first_ref[...], second_ref[...], "gx")
    for q in range(4):
        span = slice(q * chunk, (q + 1) * chunk)
        value = unpack_left(left, q)
        far[0, span, :] = value.astype(BF16)
        patched[0, span, :] = jnp.where(lane == 0, pltpu.roll(value, 1, 1), low_ref[0, span, :])
        value = unpack_right(right, q)
        far[1, span, :] = value.astype(BF16)
        patched[1, span, :] = jnp.where(
            lane == 127, pltpu.roll(value, 127, 1), high_ref[lanes - 1, span, :]
        )

    halves = ((0, 96), (96, STEP - 96))

    def copies(i, half):
        start, size = halves[half]
        span = pl.ds(pl.multiple_of(i * STEP + start, 16), size)
        place = pl.ds(pl.multiple_of(PAD + i * STEP + start, 16), size)
        sem = sems.at[i, half]
        return (
            pltpu.make_async_copy(relief.at[span], relief_hbm.at[place], sem.at[0]),
            pltpu.make_async_copy(slope.at[span], slope_hbm.at[place], sem.at[1]),
            pltpu.make_async_copy(flow.at[:, span], flow_hbm.at[:, place], sem.at[2]),
        )

    def mid(j, span):
        if j in (0, lanes - 1):
            return edge_ref[int(j > 0), span, :]
        return inner_ref[j - 1, span, :]

    def low(j, span):
        return low_ref[j, span, :] if j else patched[0, span, :]

    def high(j, span):
        return high_ref[j, span, :] if j < lanes - 1 else patched[1, span, :]

    def one_step(i, carry):
        base = pl.multiple_of(i * STEP, 16)
        tall = pl.ds(base, STEP + 2 * PAD)
        span = pl.ds(base, STEP)
        sides = [dot(down[...], far[s, tall, :]).astype(BF16) for s in range(2)]
        for j in range(lanes // 2):
            at = j * 256
            if j == 0:
                wide = jnp.concatenate([sides[0], fall_ref[span, 0:384]], axis=1)
            elif j == lanes // 2 - 1:
                wide = jnp.concatenate([fall_ref[span, at - 128 :], sides[1]], axis=1)
            else:
                wide = fall_ref[span, at - 128 : at + 384]
            value = dot(wide, across[...])
            for h in range(2):
                centre = mid(j * 2 + h, pl.ds(base + PAD, STEP))
                relief[span, at + h * 128 : at + h * 128 + 128] = (
                    centre - value[:, h * 128 : h * 128 + 128] * inverse
                )
        for q in range(STEP // 16):
            at = pl.multiple_of(base + q * 16, 16)
            for j in range(lanes):
                value, parts = cells(
                    lambda d: mid(j, pl.ds(at + PAD + d, 16)),
                    lambda d: low(j, pl.ds(at + PAD + d, 16)),
                    lambda d: high(j, pl.ds(at + PAD + d, 16)),
                )
                place = (pl.ds(at, 16), slice(j * 128, (j + 1) * 128))
                slope[place] = value
                for n, part in enumerate(parts):
                    flow[(n,) + place] = part
            for half, (start, size) in enumerate(halves):
                if q * 16 + 16 == start + size:
                    for copy in copies(i, half):
                        copy.start()
        return carry

    lax.fori_loop(0, steps, one_step, 0)
    for i in range(steps):
        for half in range(2):
            for copy in copies(i, half):
                copy.wait()


def main(edge_values, inner, low, high, fall, left, right):
    lanes, rows, _ = low.shape
    cols = lanes * 128
    tall = rows - 2 * PAD
    return pl.pallas_call(
        main_kernel,
        out_shape=out_shapes(rows, cols),
        in_specs=[VMEM] * 9,
        out_specs=[ANY] * 3,
        scratch_shapes=[
            pltpu.VMEM((tall, cols), F32),
            pltpu.VMEM((tall, cols), F32),
            pltpu.VMEM((8, tall, cols), BF16),
            pltpu.VMEM((2, rows, 128), BF16),
            pltpu.VMEM((2, rows, 128), F32),
            pltpu.SemaphoreType.DMA((tall // STEP, 2, 3)),
        ],
        cost_estimate=cost(tall * cols),
        compiler_params=pltpu.CompilerParams(vmem_limit_bytes=32 * MIB),
        name="main_cells",
    )(edge_values, inner, low, high, fall, left, right, across_taps(512, 256), down_taps(STEP))


def out_shapes(rows, cols):
    return [
        jax.ShapeDtypeStruct((rows, cols), F32),
        jax.ShapeDtypeStruct((rows, cols), F32),
        jax.ShapeDtypeStruct((8, rows, cols), BF16),
    ]


def cost(cells_done):
    return pl.CostEstimate(
        flops=cells_done * 4000, bytes_accessed=cells_done * 24, transcendentals=cells_done * 2
    )


def unpack_left(value, q):
    return value if q == 3 else pltpu.roll(value, 96 - PAD * q, 1)


def unpack_right(value, q):
    return value if q == 0 else pltpu.roll(value, 128 - PAD * q, 1)


def ends_kernel(
    edge_ref, inner_ref, band_ref, first_ref, second_ref, near_ref, next_ref, across, down,
    relief_in, slope_in, flow_in, relief_hbm, slope_hbm, flow_hbm,
    relief, slope, flow, wide, band, low_ref, high_ref, sems,
):
    rows, cols = band_ref.shape
    lanes = cols // 128
    near = 2 * PAD
    tall = PAD + 16
    inverse = 1.0 / (tap_total() ** 2)
    packed = first_ref.shape[0]
    others = before_and_after(near_ref[...], next_ref[...], "gy")
    for e in range(2):
        here = slice(PAD, PAD + near) if e == 0 else slice(0, near)
        there = slice(0, PAD) if e == 0 else slice(near, near + PAD)
        other = others[e]
        top = e * tall
        own_rows = slice(rows - near, rows) if e else slice(0, near)
        pack_rows = slice(packed - near, packed) if e else slice(0, near)
        band[e, here, 128 : 128 + cols] = band_ref[own_rows, :]
        band[e, there, 128 : 128 + cols] = other[:, 0:cols].astype(BF16)
        left, right = before_and_after(first_ref[pack_rows, :], second_ref[pack_rows, :], "gx")
        far_left = unpack_left(left, 3 * e)
        far_right = unpack_right(right, 3 * e)
        left, right = before_and_after(
            other[:, cols : cols + 128], other[:, cols + 128 : cols + 256], "gx"
        )
        corner_left = unpack_left(left, 0 if e else 3)
        corner_right = unpack_right(right, 0 if e else 3)
        band[e, here, 0:128] = far_left.astype(BF16)
        band[e, there, 0:128] = corner_left.astype(BF16)
        band[e, here, 128 + cols :] = far_right.astype(BF16)
        band[e, there, 128 + cols :] = corner_right.astype(BF16)
        if e == 0:
            wide[0, top : top + 8, :] = corner_left[PAD - 8 : PAD]
            wide[0, top + 8 : top + 48, :] = far_left[0:40]
            wide[lanes + 1, top : top + 8, :] = corner_right[PAD - 8 : PAD]
            wide[lanes + 1, top + 8 : top + 48, :] = far_right[0:40]
        else:
            wide[0, top : top + 40, :] = far_left[near - 40 : near]
            wide[0, top + 40 : top + 48, :] = corner_left[0:8]
            wide[lanes + 1, top : top + 40, :] = far_right[near - 40 : near]
            wide[lanes + 1, top + 40 : top + 48, :] = corner_right[0:8]
        for j in range(lanes):
            part = other[:, j * 128 : (j + 1) * 128]
            own = edge_ref.at[int(j > 0)] if j in (0, lanes - 1) else inner_ref.at[j - 1]
            if e == 0:
                wide[j + 1, top : top + 8, :] = part[PAD - 8 : PAD]
                wide[j + 1, top + 8 : top + 48, :] = own[0:40, :]
            else:
                wide[j + 1, top : top + 40, :] = own[rows - 40 : rows, :]
                wide[j + 1, top + 40 : top + 48, :] = part[0:8]

    for e in range(2):
        smooth = dot(down[...], band[e]).astype(BF16)
        for j in range(lanes // 2):
            value = dot(smooth[:, j * 256 : j * 256 + 512], across[...])
            for h in range(2):
                at = j * 256 + h * 128
                relief[e, :, at : at + 128] = (
                    wide[j * 2 + h + 1, e * tall + 8 : e * tall + 8 + PAD, :] - value[:, h * 128 : h * 128 + 128] * inverse
                )
    for j in range(lanes):
        low, high = sideways(wide[j + 1], wide[j], wide[j + 2])
        low_ref[j] = low
        high_ref[j] = high

    def one_end(e, carry):
        for at in range(0, PAD, 16):
            top = pl.multiple_of(e * tall + 8 + at, 8)
            for j in range(lanes):
                value, parts = cells(
                    lambda d: wide[j + 1, pl.ds(top + d, 16), :],
                    lambda d: low_ref[j, pl.ds(top + d, 16), :],
                    lambda d: high_ref[j, pl.ds(top + d, 16), :],
                )
                place = (slice(at, at + 16), slice(j * 128, (j + 1) * 128))
                slope[(e,) + place] = value
                for n, part in enumerate(parts):
                    flow[(e, n) + place] = part
        place = pl.ds(pl.multiple_of(e * (rows - PAD), PAD), PAD)
        pltpu.make_async_copy(relief.at[e], relief_hbm.at[place], sems.at[e, 0]).start()
        pltpu.make_async_copy(slope.at[e], slope_hbm.at[place], sems.at[e, 1]).start()
        pltpu.make_async_copy(flow.at[e], flow_hbm.at[:, place], sems.at[e, 2]).start()
        return carry

    lax.fori_loop(0, 2, one_end, 0)
    for e in range(2):
        place = pl.ds(e * (rows - PAD), PAD)
        pltpu.make_async_copy(relief.at[e], relief_hbm.at[place], sems.at[e, 0]).wait()
        pltpu.make_async_copy(slope.at[e], slope_hbm.at[place], sems.at[e, 1]).wait()
        pltpu.make_async_copy(flow.at[e], flow_hbm.at[:, place], sems.at[e, 2]).wait()


def ends(edge_values, inner, band, left, right, up, down, outs):
    rows, cols = band.shape
    lanes = cols // 128
    return pl.pallas_call(
        ends_kernel,
        out_shape=out_shapes(rows, cols),
        in_specs=[VMEM] * 9 + [ANY] * 3,
        out_specs=[ANY] * 3,
        input_output_aliases={9: 0, 10: 1, 11: 2},
        scratch_shapes=[
            pltpu.VMEM((2, PAD, cols), F32),
            pltpu.VMEM((2, PAD, cols), F32),
            pltpu.VMEM((2, 8, PAD, cols), BF16),
            pltpu.VMEM((lanes + 2, 2 * (PAD + 16), 128), F32),
            pltpu.VMEM((2, 3 * PAD, cols + 256), BF16),
            pltpu.VMEM((lanes, 2 * (PAD + 16), 128), F32),
            pltpu.VMEM((lanes, 2 * (PAD + 16), 128), F32),
            pltpu.SemaphoreType.DMA((2, 3)),
        ],
        cost_estimate=cost(2 * PAD * cols),
        compiler_params=pltpu.CompilerParams(vmem_limit_bytes=16 * MIB),
        name="end_cells",
    )(
        edge_values, inner, band, left, right, up, down,
        across_taps(512, 256), down_taps(PAD), *outs,
    )


def swap(first, second, axis):
    devices = lax.axis_size(axis)
    received = []
    for start, value in enumerate((first, second)):
        pairs = [(i, i + 1) for i in range(start, devices - 1, 2)]
        received.append(lax.ppermute(value, axis, pairs + [(j, i) for i, j in pairs]))
    return received


def local(source_blocks, block_scale, block_list, block_count, row_weights, col_weights):
    block_list = block_list.T
    outgoing, source = gather(block_list, block_count, block_scale, source_blocks)
    edge = source_blocks.shape[1]
    arrived = lax.all_to_all(outgoing, "gy", split_axis=0, concat_axis=0, tiled=True)
    arrived = arrived.reshape(-1, edge, edge)
    weights = (row_weights, col_weights)
    edge_values, *messages = edges(source, arrived, *weights)
    beside = swap(*messages, "gx")
    inner, low, high, band, fall, strips, odd = middle(source, arrived, *weights, edge_values)
    messages = []
    for n in range(2):
        corners = [jnp.where(odd[:1] == n, side[-PAD:], side[:PAD]) for side in beside]
        messages.append(jnp.concatenate([strips[n], *corners], axis=1))
    ahead = swap(*messages, "gy")
    outs = main(edge_values, inner, low, high, fall, *beside)
    return tuple(ends(edge_values, inner, band, *beside, *ahead, outs))


def solution(mesh):
    in_specs = (
        P(("gx", "gy"), None, None),
        P(("gx", "gy")),
        P(),
        P(),
        P(("gx", "gy"), None, None),
        P(("gx", "gy"), None, None),
    )
    out_specs = (P("gy", "gx"), P("gy", "gx"), P(None, "gy", "gx"))
    return jax.shard_map(local, mesh=mesh, in_specs=in_specs, out_specs=out_specs, check_vma=False)
```

```python
import jax
import jax.numpy as jnp
import ml_dtypes
import numpy as np
from jax import lax
from jax.experimental import pallas as pl
from jax.experimental.pallas import tpu as pltpu
from jax.sharding import PartitionSpec as P

W = 6
CAP = 4
RIM = 24
PAD = 32
SIGMA = 10.0
FLAT = 0.05
DIAG = 0.5**0.5
F32 = jnp.float32
BF16 = jnp.bfloat16
MIB = 1 << 20
ZERO_AT = W * W

SMEM = pl.BlockSpec(memory_space=pltpu.SMEM)
VMEM = pl.BlockSpec(memory_space=pltpu.VMEM)
ANY = pl.BlockSpec(memory_space=pl.ANY)


def gather_kernel(
    list_hbm, count_hbm, scale_hbm, blocks_hbm, out_hbm, source_hbm,
    listed, counted, scale, blocks, found, table, staged,
    named, numbered, seen, source, sems, out_sems,
):
    holders = lax.axis_size("gy")
    first = lax.axis_index("gx") * holders
    held = blocks.shape[0]
    base = (first + lax.axis_index("gy")) * held
    slots = listed.shape[0]
    copies = [
        pltpu.make_async_copy(list_hbm, listed, sems.at[0]),
        pltpu.make_async_copy(count_hbm, counted, sems.at[1]),
        pltpu.make_async_copy(scale_hbm, scale, sems.at[2]),
        pltpu.make_async_copy(blocks_hbm, blocks, sems.at[3]),
        pltpu.make_async_copy(list_hbm, named, sems.at[5]),
        pltpu.make_async_copy(count_hbm, numbered, sems.at[6]),
    ]
    for copy in copies:
        copy.start()
    copies[0].wait()
    copies[1].wait()
    shape = found.shape
    row = lax.broadcasted_iota(jnp.int32, shape, 0)
    live = jnp.broadcast_to(counted[...], shape)
    rank = jnp.zeros(shape, jnp.int32)
    chosen = jnp.zeros(shape, jnp.int32)
    for k in range(slots):
        block = jnp.broadcast_to(listed[k : k + 1, :], shape) - base
        hit = (block >= 0) & (block < held) & (k < live)
        chosen = jnp.where(hit & (rank == row), block, chosen)
        rank = rank + hit.astype(jnp.int32)
    found[...] = jnp.where(row < CAP, chosen, rank)
    handed = pltpu.make_async_copy(found, table, sems.at[4])
    handed.start()
    copies[4].wait()
    copies[5].wait()
    tile = first + lax.axis_index("gy")
    count = numbered[0, tile]
    for h in range(out_hbm.shape[0]):
        seen[h] = 0
    for k in range(slots):
        block = jnp.clip(named[k, tile] - first * held, 0, out_hbm.shape[0] * held - 1)
        owner = lax.shift_right_logical(block, jnp.int32(held.bit_length() - 1))
        rank = seen[owner]
        source[0, k] = owner * CAP + jnp.minimum(rank, CAP - 1)
        seen[owner] = rank + (k < count).astype(jnp.int32)
    source[0, slots] = count
    told = pltpu.make_async_copy(source, source_hbm, sems.at[7])
    told.start()
    handed.wait()
    copies[2].wait()
    copies[3].wait()

    def one_tile(t, carry):
        @pl.when(table[CAP, first + t] > 0)
        def fill():
            for j in range(CAP):
                block = table[j, first + t]
                value = blocks[block].astype(F32) * scale[block]
                staged[t, j] = value.astype(BF16)
            pltpu.make_async_copy(staged.at[t], out_hbm.at[t], out_sems.at[t]).start()

        return carry

    lax.fori_loop(0, holders, one_tile, 0)

    def one_wait(t, carry):
        @pl.when(table[CAP, first + t] > 0)
        def drain():
            pltpu.make_async_copy(staged.at[t], out_hbm.at[t], out_sems.at[t]).wait()

        return carry

    lax.fori_loop(0, holders, one_wait, 0)
    told.wait()


def gather(block_list, block_count, block_scale, source_blocks):
    held, edge, _ = source_blocks.shape
    holders = lax.axis_size("gy")
    slots, tiles = block_list.shape
    return pl.pallas_call(
        gather_kernel,
        out_shape=[
            jax.ShapeDtypeStruct((holders, CAP, edge, edge), BF16),
            jax.ShapeDtypeStruct((1, tiles), jnp.int32),
        ],
        in_specs=[ANY] * 4,
        out_specs=[ANY] * 2,
        scratch_shapes=[
            pltpu.VMEM((slots, tiles), jnp.int32),
            pltpu.VMEM((1, tiles), jnp.int32),
            pltpu.SMEM((held,), F32),
            pltpu.VMEM((held, edge, edge), BF16),
            pltpu.VMEM((8, tiles), jnp.int32),
            pltpu.SMEM((8, tiles), jnp.int32),
            pltpu.VMEM((holders, CAP, edge, edge), BF16),
            pltpu.SMEM((slots, tiles), jnp.int32),
            pltpu.SMEM((1, tiles), jnp.int32),
            pltpu.SMEM((holders,), jnp.int32),
            pltpu.SMEM((1, tiles), jnp.int32),
            pltpu.SemaphoreType.DMA((8,)),
            pltpu.SemaphoreType.DMA((holders,)),
        ],
        compiler_params=pltpu.CompilerParams(vmem_limit_bytes=56 * MIB),
        name="gather_blocks",
    )(block_list, block_count.reshape(1, tiles), block_scale, source_blocks)


def is_even(axis):
    return lax.rem(lax.axis_index(axis), 2) == 0


def before_and_after(first, second, axis):
    even = is_even(axis)
    first, second = first.astype(F32), second.astype(F32)
    return jnp.where(even, second, first), jnp.where(even, first, second)


def window(k, source_ref, arrived_ref, row_ref, col_ref):
    live = source_ref[0, row_ref.shape[0]]
    part = dot(row_ref[k], arrived_ref[source_ref[0, k]])
    part = jnp.where(k < live, part, 0.0).astype(BF16)
    return dot(part, col_ref[k])


def edges_kernel(
    source_ref, arrived_ref, row_ref, col_ref, edge_ref, first_ref, second_ref
):
    edge = row_ref.shape[1]
    for i in range(W):
        for s in range(2):
            k = i * W + s * (W - 1)
            edge_ref[s, i * edge : (i + 1) * edge, :] = window(
                k, source_ref, arrived_ref, row_ref, col_ref
            )
    rows = edge_ref.shape[1]
    chunk = rows // 4
    lane = lax.broadcasted_iota(jnp.int32, (chunk, 128), 1)
    left = jnp.zeros((chunk, 128), F32)
    right = jnp.zeros((chunk, 128), F32)
    for q in range(4):
        mine = (lane >= PAD * q) & (lane < PAD * (q + 1))
        part = edge_ref[0, q * chunk : (q + 1) * chunk, :]
        if q:
            part = pltpu.roll(part, PAD * q, 1)
        left = jnp.where(mine, part, left)
        part = edge_ref[1, q * chunk : (q + 1) * chunk, :]
        if q != 3:
            part = pltpu.roll(part, PAD * (q + 1), 1)
        right = jnp.where(mine, part, right)
    even = is_even("gx")
    first_ref[...] = jnp.where(even, right, left).astype(BF16)
    second_ref[...] = jnp.where(even, left, right).astype(BF16)


def edges(source, arrived, row_weights, col_weights):
    edge = row_weights.shape[1]
    side = W * edge
    shapes = [((2, side, edge), F32), ((side // 4, 128), BF16), ((side // 4, 128), BF16)]
    return pl.pallas_call(
        edges_kernel,
        out_shape=[jax.ShapeDtypeStruct(s, d) for s, d in shapes],
        in_specs=[SMEM, VMEM, VMEM, VMEM],
        out_specs=[VMEM] * len(shapes),
        cost_estimate=cost(side * 256),
        compiler_params=pltpu.CompilerParams(vmem_limit_bytes=16 * MIB),
        name="edge_windows",
    )(source, arrived, row_weights, col_weights)


def middle_kernel(
    source_ref, arrived_ref, row_ref, col_ref, edge_ref, down,
    inner_ref, low_ref, high_ref, band_ref, fall_ref, strips_ref, odd_ref,
):
    edge = row_ref.shape[1]
    rows = band_ref.shape[0]
    odd = lax.rem(lax.axis_index("gy"), 2)
    odd_ref[...] = jnp.full(odd_ref.shape, odd, jnp.int32)
    for s in range(2):
        band_ref[:, s * (W - 1) * edge : (s * (W - 1) + 1) * edge] = edge_ref[s].astype(BF16)


    def windows(i):
        span = slice(i * edge, (i + 1) * edge)
        for j in range(1, W - 1):
            value = window(i * W + j, source_ref, arrived_ref, row_ref, col_ref)
            inner_ref[j - 1, span, :] = value
            band_ref[span, j * edge : (j + 1) * edge] = value.astype(BF16)

    def shifts(i):
        span = slice(i * edge, (i + 1) * edge)
        pieces = [edge_ref[0, span, :]]
        pieces += [inner_ref[j, span, :] for j in range(W - 2)] + [edge_ref[1, span, :]]
        lane = lax.broadcasted_iota(jnp.int32, pieces[0].shape, 1)
        lows = [pltpu.roll(piece, 1, 1) for piece in pieces]
        highs = [pltpu.roll(piece, 127, 1) for piece in pieces]
        for j in range(W):
            low_ref[j, span, :] = jnp.where(lane == 0, lows[j - 1], lows[j]) if j else lows[j]
            high_ref[j, span, :] = (
                jnp.where(lane == 127, highs[j + 1], highs[j]) if j < W - 1 else highs[j]
            )

    fallen = 0
    for t in range(W + 1):
        while fallen < rows - 2 * PAD and fallen + STEP + 2 * PAD <= t * edge:
            value = dot(down[...], band_ref[fallen : fallen + STEP + 2 * PAD, :])
            fall_ref[fallen : fallen + STEP, :] = value.astype(BF16)
            fallen += STEP
        if t:
            shifts(t - 1)
        if t < W:
            windows(t)
    for n in range(2):
        at = pl.multiple_of(jnp.where(odd == n, rows - PAD, 0), PAD)
        strips_ref[n] = band_ref[pl.ds(at, PAD), :]


def middle(source, arrived, row_weights, col_weights, edge_values):
    edge = row_weights.shape[1]
    side = W * edge
    shapes = [
        ((W - 2, side, edge), F32),
        ((W, side, edge), F32),
        ((W, side, edge), F32),
        ((side, side), BF16),
        ((side - 2 * PAD, side), BF16),
        ((2, PAD, side), BF16),
        ((8, 128), jnp.int32),
    ]
    return pl.pallas_call(
        middle_kernel,
        out_shape=[jax.ShapeDtypeStruct(s, d) for s, d in shapes],
        in_specs=[SMEM] + [VMEM] * 5,
        out_specs=[VMEM] * len(shapes),
        cost_estimate=cost(side * side),
        compiler_params=pltpu.CompilerParams(vmem_limit_bytes=24 * MIB),
        name="middle_windows",
    )(source, arrived, row_weights, col_weights, edge_values, down_taps(STEP))


def tap(offset):
    value = np.exp(-(offset * offset).astype(np.float32) / np.float32(2.0 * SIGMA * SIGMA))
    return np.where(np.abs(offset) <= RIM, value, 0.0).astype(ml_dtypes.bfloat16)


def tap_total():
    return float(np.sum(tap(np.arange(-RIM, RIM + 1)).astype(np.float64)))


def across_taps(wide, out):
    return jnp.asarray(tap(np.arange(wide)[:, None] - np.arange(out)[None, :] - 128))


def down_taps(step):
    return jnp.asarray(tap(np.arange(step + 2 * PAD)[None, :] - np.arange(step)[:, None] - PAD))


def cells(mid, low, high):
    centre, cl, cr = [load(0).astype(BF16) for load in (mid, low, high)]
    uc, ul, ur = [load(-1).astype(BF16) for load in (mid, low, high)]
    dc, dl, dr = [load(1).astype(BF16) for load in (mid, low, high)]
    one = dr - ul
    two = ur - dl
    across = cr - cl
    along = dc - uc
    grad_x = (one + two) + (across + across)
    grad_y = (one - two) + (along + along)
    steep = grad_x * grad_x + grad_y * grad_y
    square = BF16(1.0) + steep * BF16(1.0 / 64.0)
    slope = (square * lax.rsqrt(square)).astype(F32)
    flows = []
    for value, diagonal in (
        (ul, True), (uc, False), (ur, True), (cl, False),
        (cr, False), (dl, True), (dc, False), (dr, True),
    ):
        drop = jnp.maximum(centre - value, 0)
        flows.append((drop * BF16(DIAG) if diagonal else drop) + BF16(FLAT))
    total = (
        ((flows[0] + flows[1]) + (flows[2] + flows[3]))
        + ((flows[4] + flows[5]) + (flows[6] + flows[7]))
    )
    share = pl.reciprocal(total.astype(F32), approx=True).astype(BF16)
    return slope, [flow * share for flow in flows]


def sideways(centre, before, after):
    lane = lax.broadcasted_iota(jnp.int32, centre.shape, 1)
    low = jnp.where(lane == 0, pltpu.roll(before, 1, 1), pltpu.roll(centre, 1, 1))
    high = jnp.where(lane == 127, pltpu.roll(after, 127, 1), pltpu.roll(centre, 127, 1))
    return low, high


def dot(a, b):
    return jnp.dot(a, b, preferred_element_type=F32)


STEP = 176


def main_kernel(
    edge_ref, inner_ref, low_ref, high_ref, fall_ref, first_ref, second_ref, across, down,
    zero_ref, relief_hbm, slope_hbm, flow_hbm, relief, slope, flow, far, patched, sems, relief_sems,
):
    rows, cols = low_ref.shape[1], relief.shape[1]
    lanes = cols // 128
    steps = (rows - 2 * PAD) // STEP
    chunk = rows // 4
    inverse = 1.0 / (tap_total() ** 2)
    lane = lax.broadcasted_iota(jnp.int32, (chunk, 128), 1)
    left, right = before_and_after(first_ref[...], second_ref[...], "gx")
    for q in range(4):
        span = slice(q * chunk, (q + 1) * chunk)
        value = unpack_left(left, q)
        far[span, 0:128] = value.astype(BF16)
        patched[0, span, :] = jnp.where(lane == 0, pltpu.roll(value, 1, 1), low_ref[0, span, :])
        value = unpack_right(right, q)
        far[span, 128:256] = value.astype(BF16)
        patched[1, span, :] = jnp.where(
            lane == 127, pltpu.roll(value, 127, 1), high_ref[lanes - 1, span, :]
        )

    halves = ((0, 96), (96, STEP - 96))

    def copies(i, half):
        start, size = halves[half]
        span = slice(i * STEP + start, i * STEP + start + size)
        place = pl.ds(PAD + i * STEP + start, size)
        sem = sems.at[i, half]
        return (
            pltpu.make_async_copy(slope.at[span], slope_hbm.at[place], sem.at[0]),
            pltpu.make_async_copy(flow.at[:, span], flow_hbm.at[:, place], sem.at[1]),
        )

    def relief_copy(j):
        column = pl.ds(j * 256, 256)
        return pltpu.make_async_copy(
            relief.at[:, column], relief_hbm.at[pl.ds(PAD, rows - 2 * PAD), column], relief_sems.at[j]
        )

    def mid(j, span):
        if j in (0, lanes - 1):
            return edge_ref[int(j > 0), span, :]
        return inner_ref[j - 1, span, :]

    def low(j, span):
        return low_ref[j, span, :] if j else patched[0, span, :]

    def high(j, span):
        return high_ref[j, span, :] if j < lanes - 1 else patched[1, span, :]

    def smooth(j):
        at = j * 256
        if j == 0:
            wide = jnp.concatenate([sides[:, 0:128], fall_ref[:, 0:384]], axis=1)
        elif j == lanes // 2 - 1:
            wide = jnp.concatenate([fall_ref[:, at - 128 :], sides[:, 128:256]], axis=1)
        else:
            wide = fall_ref[:, at - 128 : at + 384]
        value = dot(wide, across[...])
        for h in range(2):
            centre = mid(j * 2 + h, slice(PAD, rows - PAD))
            relief[:, at + h * 128 : at + h * 128 + 128] = (
                centre - value[:, h * 128 : h * 128 + 128] * inverse
            )
        relief_copy(j).start()

    zero = jnp.minimum(zero_ref[0, ZERO_AT], 0)
    sides = jnp.concatenate(
        [dot(down[...], far[i * STEP : (i + 1) * STEP + 2 * PAD, :]).astype(BF16) for i in range(steps)],
        axis=0,
    )
    for i in range(steps):
        if i < lanes // 2:
            smooth(i)
        for q in range(STEP // 16):
            at = i * STEP + q * 16
            for j in range(lanes):
                def load(piece):
                    return lambda d: piece(j, pl.ds(at + PAD + (zero + d if d else 0), 16))

                value, parts = cells(load(mid), load(low), load(high))
                place = (slice(at, at + 16), slice(j * 128, (j + 1) * 128))
                slope[place] = value
                for n, part in enumerate(parts):
                    flow[(n,) + place] = part
            for half, (start, size) in enumerate(halves):
                if q * 16 + 16 == start + size:
                    for copy in copies(i, half):
                        copy.start()
    for j in range(lanes // 2):
        relief_copy(j).wait()
    for i in range(steps):
        for half in range(2):
            for copy in copies(i, half):
                copy.wait()


def main(edge_values, inner, low, high, fall, left, right, source):
    lanes, rows, _ = low.shape
    cols = lanes * 128
    tall = rows - 2 * PAD
    return pl.pallas_call(
        main_kernel,
        out_shape=out_shapes(rows, cols),
        in_specs=[VMEM] * 9 + [SMEM],
        out_specs=[ANY] * 3,
        scratch_shapes=[
            pltpu.VMEM((tall, cols), F32),
            pltpu.VMEM((tall, cols), F32),
            pltpu.VMEM((8, tall, cols), BF16),
            pltpu.VMEM((rows, 256), BF16),
            pltpu.VMEM((2, rows, 128), F32),
            pltpu.SemaphoreType.DMA((tall // STEP, 2, 2)),
            pltpu.SemaphoreType.DMA((cols // 256,)),
        ],
        cost_estimate=cost(tall * cols),
        compiler_params=pltpu.CompilerParams(vmem_limit_bytes=32 * MIB),
        name="main_cells",
    )(
        edge_values, inner, low, high, fall, left, right,
        across_taps(512, 256), down_taps(STEP), source,
    )


def out_shapes(rows, cols):
    return [
        jax.ShapeDtypeStruct((rows, cols), F32),
        jax.ShapeDtypeStruct((rows, cols), F32),
        jax.ShapeDtypeStruct((8, rows, cols), BF16),
    ]


def cost(cells_done):
    return pl.CostEstimate(
        flops=cells_done * 4000, bytes_accessed=cells_done * 24, transcendentals=cells_done * 2
    )


def unpack_left(value, q):
    return value if q == 3 else pltpu.roll(value, 96 - PAD * q, 1)


def unpack_right(value, q):
    return value if q == 0 else pltpu.roll(value, 128 - PAD * q, 1)


def ends_kernel(
    edge_ref, inner_ref, band_ref, first_ref, second_ref, near_ref, next_ref, across, down,
    relief_in, slope_in, flow_in, relief_hbm, slope_hbm, flow_hbm,
    relief, slope, flow, wide, band, low_ref, high_ref, sems,
):
    rows, cols = band_ref.shape
    lanes = cols // 128
    near = 2 * PAD
    tall = PAD + 16
    inverse = 1.0 / (tap_total() ** 2)
    packed = first_ref.shape[0]
    others = before_and_after(near_ref[...], next_ref[...], "gy")
    for e in range(2):
        here = slice(PAD, PAD + near) if e == 0 else slice(0, near)
        there = slice(0, PAD) if e == 0 else slice(near, near + PAD)
        other = others[e]
        top = e * tall
        own_rows = slice(rows - near, rows) if e else slice(0, near)
        pack_rows = slice(packed - near, packed) if e else slice(0, near)
        band[e, here, 128 : 128 + cols] = band_ref[own_rows, :]
        band[e, there, 128 : 128 + cols] = other[:, 0:cols].astype(BF16)
        left, right = before_and_after(first_ref[pack_rows, :], second_ref[pack_rows, :], "gx")
        far_left = unpack_left(left, 3 * e)
        far_right = unpack_right(right, 3 * e)
        left, right = before_and_after(
            other[:, cols : cols + 128], other[:, cols + 128 : cols + 256], "gx"
        )
        corner_left = unpack_left(left, 0 if e else 3)
        corner_right = unpack_right(right, 0 if e else 3)
        band[e, here, 0:128] = far_left.astype(BF16)
        band[e, there, 0:128] = corner_left.astype(BF16)
        band[e, here, 128 + cols :] = far_right.astype(BF16)
        band[e, there, 128 + cols :] = corner_right.astype(BF16)
        if e == 0:
            wide[0, top : top + 8, :] = corner_left[PAD - 8 : PAD]
            wide[0, top + 8 : top + 48, :] = far_left[0:40]
            wide[lanes + 1, top : top + 8, :] = corner_right[PAD - 8 : PAD]
            wide[lanes + 1, top + 8 : top + 48, :] = far_right[0:40]
        else:
            wide[0, top : top + 40, :] = far_left[near - 40 : near]
            wide[0, top + 40 : top + 48, :] = corner_left[0:8]
            wide[lanes + 1, top : top + 40, :] = far_right[near - 40 : near]
            wide[lanes + 1, top + 40 : top + 48, :] = corner_right[0:8]
        for j in range(lanes):
            part = other[:, j * 128 : (j + 1) * 128]
            own = edge_ref.at[int(j > 0)] if j in (0, lanes - 1) else inner_ref.at[j - 1]
            if e == 0:
                wide[j + 1, top : top + 8, :] = part[PAD - 8 : PAD]
                wide[j + 1, top + 8 : top + 48, :] = own[0:40, :]
            else:
                wide[j + 1, top : top + 40, :] = own[rows - 40 : rows, :]
                wide[j + 1, top + 40 : top + 48, :] = part[0:8]

    smooth = jnp.concatenate([dot(down[...], band[e]).astype(BF16) for e in range(2)], axis=0)
    for j in range(lanes // 2):
        value = dot(smooth[:, j * 256 : j * 256 + 512], across[...])
        for e in range(2):
            for h in range(2):
                at = j * 256 + h * 128
                centre = wide[j * 2 + h + 1, e * tall + 8 : e * tall + 8 + PAD, :]
                part = value[e * PAD : (e + 1) * PAD, h * 128 : h * 128 + 128]
                relief[e, :, at : at + 128] = centre - part * inverse
    for j in range(lanes):
        low, high = sideways(wide[j + 1], wide[j], wide[j + 2])
        low_ref[j] = low
        high_ref[j] = high

    def one_end(e, carry):
        for at in range(0, PAD, 16):
            top = pl.multiple_of(e * tall + 8 + at, 8)
            for j in range(lanes):
                value, parts = cells(
                    lambda d: wide[j + 1, pl.ds(top + d, 16), :],
                    lambda d: low_ref[j, pl.ds(top + d, 16), :],
                    lambda d: high_ref[j, pl.ds(top + d, 16), :],
                )
                place = (slice(at, at + 16), slice(j * 128, (j + 1) * 128))
                slope[(e,) + place] = value
                for n, part in enumerate(parts):
                    flow[(e, n) + place] = part
        place = pl.ds(pl.multiple_of(e * (rows - PAD), PAD), PAD)
        pltpu.make_async_copy(relief.at[e], relief_hbm.at[place], sems.at[e, 0]).start()
        pltpu.make_async_copy(slope.at[e], slope_hbm.at[place], sems.at[e, 1]).start()
        pltpu.make_async_copy(flow.at[e], flow_hbm.at[:, place], sems.at[e, 2]).start()
        return carry

    lax.fori_loop(0, 2, one_end, 0)
    for e in range(2):
        place = pl.ds(e * (rows - PAD), PAD)
        pltpu.make_async_copy(relief.at[e], relief_hbm.at[place], sems.at[e, 0]).wait()
        pltpu.make_async_copy(slope.at[e], slope_hbm.at[place], sems.at[e, 1]).wait()
        pltpu.make_async_copy(flow.at[e], flow_hbm.at[:, place], sems.at[e, 2]).wait()


def ends(edge_values, inner, band, left, right, up, down, outs):
    rows, cols = band.shape
    lanes = cols // 128
    return pl.pallas_call(
        ends_kernel,
        out_shape=out_shapes(rows, cols),
        in_specs=[VMEM] * 9 + [ANY] * 3,
        out_specs=[ANY] * 3,
        input_output_aliases={9: 0, 10: 1, 11: 2},
        scratch_shapes=[
            pltpu.VMEM((2, PAD, cols), F32),
            pltpu.VMEM((2, PAD, cols), F32),
            pltpu.VMEM((2, 8, PAD, cols), BF16),
            pltpu.VMEM((lanes + 2, 2 * (PAD + 16), 128), F32),
            pltpu.VMEM((2, 3 * PAD, cols + 256), BF16),
            pltpu.VMEM((lanes, 2 * (PAD + 16), 128), F32),
            pltpu.VMEM((lanes, 2 * (PAD + 16), 128), F32),
            pltpu.SemaphoreType.DMA((2, 3)),
        ],
        cost_estimate=cost(2 * PAD * cols),
        compiler_params=pltpu.CompilerParams(vmem_limit_bytes=16 * MIB),
        name="end_cells",
    )(
        edge_values, inner, band, left, right, up, down,
        across_taps(512, 256), down_taps(PAD), *outs,
    )


def swap(first, second, axis):
    devices = lax.axis_size(axis)
    received = []
    for start, value in enumerate((first, second)):
        pairs = [(i, i + 1) for i in range(start, devices - 1, 2)]
        received.append(lax.ppermute(value, axis, pairs + [(j, i) for i, j in pairs]))
    return received


def local(source_blocks, block_scale, block_list, block_count, row_weights, col_weights):
    block_list = block_list.T
    outgoing, source = gather(block_list, block_count, block_scale, source_blocks)
    edge = source_blocks.shape[1]
    arrived = lax.all_to_all(outgoing, "gy", split_axis=0, concat_axis=0, tiled=True)
    arrived = arrived.reshape(-1, edge, edge)
    weights = (row_weights, col_weights)
    edge_values, *messages = edges(source, arrived, *weights)
    beside = swap(*messages, "gx")
    inner, low, high, band, fall, strips, odd = middle(source, arrived, *weights, edge_values)
    messages = []
    for n in range(2):
        corners = [jnp.where(odd[:1] == n, side[-PAD:], side[:PAD]) for side in beside]
        messages.append(jnp.concatenate([strips[n], *corners], axis=1))
    ahead = swap(*messages, "gy")
    outs = main(edge_values, inner, low, high, fall, *beside, source)
    return tuple(ends(edge_values, inner, band, *beside, *ahead, outs))


def solution(mesh):
    in_specs = (
        P(("gx", "gy"), None, None),
        P(("gx", "gy")),
        P(),
        P(),
        P(("gx", "gy"), None, None),
        P(("gx", "gy"), None, None),
    )
    out_specs = (P("gy", "gx"), P("gy", "gx"), P(None, "gy", "gx"))
    return jax.shard_map(local, mesh=mesh, in_specs=in_specs, out_specs=out_specs, check_vma=False)
```

```python
import jax
import jax.numpy as jnp
import ml_dtypes
import numpy as np
from jax import lax
from jax.experimental import pallas as pl
from jax.experimental.pallas import tpu as pltpu
from jax.sharding import PartitionSpec as P

W = 6
CAP = 4
RIM = 24
PAD = 32
SIGMA = 10.0
FLAT = 0.05
DIAG = 0.5**0.5
F32 = jnp.float32
BF16 = jnp.bfloat16
MIB = 1 << 20
ZERO_AT = W * W

SMEM = pl.BlockSpec(memory_space=pltpu.SMEM)
VMEM = pl.BlockSpec(memory_space=pltpu.VMEM)
ANY = pl.BlockSpec(memory_space=pl.ANY)


def gather_kernel(
    list_hbm, count_hbm, scale_hbm, blocks_hbm, out_hbm, source_hbm,
    listed, counted, scale, blocks, found, table, staged,
    named, numbered, seen, source, sems, out_sems,
):
    holders = lax.axis_size("gy")
    first = lax.axis_index("gx") * holders
    held = blocks.shape[0]
    base = (first + lax.axis_index("gy")) * held
    slots = listed.shape[0]
    copies = [
        pltpu.make_async_copy(list_hbm, listed, sems.at[0]),
        pltpu.make_async_copy(count_hbm, counted, sems.at[1]),
        pltpu.make_async_copy(scale_hbm, scale, sems.at[2]),
        pltpu.make_async_copy(blocks_hbm, blocks, sems.at[3]),
        pltpu.make_async_copy(list_hbm, named, sems.at[5]),
        pltpu.make_async_copy(count_hbm, numbered, sems.at[6]),
    ]
    for copy in copies:
        copy.start()
    copies[0].wait()
    copies[1].wait()
    shape = found.shape
    row = lax.broadcasted_iota(jnp.int32, shape, 0)
    live = jnp.broadcast_to(counted[...], shape)
    rank = jnp.zeros(shape, jnp.int32)
    chosen = jnp.zeros(shape, jnp.int32)
    for k in range(slots):
        block = jnp.broadcast_to(listed[k : k + 1, :], shape) - base
        hit = (block >= 0) & (block < held) & (k < live)
        chosen = jnp.where(hit & (rank == row), block, chosen)
        rank = rank + hit.astype(jnp.int32)
    found[...] = jnp.where(row < CAP, chosen, rank)
    handed = pltpu.make_async_copy(found, table, sems.at[4])
    handed.start()
    copies[4].wait()
    copies[5].wait()
    tile = first + lax.axis_index("gy")
    count = numbered[0, tile]
    for h in range(out_hbm.shape[0]):
        seen[h] = 0
    for k in range(slots):
        block = jnp.clip(named[k, tile] - first * held, 0, out_hbm.shape[0] * held - 1)
        owner = lax.shift_right_logical(block, jnp.int32(held.bit_length() - 1))
        rank = seen[owner]
        source[0, k] = owner * CAP + jnp.minimum(rank, CAP - 1)
        seen[owner] = rank + (k < count).astype(jnp.int32)
    source[0, slots] = count
    told = pltpu.make_async_copy(source, source_hbm, sems.at[7])
    told.start()
    handed.wait()
    copies[2].wait()
    copies[3].wait()

    def one_tile(t, carry):
        @pl.when(table[CAP, first + t] > 0)
        def fill():
            for j in range(CAP):
                block = table[j, first + t]
                value = blocks[block].astype(F32) * scale[block]
                staged[t, j] = value.astype(BF16)
            pltpu.make_async_copy(staged.at[t], out_hbm.at[t], out_sems.at[t]).start()

        return carry

    lax.fori_loop(0, holders, one_tile, 0)

    def one_wait(t, carry):
        @pl.when(table[CAP, first + t] > 0)
        def drain():
            pltpu.make_async_copy(staged.at[t], out_hbm.at[t], out_sems.at[t]).wait()

        return carry

    lax.fori_loop(0, holders, one_wait, 0)
    told.wait()


def gather(block_list, block_count, block_scale, source_blocks):
    held, edge, _ = source_blocks.shape
    holders = lax.axis_size("gy")
    slots, tiles = block_list.shape
    return pl.pallas_call(
        gather_kernel,
        out_shape=[
            jax.ShapeDtypeStruct((holders, CAP, edge, edge), BF16),
            jax.ShapeDtypeStruct((1, tiles), jnp.int32),
        ],
        in_specs=[ANY] * 4,
        out_specs=[ANY] * 2,
        scratch_shapes=[
            pltpu.VMEM((slots, tiles), jnp.int32),
            pltpu.VMEM((1, tiles), jnp.int32),
            pltpu.SMEM((held,), F32),
            pltpu.VMEM((held, edge, edge), BF16),
            pltpu.VMEM((8, tiles), jnp.int32),
            pltpu.SMEM((8, tiles), jnp.int32),
            pltpu.VMEM((holders, CAP, edge, edge), BF16),
            pltpu.SMEM((slots, tiles), jnp.int32),
            pltpu.SMEM((1, tiles), jnp.int32),
            pltpu.SMEM((holders,), jnp.int32),
            pltpu.SMEM((1, tiles), jnp.int32),
            pltpu.SemaphoreType.DMA((8,)),
            pltpu.SemaphoreType.DMA((holders,)),
        ],
        compiler_params=pltpu.CompilerParams(vmem_limit_bytes=56 * MIB),
        name="gather_blocks",
    )(block_list, block_count.reshape(1, tiles), block_scale, source_blocks)


def is_even(axis):
    return lax.rem(lax.axis_index(axis), 2) == 0


def before_and_after(first, second, axis):
    even = is_even(axis)
    first, second = first.astype(F32), second.astype(F32)
    return jnp.where(even, second, first), jnp.where(even, first, second)


def first_products(windows, source_ref, arrived_ref, row_ref):
    live = source_ref[0, row_ref.shape[0]]
    values = [dot(row_ref[k], arrived_ref[source_ref[0, k]]) for k in windows]
    return [jnp.where(k < live, value, 0.0).astype(BF16) for k, value in zip(windows, values)]


def edges_kernel(
    source_ref, arrived_ref, row_ref, col_ref, edge_ref, first_ref, second_ref
):
    edge = row_ref.shape[1]
    for s in range(2):
        windows = [i * W + s * (W - 1) for i in range(W)]
        parts = first_products(windows, source_ref, arrived_ref, row_ref)
        values = [dot(part, col_ref[k]) for k, part in zip(windows, parts)]
        for i, value in enumerate(values):
            edge_ref[s, i * edge : (i + 1) * edge, :] = value
    rows = edge_ref.shape[1]
    chunk = rows // 4
    lane = lax.broadcasted_iota(jnp.int32, (chunk, 128), 1)
    left = jnp.zeros((chunk, 128), F32)
    right = jnp.zeros((chunk, 128), F32)
    for q in range(4):
        mine = (lane >= PAD * q) & (lane < PAD * (q + 1))
        part = edge_ref[0, q * chunk : (q + 1) * chunk, :]
        if q:
            part = pltpu.roll(part, PAD * q, 1)
        left = jnp.where(mine, part, left)
        part = edge_ref[1, q * chunk : (q + 1) * chunk, :]
        if q != 3:
            part = pltpu.roll(part, PAD * (q + 1), 1)
        right = jnp.where(mine, part, right)
    even = is_even("gx")
    first_ref[...] = jnp.where(even, right, left).astype(BF16)
    second_ref[...] = jnp.where(even, left, right).astype(BF16)


def edges(source, arrived, row_weights, col_weights):
    edge = row_weights.shape[1]
    side = W * edge
    shapes = [((2, side, edge), F32), ((side // 4, 128), BF16), ((side // 4, 128), BF16)]
    return pl.pallas_call(
        edges_kernel,
        out_shape=[jax.ShapeDtypeStruct(s, d) for s, d in shapes],
        in_specs=[SMEM, VMEM, VMEM, VMEM],
        out_specs=[VMEM] * len(shapes),
        cost_estimate=cost(side * 256),
        compiler_params=pltpu.CompilerParams(vmem_limit_bytes=16 * MIB),
        name="edge_windows",
    )(source, arrived, row_weights, col_weights)


def middle_kernel(
    source_ref, arrived_ref, row_ref, col_ref, edge_ref, down,
    inner_ref, low_ref, high_ref, band_ref, fall_ref, strips_ref, odd_ref,
):
    edge = row_ref.shape[1]
    rows = band_ref.shape[0]
    odd = lax.rem(lax.axis_index("gy"), 2)
    odd_ref[...] = jnp.full(odd_ref.shape, odd, jnp.int32)
    for s in range(2):
        band_ref[:, s * (W - 1) * edge : (s * (W - 1) + 1) * edge] = edge_ref[s].astype(BF16)


    def shifts(i):
        span = slice(i * edge, (i + 1) * edge)
        pieces = [edge_ref[0, span, :]]
        pieces += [inner_ref[j, span, :] for j in range(W - 2)] + [edge_ref[1, span, :]]
        lane = lax.broadcasted_iota(jnp.int32, pieces[0].shape, 1)
        lows = [pltpu.roll(piece, 1, 1) for piece in pieces]
        highs = [pltpu.roll(piece, 127, 1) for piece in pieces]
        for j in range(W):
            low_ref[j, span, :] = jnp.where(lane == 0, lows[j - 1], lows[j]) if j else lows[j]
            high_ref[j, span, :] = (
                jnp.where(lane == 127, highs[j + 1], highs[j]) if j < W - 1 else highs[j]
            )

    fallen = 0
    for t in range(W + 1):
        while fallen < rows - 2 * PAD and fallen + STEP + 2 * PAD <= t * edge:
            value = dot(down[...], band_ref[fallen : fallen + STEP + 2 * PAD, :])
            fall_ref[fallen : fallen + STEP, :] = value.astype(BF16)
            fallen += STEP
        windows = [t * W + j for j in range(1, W - 1)] if t < W else []
        parts = first_products(windows, source_ref, arrived_ref, row_ref)
        if t:
            shifts(t - 1)
        values = [dot(part, col_ref[k]) for k, part in zip(windows, parts)]
        span = slice(t * edge, (t + 1) * edge)
        for j, value in enumerate(values):
            inner_ref[j, span, :] = value
            band_ref[span, (j + 1) * edge : (j + 2) * edge] = value.astype(BF16)
    for n in range(2):
        at = pl.multiple_of(jnp.where(odd == n, rows - PAD, 0), PAD)
        strips_ref[n] = band_ref[pl.ds(at, PAD), :]


def middle(source, arrived, row_weights, col_weights, edge_values):
    edge = row_weights.shape[1]
    side = W * edge
    shapes = [
        ((W - 2, side, edge), F32),
        ((W, side, edge), F32),
        ((W, side, edge), F32),
        ((side, side), BF16),
        ((side - 2 * PAD, side), BF16),
        ((2, PAD, side), BF16),
        ((8, 128), jnp.int32),
    ]
    return pl.pallas_call(
        middle_kernel,
        out_shape=[jax.ShapeDtypeStruct(s, d) for s, d in shapes],
        in_specs=[SMEM] + [VMEM] * 5,
        out_specs=[VMEM] * len(shapes),
        cost_estimate=cost(side * side),
        compiler_params=pltpu.CompilerParams(vmem_limit_bytes=24 * MIB),
        name="middle_windows",
    )(source, arrived, row_weights, col_weights, edge_values, down_taps(STEP))


def tap(offset):
    value = np.exp(-(offset * offset).astype(np.float32) / np.float32(2.0 * SIGMA * SIGMA))
    return np.where(np.abs(offset) <= RIM, value, 0.0).astype(ml_dtypes.bfloat16)


def tap_total():
    return float(np.sum(tap(np.arange(-RIM, RIM + 1)).astype(np.float64)))


def across_taps(wide, out):
    return jnp.asarray(tap(np.arange(wide)[:, None] - np.arange(out)[None, :] - 128))


def down_taps(step):
    return jnp.asarray(tap(np.arange(step + 2 * PAD)[None, :] - np.arange(step)[:, None] - PAD))


def cells(mid, low, high):
    centre, cl, cr = [load(0).astype(BF16) for load in (mid, low, high)]
    uc, ul, ur = [load(-1).astype(BF16) for load in (mid, low, high)]
    dc, dl, dr = [load(1).astype(BF16) for load in (mid, low, high)]
    one = dr - ul
    two = ur - dl
    across = cr - cl
    along = dc - uc
    grad_x = (one + two) + (across + across)
    grad_y = (one - two) + (along + along)
    steep = grad_x * grad_x + grad_y * grad_y
    square = BF16(1.0) + steep * BF16(1.0 / 64.0)
    slope = (square * lax.rsqrt(square)).astype(F32)
    flows = []
    for value, diagonal in (
        (ul, True), (uc, False), (ur, True), (cl, False),
        (cr, False), (dl, True), (dc, False), (dr, True),
    ):
        drop = jnp.maximum(centre - value, 0)
        flows.append((drop * BF16(DIAG) if diagonal else drop) + BF16(FLAT))
    total = (
        ((flows[0] + flows[1]) + (flows[2] + flows[3]))
        + ((flows[4] + flows[5]) + (flows[6] + flows[7]))
    )
    share = pl.reciprocal(total.astype(F32), approx=True).astype(BF16)
    return slope, [flow * share for flow in flows]


def sideways(centre, before, after):
    lane = lax.broadcasted_iota(jnp.int32, centre.shape, 1)
    low = jnp.where(lane == 0, pltpu.roll(before, 1, 1), pltpu.roll(centre, 1, 1))
    high = jnp.where(lane == 127, pltpu.roll(after, 127, 1), pltpu.roll(centre, 127, 1))
    return low, high


def dot(a, b):
    return jnp.dot(a, b, preferred_element_type=F32)


STEP = 176


def main_kernel(
    edge_ref, inner_ref, low_ref, high_ref, fall_ref, first_ref, second_ref, across, down,
    zero_ref, relief_hbm, slope_hbm, flow_hbm, relief, slope, flow, far, patched, sems, relief_sems,
):
    rows, cols = low_ref.shape[1], relief.shape[1]
    lanes = cols // 128
    steps = (rows - 2 * PAD) // STEP
    chunk = rows // 4
    inverse = 1.0 / (tap_total() ** 2)
    lane = lax.broadcasted_iota(jnp.int32, (chunk, 128), 1)
    left, right = before_and_after(first_ref[...], second_ref[...], "gx")
    for q in range(4):
        span = slice(q * chunk, (q + 1) * chunk)
        value = unpack_left(left, q)
        far[span, 0:128] = value.astype(BF16)
        patched[0, span, :] = jnp.where(lane == 0, pltpu.roll(value, 1, 1), low_ref[0, span, :])
        value = unpack_right(right, q)
        far[span, 128:256] = value.astype(BF16)
        patched[1, span, :] = jnp.where(
            lane == 127, pltpu.roll(value, 127, 1), high_ref[lanes - 1, span, :]
        )

    halves = ((0, 96), (96, STEP - 96))

    def copies(i, half):
        start, size = halves[half]
        span = slice(i * STEP + start, i * STEP + start + size)
        place = pl.ds(PAD + i * STEP + start, size)
        sem = sems.at[i, half]
        return (
            pltpu.make_async_copy(slope.at[span], slope_hbm.at[place], sem.at[0]),
            pltpu.make_async_copy(flow.at[:, span], flow_hbm.at[:, place], sem.at[1]),
        )

    def relief_copy(j):
        column = pl.ds(j * 256, 256)
        return pltpu.make_async_copy(
            relief.at[:, column], relief_hbm.at[pl.ds(PAD, rows - 2 * PAD), column], relief_sems.at[j]
        )

    def mid(j, span):
        if j in (0, lanes - 1):
            return edge_ref[int(j > 0), span, :]
        return inner_ref[j - 1, span, :]

    def low(j, span):
        return low_ref[j, span, :] if j else patched[0, span, :]

    def high(j, span):
        return high_ref[j, span, :] if j < lanes - 1 else patched[1, span, :]

    def smooth(j):
        at = j * 256
        if j == 0:
            wide = jnp.concatenate([sides[:, 0:128], fall_ref[:, 0:384]], axis=1)
        elif j == lanes // 2 - 1:
            wide = jnp.concatenate([fall_ref[:, at - 128 :], sides[:, 128:256]], axis=1)
        else:
            wide = fall_ref[:, at - 128 : at + 384]
        return dot(wide, across[...])

    def relieve(j, value):
        at = j * 256
        for h in range(2):
            centre = mid(j * 2 + h, slice(PAD, rows - PAD))
            relief[:, at + h * 128 : at + h * 128 + 128] = (
                centre - value[:, h * 128 : h * 128 + 128] * inverse
            )
        relief_copy(j).start()

    zero = jnp.minimum(zero_ref[0, ZERO_AT], 0)
    sides = jnp.concatenate(
        [dot(down[...], far[i * STEP : (i + 1) * STEP + 2 * PAD, :]).astype(BF16) for i in range(steps)],
        axis=0,
    )
    for i in range(steps):
        smoothed = smooth(i) if i < lanes // 2 else None
        for q in range(STEP // 16):
            if q == 5 and smoothed is not None:
                relieve(i, smoothed)
            at = i * STEP + q * 16
            for j in range(lanes):
                def load(piece):
                    return lambda d: piece(j, pl.ds(at + PAD + (zero + d if d else 0), 16))

                value, parts = cells(load(mid), load(low), load(high))
                place = (slice(at, at + 16), slice(j * 128, (j + 1) * 128))
                slope[place] = value
                for n, part in enumerate(parts):
                    flow[(n,) + place] = part
            for half, (start, size) in enumerate(halves):
                if q * 16 + 16 == start + size:
                    for copy in copies(i, half):
                        copy.start()
    for j in range(lanes // 2):
        relief_copy(j).wait()
    for i in range(steps):
        for half in range(2):
            for copy in copies(i, half):
                copy.wait()


def main(edge_values, inner, low, high, fall, left, right, source):
    lanes, rows, _ = low.shape
    cols = lanes * 128
    tall = rows - 2 * PAD
    return pl.pallas_call(
        main_kernel,
        out_shape=out_shapes(rows, cols),
        in_specs=[VMEM] * 9 + [SMEM],
        out_specs=[ANY] * 3,
        scratch_shapes=[
            pltpu.VMEM((tall, cols), F32),
            pltpu.VMEM((tall, cols), F32),
            pltpu.VMEM((8, tall, cols), BF16),
            pltpu.VMEM((rows, 256), BF16),
            pltpu.VMEM((2, rows, 128), F32),
            pltpu.SemaphoreType.DMA((tall // STEP, 2, 2)),
            pltpu.SemaphoreType.DMA((cols // 256,)),
        ],
        cost_estimate=cost(tall * cols),
        compiler_params=pltpu.CompilerParams(vmem_limit_bytes=32 * MIB),
        name="main_cells",
    )(
        edge_values, inner, low, high, fall, left, right,
        across_taps(512, 256), down_taps(STEP), source,
    )


def out_shapes(rows, cols):
    return [
        jax.ShapeDtypeStruct((rows, cols), F32),
        jax.ShapeDtypeStruct((rows, cols), F32),
        jax.ShapeDtypeStruct((8, rows, cols), BF16),
    ]


def cost(cells_done):
    return pl.CostEstimate(
        flops=cells_done * 4000, bytes_accessed=cells_done * 24, transcendentals=cells_done * 2
    )


def unpack_left(value, q):
    return value if q == 3 else pltpu.roll(value, 96 - PAD * q, 1)


def unpack_right(value, q):
    return value if q == 0 else pltpu.roll(value, 128 - PAD * q, 1)


def ends_kernel(
    edge_ref, inner_ref, band_ref, first_ref, second_ref, near_ref, next_ref, across, down,
    relief_in, slope_in, flow_in, relief_hbm, slope_hbm, flow_hbm,
    relief, slope, flow, wide, band, low_ref, high_ref, sems,
):
    rows, cols = band_ref.shape
    lanes = cols // 128
    near = 2 * PAD
    tall = PAD + 16
    inverse = 1.0 / (tap_total() ** 2)
    packed = first_ref.shape[0]
    others = before_and_after(near_ref[...], next_ref[...], "gy")
    for e in range(2):
        here = slice(PAD, PAD + near) if e == 0 else slice(0, near)
        there = slice(0, PAD) if e == 0 else slice(near, near + PAD)
        other = others[e]
        top = e * tall
        own_rows = slice(rows - near, rows) if e else slice(0, near)
        pack_rows = slice(packed - near, packed) if e else slice(0, near)
        band[e, here, 128 : 128 + cols] = band_ref[own_rows, :]
        band[e, there, 128 : 128 + cols] = other[:, 0:cols].astype(BF16)
        left, right = before_and_after(first_ref[pack_rows, :], second_ref[pack_rows, :], "gx")
        far_left = unpack_left(left, 3 * e)
        far_right = unpack_right(right, 3 * e)
        left, right = before_and_after(
            other[:, cols : cols + 128], other[:, cols + 128 : cols + 256], "gx"
        )
        corner_left = unpack_left(left, 0 if e else 3)
        corner_right = unpack_right(right, 0 if e else 3)
        band[e, here, 0:128] = far_left.astype(BF16)
        band[e, there, 0:128] = corner_left.astype(BF16)
        band[e, here, 128 + cols :] = far_right.astype(BF16)
        band[e, there, 128 + cols :] = corner_right.astype(BF16)
        if e == 0:
            wide[0, top : top + 8, :] = corner_left[PAD - 8 : PAD]
            wide[0, top + 8 : top + 48, :] = far_left[0:40]
            wide[lanes + 1, top : top + 8, :] = corner_right[PAD - 8 : PAD]
            wide[lanes + 1, top + 8 : top + 48, :] = far_right[0:40]
        else:
            wide[0, top : top + 40, :] = far_left[near - 40 : near]
            wide[0, top + 40 : top + 48, :] = corner_left[0:8]
            wide[lanes + 1, top : top + 40, :] = far_right[near - 40 : near]
            wide[lanes + 1, top + 40 : top + 48, :] = corner_right[0:8]
        for j in range(lanes):
            part = other[:, j * 128 : (j + 1) * 128]
            own = edge_ref.at[int(j > 0)] if j in (0, lanes - 1) else inner_ref.at[j - 1]
            if e == 0:
                wide[j + 1, top : top + 8, :] = part[PAD - 8 : PAD]
                wide[j + 1, top + 8 : top + 48, :] = own[0:40, :]
            else:
                wide[j + 1, top : top + 40, :] = own[rows - 40 : rows, :]
                wide[j + 1, top + 40 : top + 48, :] = part[0:8]

    smooth = jnp.concatenate([dot(down[...], band[e]).astype(BF16) for e in range(2)], axis=0)
    for j in range(lanes // 2):
        value = dot(smooth[:, j * 256 : j * 256 + 512], across[...])
        for e in range(2):
            for h in range(2):
                at = j * 256 + h * 128
                centre = wide[j * 2 + h + 1, e * tall + 8 : e * tall + 8 + PAD, :]
                part = value[e * PAD : (e + 1) * PAD, h * 128 : h * 128 + 128]
                relief[e, :, at : at + 128] = centre - part * inverse
    for j in range(lanes):
        low, high = sideways(wide[j + 1], wide[j], wide[j + 2])
        low_ref[j] = low
        high_ref[j] = high

    def one_end(e, carry):
        for at in range(0, PAD, 16):
            top = pl.multiple_of(e * tall + 8 + at, 8)
            for j in range(lanes):
                value, parts = cells(
                    lambda d: wide[j + 1, pl.ds(top + d, 16), :],
                    lambda d: low_ref[j, pl.ds(top + d, 16), :],
                    lambda d: high_ref[j, pl.ds(top + d, 16), :],
                )
                place = (slice(at, at + 16), slice(j * 128, (j + 1) * 128))
                slope[(e,) + place] = value
                for n, part in enumerate(parts):
                    flow[(e, n) + place] = part
        place = pl.ds(pl.multiple_of(e * (rows - PAD), PAD), PAD)
        pltpu.make_async_copy(relief.at[e], relief_hbm.at[place], sems.at[e, 0]).start()
        pltpu.make_async_copy(slope.at[e], slope_hbm.at[place], sems.at[e, 1]).start()
        pltpu.make_async_copy(flow.at[e], flow_hbm.at[:, place], sems.at[e, 2]).start()
        return carry

    lax.fori_loop(0, 2, one_end, 0)
    for e in range(2):
        place = pl.ds(e * (rows - PAD), PAD)
        pltpu.make_async_copy(relief.at[e], relief_hbm.at[place], sems.at[e, 0]).wait()
        pltpu.make_async_copy(slope.at[e], slope_hbm.at[place], sems.at[e, 1]).wait()
        pltpu.make_async_copy(flow.at[e], flow_hbm.at[:, place], sems.at[e, 2]).wait()


def ends(edge_values, inner, band, left, right, up, down, outs):
    rows, cols = band.shape
    lanes = cols // 128
    return pl.pallas_call(
        ends_kernel,
        out_shape=out_shapes(rows, cols),
        in_specs=[VMEM] * 9 + [ANY] * 3,
        out_specs=[ANY] * 3,
        input_output_aliases={9: 0, 10: 1, 11: 2},
        scratch_shapes=[
            pltpu.VMEM((2, PAD, cols), F32),
            pltpu.VMEM((2, PAD, cols), F32),
            pltpu.VMEM((2, 8, PAD, cols), BF16),
            pltpu.VMEM((lanes + 2, 2 * (PAD + 16), 128), F32),
            pltpu.VMEM((2, 3 * PAD, cols + 256), BF16),
            pltpu.VMEM((lanes, 2 * (PAD + 16), 128), F32),
            pltpu.VMEM((lanes, 2 * (PAD + 16), 128), F32),
            pltpu.SemaphoreType.DMA((2, 3)),
        ],
        cost_estimate=cost(2 * PAD * cols),
        compiler_params=pltpu.CompilerParams(vmem_limit_bytes=16 * MIB),
        name="end_cells",
    )(
        edge_values, inner, band, left, right, up, down,
        across_taps(512, 256), down_taps(PAD), *outs,
    )


def swap(first, second, axis):
    devices = lax.axis_size(axis)
    received = []
    for start, value in enumerate((first, second)):
        pairs = [(i, i + 1) for i in range(start, devices - 1, 2)]
        received.append(lax.ppermute(value, axis, pairs + [(j, i) for i, j in pairs]))
    return received


def local(source_blocks, block_scale, block_list, block_count, row_weights, col_weights):
    block_list = block_list.T
    outgoing, source = gather(block_list, block_count, block_scale, source_blocks)
    edge = source_blocks.shape[1]
    arrived = lax.all_to_all(outgoing, "gy", split_axis=0, concat_axis=0, tiled=True)
    arrived = arrived.reshape(-1, edge, edge)
    weights = (row_weights, col_weights)
    edge_values, *messages = edges(source, arrived, *weights)
    beside = swap(*messages, "gx")
    inner, low, high, band, fall, strips, odd = middle(source, arrived, *weights, edge_values)
    messages = []
    for n in range(2):
        corners = [jnp.where(odd[:1] == n, side[-PAD:], side[:PAD]) for side in beside]
        messages.append(jnp.concatenate([strips[n], *corners], axis=1))
    ahead = swap(*messages, "gy")
    outs = main(edge_values, inner, low, high, fall, *beside, source)
    return tuple(ends(edge_values, inner, band, *beside, *ahead, outs))


def solution(mesh):
    in_specs = (
        P(("gx", "gy"), None, None),
        P(("gx", "gy")),
        P(),
        P(),
        P(("gx", "gy"), None, None),
        P(("gx", "gy"), None, None),
    )
    out_specs = (P("gy", "gx"), P("gy", "gx"), P(None, "gy", "gx"))
    return jax.shard_map(local, mesh=mesh, in_specs=in_specs, out_specs=out_specs, check_vma=False)
```

```python
import jax
import jax.numpy as jnp
import ml_dtypes
import numpy as np
from jax import lax
from jax.experimental import pallas as pl
from jax.experimental.pallas import tpu as pltpu
from jax.sharding import PartitionSpec as P

W = 6
CAP = 4
RIM = 24
PAD = 32
SIGMA = 10.0
FLAT = 0.05
DIAG = 0.5**0.5
F32 = jnp.float32
BF16 = jnp.bfloat16
MIB = 1 << 20
EARLY = 4
EARLY_ROWS = EARLY * 128 - 16 - PAD
ZERO_AT = W * W

SMEM = pl.BlockSpec(memory_space=pltpu.SMEM)
VMEM = pl.BlockSpec(memory_space=pltpu.VMEM)
ANY = pl.BlockSpec(memory_space=pl.ANY)


def gather_kernel(
    list_hbm, count_hbm, scale_hbm, blocks_hbm, out_hbm, source_hbm,
    listed, counted, scale, blocks, found, table, staged,
    named, numbered, seen, source, sems, out_sems,
):
    holders = lax.axis_size("gy")
    first = lax.axis_index("gx") * holders
    held = blocks.shape[0]
    base = (first + lax.axis_index("gy")) * held
    slots = listed.shape[0]
    copies = [
        pltpu.make_async_copy(list_hbm, listed, sems.at[0]),
        pltpu.make_async_copy(count_hbm, counted, sems.at[1]),
        pltpu.make_async_copy(scale_hbm, scale, sems.at[2]),
        pltpu.make_async_copy(blocks_hbm, blocks, sems.at[3]),
        pltpu.make_async_copy(list_hbm, named, sems.at[5]),
        pltpu.make_async_copy(count_hbm, numbered, sems.at[6]),
    ]
    for copy in copies:
        copy.start()
    copies[0].wait()
    copies[1].wait()
    shape = found.shape
    row = lax.broadcasted_iota(jnp.int32, shape, 0)
    live = jnp.broadcast_to(counted[...], shape)
    rank = jnp.zeros(shape, jnp.int32)
    chosen = jnp.zeros(shape, jnp.int32)
    for k in range(slots):
        block = jnp.broadcast_to(listed[k : k + 1, :], shape) - base
        hit = (block >= 0) & (block < held) & (k < live)
        chosen = jnp.where(hit & (rank == row), block, chosen)
        rank = rank + hit.astype(jnp.int32)
    found[...] = jnp.where(row < CAP, chosen, rank)
    handed = pltpu.make_async_copy(found, table, sems.at[4])
    handed.start()
    copies[4].wait()
    copies[5].wait()
    tile = first + lax.axis_index("gy")
    count = numbered[0, tile]
    for h in range(out_hbm.shape[0]):
        seen[h] = 0
    for k in range(slots):
        block = jnp.clip(named[k, tile] - first * held, 0, out_hbm.shape[0] * held - 1)
        owner = lax.shift_right_logical(block, jnp.int32(held.bit_length() - 1))
        rank = seen[owner]
        source[0, k] = owner * CAP + jnp.minimum(rank, CAP - 1)
        seen[owner] = rank + (k < count).astype(jnp.int32)
    source[0, slots] = count
    told = pltpu.make_async_copy(source, source_hbm, sems.at[7])
    told.start()
    handed.wait()
    copies[2].wait()
    copies[3].wait()

    def one_tile(t, carry):
        @pl.when(table[CAP, first + t] > 0)
        def fill():
            for j in range(CAP):
                block = table[j, first + t]
                value = blocks[block].astype(F32) * scale[block]
                staged[t, j] = value.astype(BF16)
            pltpu.make_async_copy(staged.at[t], out_hbm.at[t], out_sems.at[t]).start()

        return carry

    lax.fori_loop(0, holders, one_tile, 0)

    def one_wait(t, carry):
        @pl.when(table[CAP, first + t] > 0)
        def drain():
            pltpu.make_async_copy(staged.at[t], out_hbm.at[t], out_sems.at[t]).wait()

        return carry

    lax.fori_loop(0, holders, one_wait, 0)
    told.wait()


def gather(block_list, block_count, block_scale, source_blocks):
    held, edge, _ = source_blocks.shape
    holders = lax.axis_size("gy")
    slots, tiles = block_list.shape
    return pl.pallas_call(
        gather_kernel,
        out_shape=[
            jax.ShapeDtypeStruct((holders, CAP, edge, edge), BF16),
            jax.ShapeDtypeStruct((1, tiles), jnp.int32),
        ],
        in_specs=[ANY] * 4,
        out_specs=[ANY] * 2,
        scratch_shapes=[
            pltpu.VMEM((slots, tiles), jnp.int32),
            pltpu.VMEM((1, tiles), jnp.int32),
            pltpu.SMEM((held,), F32),
            pltpu.VMEM((held, edge, edge), BF16),
            pltpu.VMEM((8, tiles), jnp.int32),
            pltpu.SMEM((8, tiles), jnp.int32),
            pltpu.VMEM((holders, CAP, edge, edge), BF16),
            pltpu.SMEM((slots, tiles), jnp.int32),
            pltpu.SMEM((1, tiles), jnp.int32),
            pltpu.SMEM((holders,), jnp.int32),
            pltpu.SMEM((1, tiles), jnp.int32),
            pltpu.SemaphoreType.DMA((8,)),
            pltpu.SemaphoreType.DMA((holders,)),
        ],
        compiler_params=pltpu.CompilerParams(vmem_limit_bytes=56 * MIB),
        name="gather_blocks",
    )(block_list, block_count.reshape(1, tiles), block_scale, source_blocks)


def is_even(axis):
    return lax.rem(lax.axis_index(axis), 2) == 0


def before_and_after(first, second, axis):
    even = is_even(axis)
    first, second = first.astype(F32), second.astype(F32)
    return jnp.where(even, second, first), jnp.where(even, first, second)


def first_products(windows, source_ref, arrived_ref, row_ref):
    live = source_ref[0, row_ref.shape[0]]
    values = [dot(row_ref[k], arrived_ref[source_ref[0, k]]) for k in windows]
    return [jnp.where(k < live, value, 0.0).astype(BF16) for k, value in zip(windows, values)]


def edges_kernel(
    source_ref, arrived_ref, row_ref, col_ref, edge_ref, first_ref, second_ref
):
    edge = row_ref.shape[1]
    for s in range(2):
        windows = [i * W + s * (W - 1) for i in range(W)]
        parts = first_products(windows, source_ref, arrived_ref, row_ref)
        values = [dot(part, col_ref[k]) for k, part in zip(windows, parts)]
        for i, value in enumerate(values):
            edge_ref[s, i * edge : (i + 1) * edge, :] = value
    rows = edge_ref.shape[1]
    chunk = rows // 4
    lane = lax.broadcasted_iota(jnp.int32, (chunk, 128), 1)
    left = jnp.zeros((chunk, 128), F32)
    right = jnp.zeros((chunk, 128), F32)
    for q in range(4):
        mine = (lane >= PAD * q) & (lane < PAD * (q + 1))
        part = edge_ref[0, q * chunk : (q + 1) * chunk, :]
        if q:
            part = pltpu.roll(part, PAD * q, 1)
        left = jnp.where(mine, part, left)
        part = edge_ref[1, q * chunk : (q + 1) * chunk, :]
        if q != 3:
            part = pltpu.roll(part, PAD * (q + 1), 1)
        right = jnp.where(mine, part, right)
    even = is_even("gx")
    first_ref[...] = jnp.where(even, right, left).astype(BF16)
    second_ref[...] = jnp.where(even, left, right).astype(BF16)


def edges(source, arrived, row_weights, col_weights):
    edge = row_weights.shape[1]
    side = W * edge
    shapes = [((2, side, edge), F32), ((side // 4, 128), BF16), ((side // 4, 128), BF16)]
    return pl.pallas_call(
        edges_kernel,
        out_shape=[jax.ShapeDtypeStruct(s, d) for s, d in shapes],
        in_specs=[SMEM, VMEM, VMEM, VMEM],
        out_specs=[VMEM] * len(shapes),
        cost_estimate=cost(side * 256),
        compiler_params=pltpu.CompilerParams(vmem_limit_bytes=16 * MIB),
        name="edge_windows",
    )(source, arrived, row_weights, col_weights)


def middle_kernel(
    source_ref, arrived_ref, row_ref, col_ref, edge_ref, down,
    inner_ref, low_ref, high_ref, band_ref, fall_ref, strips_ref, odd_ref, slope_hbm, flow_hbm,
    slope, flow, sems,
):
    edge = row_ref.shape[1]
    rows = band_ref.shape[0]
    odd = lax.rem(lax.axis_index("gy"), 2)
    odd_ref[...] = jnp.full(odd_ref.shape, odd, jnp.int32)
    for s in range(2):
        band_ref[:, s * (W - 1) * edge : (s * (W - 1) + 1) * edge] = edge_ref[s].astype(BF16)


    def shifts(i):
        span = slice(i * edge, (i + 1) * edge)
        pieces = [edge_ref[0, span, :]]
        pieces += [inner_ref[j, span, :] for j in range(W - 2)] + [edge_ref[1, span, :]]
        lane = lax.broadcasted_iota(jnp.int32, pieces[0].shape, 1)
        lows = [pltpu.roll(piece, 1, 1) for piece in pieces]
        highs = [pltpu.roll(piece, 127, 1) for piece in pieces]
        for j in range(W):
            low_ref[j, span, :] = jnp.where(lane == 0, lows[j - 1], lows[j]) if j else lows[j]
            high_ref[j, span, :] = (
                jnp.where(lane == 127, highs[j + 1], highs[j]) if j < W - 1 else highs[j]
            )

    zero = jnp.minimum(source_ref[0, ZERO_AT], 0)

    def bounds(i):
        return max(i * edge - 16, PAD), (i + 1) * edge - 16

    def copies(i):
        start, stop = bounds(i)
        place = (pl.ds(start, stop - start), pl.ds(edge, (W - 2) * edge))
        span = slice(start - PAD, stop - PAD)
        return (
            pltpu.make_async_copy(slope.at[span], slope_hbm.at[place], sems.at[i, 0]),
            pltpu.make_async_copy(
                flow.at[:, span], flow_hbm.at[(slice(None),) + place], sems.at[i, 1]
            ),
        )

    def inner_cells(i):
        for at in range(*bounds(i), 16):
            for j in range(W - 2):
                def load(ref, j):
                    return lambda d: ref[j, pl.ds(at + (zero + d if d else 0), 16), :]

                value, parts = cells(load(inner_ref, j), load(low_ref, j + 1), load(high_ref, j + 1))
                place = (slice(at - PAD, at - PAD + 16), slice(j * edge, (j + 1) * edge))
                slope[place] = value
                for n, part in enumerate(parts):
                    flow[(n,) + place] = part
        for copy in copies(i):
            copy.start()

    fallen = 0
    for t in range(W + 1):
        while fallen < rows - 2 * PAD and fallen + STEP + 2 * PAD <= t * edge:
            value = dot(down[...], band_ref[fallen : fallen + STEP + 2 * PAD, :])
            fall_ref[fallen : fallen + STEP, :] = value.astype(BF16)
            fallen += STEP
        windows = [t * W + j for j in range(1, W - 1)] if t < W else []
        parts = first_products(windows, source_ref, arrived_ref, row_ref)
        if t >= 2 and t - 2 < EARLY:
            inner_cells(t - 2)
        if t:
            shifts(t - 1)
        values = [dot(part, col_ref[k]) for k, part in zip(windows, parts)]
        span = slice(t * edge, (t + 1) * edge)
        for j, value in enumerate(values):
            inner_ref[j, span, :] = value
            band_ref[span, (j + 1) * edge : (j + 2) * edge] = value.astype(BF16)
    for n in range(2):
        at = pl.multiple_of(jnp.where(odd == n, rows - PAD, 0), PAD)
        strips_ref[n] = band_ref[pl.ds(at, PAD), :]
    for i in range(EARLY):
        for copy in copies(i):
            copy.wait()


def middle(source, arrived, row_weights, col_weights, edge_values):
    edge = row_weights.shape[1]
    side = W * edge
    shapes = [
        ((W - 2, side, edge), F32),
        ((W, side, edge), F32),
        ((W, side, edge), F32),
        ((side, side), BF16),
        ((side - 2 * PAD, side), BF16),
        ((2, PAD, side), BF16),
        ((8, 128), jnp.int32),
    ]
    outs = out_shapes(side, side)[1:]
    return pl.pallas_call(
        middle_kernel,
        out_shape=[jax.ShapeDtypeStruct(s, d) for s, d in shapes] + outs,
        in_specs=[SMEM] + [VMEM] * 5,
        out_specs=[VMEM] * len(shapes) + [ANY] * len(outs),
        scratch_shapes=[
            pltpu.VMEM((EARLY_ROWS, (W - 2) * edge), F32),
            pltpu.VMEM((8, EARLY_ROWS, (W - 2) * edge), BF16),
            pltpu.SemaphoreType.DMA((EARLY, 2)),
        ],
        cost_estimate=cost(side * side),
        compiler_params=pltpu.CompilerParams(vmem_limit_bytes=32 * MIB),
        name="middle_windows",
    )(source, arrived, row_weights, col_weights, edge_values, down_taps(STEP))


def tap(offset):
    value = np.exp(-(offset * offset).astype(np.float32) / np.float32(2.0 * SIGMA * SIGMA))
    return np.where(np.abs(offset) <= RIM, value, 0.0).astype(ml_dtypes.bfloat16)


def tap_total():
    return float(np.sum(tap(np.arange(-RIM, RIM + 1)).astype(np.float64)))


def across_taps(wide, out):
    return jnp.asarray(tap(np.arange(wide)[:, None] - np.arange(out)[None, :] - 128))


def down_taps(step):
    return jnp.asarray(tap(np.arange(step + 2 * PAD)[None, :] - np.arange(step)[:, None] - PAD))


def cells(mid, low, high):
    centre, cl, cr = [load(0).astype(BF16) for load in (mid, low, high)]
    uc, ul, ur = [load(-1).astype(BF16) for load in (mid, low, high)]
    dc, dl, dr = [load(1).astype(BF16) for load in (mid, low, high)]
    one = dr - ul
    two = ur - dl
    across = cr - cl
    along = dc - uc
    grad_x = (one + two) + (across + across)
    grad_y = (one - two) + (along + along)
    steep = grad_x * grad_x + grad_y * grad_y
    square = BF16(1.0) + steep * BF16(1.0 / 64.0)
    slope = (square * lax.rsqrt(square)).astype(F32)
    flows = []
    for value, diagonal in (
        (ul, True), (uc, False), (ur, True), (cl, False),
        (cr, False), (dl, True), (dc, False), (dr, True),
    ):
        drop = jnp.maximum(centre - value, 0)
        flows.append((drop * BF16(DIAG) if diagonal else drop) + BF16(FLAT))
    total = (
        ((flows[0] + flows[1]) + (flows[2] + flows[3]))
        + ((flows[4] + flows[5]) + (flows[6] + flows[7]))
    )
    share = pl.reciprocal(total.astype(F32), approx=True).astype(BF16)
    return slope, [flow * share for flow in flows]


def sideways(centre, before, after):
    lane = lax.broadcasted_iota(jnp.int32, centre.shape, 1)
    low = jnp.where(lane == 0, pltpu.roll(before, 1, 1), pltpu.roll(centre, 1, 1))
    high = jnp.where(lane == 127, pltpu.roll(after, 127, 1), pltpu.roll(centre, 127, 1))
    return low, high


def dot(a, b):
    return jnp.dot(a, b, preferred_element_type=F32)


STEP = 176


def main_kernel(
    edge_ref, inner_ref, low_ref, high_ref, fall_ref, first_ref, second_ref, across, down,
    zero_ref, slope_in, flow_in, relief_hbm, slope_hbm, flow_hbm, relief, slope, flow, far, patched, sems, relief_sems,
):
    rows, cols = low_ref.shape[1], relief.shape[1]
    lanes = cols // 128
    steps = (rows - 2 * PAD) // STEP
    chunk = rows // 4
    inverse = 1.0 / (tap_total() ** 2)
    lane = lax.broadcasted_iota(jnp.int32, (chunk, 128), 1)
    left, right = before_and_after(first_ref[...], second_ref[...], "gx")
    for q in range(4):
        span = slice(q * chunk, (q + 1) * chunk)
        value = unpack_left(left, q)
        far[span, 0:128] = value.astype(BF16)
        patched[0, span, :] = jnp.where(lane == 0, pltpu.roll(value, 1, 1), low_ref[0, span, :])
        value = unpack_right(right, q)
        far[span, 128:256] = value.astype(BF16)
        patched[1, span, :] = jnp.where(
            lane == 127, pltpu.roll(value, 127, 1), high_ref[lanes - 1, span, :]
        )

    marks = (0, 96, 192, 288, 384, EARLY_ROWS, 544, 624, rows - 2 * PAD)
    pieces = tuple(zip(marks[:-1], marks[1:]))

    def copies(i):
        start, stop = pieces[i]
        span = slice(start, stop)
        place = pl.ds(PAD + start, stop - start)
        if start < EARLY_ROWS:
            columns = (pl.ds(0, 128), pl.ds(cols - 128, 128))
        else:
            columns = (pl.ds(0, cols),)
        found = []
        for n, column in enumerate(columns):
            found += [
                pltpu.make_async_copy(
                    slope.at[span, column], slope_hbm.at[place, column], sems.at[i, n, 0]
                ),
                pltpu.make_async_copy(
                    flow.at[:, span, column], flow_hbm.at[:, place, column], sems.at[i, n, 1]
                ),
            ]
        return found

    def relief_copy(j):
        column = pl.ds(j * 256, 256)
        return pltpu.make_async_copy(
            relief.at[:, column], relief_hbm.at[pl.ds(PAD, rows - 2 * PAD), column], relief_sems.at[j]
        )

    def mid(j, span):
        if j in (0, lanes - 1):
            return edge_ref[int(j > 0), span, :]
        return inner_ref[j - 1, span, :]

    def low(j, span):
        return low_ref[j, span, :] if j else patched[0, span, :]

    def high(j, span):
        return high_ref[j, span, :] if j < lanes - 1 else patched[1, span, :]

    def smooth(j):
        at = j * 256
        if j == 0:
            wide = jnp.concatenate([sides[:, 0:128], fall_ref[:, 0:384]], axis=1)
        elif j == lanes // 2 - 1:
            wide = jnp.concatenate([fall_ref[:, at - 128 :], sides[:, 128:256]], axis=1)
        else:
            wide = fall_ref[:, at - 128 : at + 384]
        return dot(wide, across[...])

    def relieve(j, value):
        at = j * 256
        for h in range(2):
            centre = mid(j * 2 + h, slice(PAD, rows - PAD))
            relief[:, at + h * 128 : at + h * 128 + 128] = (
                centre - value[:, h * 128 : h * 128 + 128] * inverse
            )
        relief_copy(j).start()

    zero = jnp.minimum(zero_ref[0, ZERO_AT], 0)
    sides = jnp.concatenate(
        [dot(down[...], far[i * STEP : (i + 1) * STEP + 2 * PAD, :]).astype(BF16) for i in range(steps)],
        axis=0,
    )
    piece = 0
    for q in range((rows - 2 * PAD) // 16):
        at = q * 16
        if q % 8 == 0:
            if q and q // 8 <= lanes // 2:
                relieve(q // 8 - 1, smoothed)
            if q // 8 < lanes // 2:
                smoothed = smooth(q // 8)
        for j in range(lanes) if at >= EARLY_ROWS else (0, lanes - 1):
            def load(piece):
                return lambda d: piece(j, pl.ds(at + PAD + (zero + d if d else 0), 16))

            value, parts = cells(load(mid), load(low), load(high))
            place = (slice(at, at + 16), slice(j * 128, (j + 1) * 128))
            slope[place] = value
            for n, part in enumerate(parts):
                flow[(n,) + place] = part
        if at + 16 == pieces[piece][1]:
            for copy in copies(piece):
                copy.start()
            piece += 1
    for j in range(lanes // 2):
        relief_copy(j).wait()
    for i in range(len(pieces)):
        for copy in copies(i):
            copy.wait()


def main(edge_values, inner, low, high, fall, left, right, source, slope, flow):
    lanes, rows, _ = low.shape
    cols = lanes * 128
    tall = rows - 2 * PAD
    return pl.pallas_call(
        main_kernel,
        out_shape=out_shapes(rows, cols),
        in_specs=[VMEM] * 9 + [SMEM] + [ANY] * 2,
        out_specs=[ANY] * 3,
        input_output_aliases={10: 1, 11: 2},
        scratch_shapes=[
            pltpu.VMEM((tall, cols), F32),
            pltpu.VMEM((tall, cols), F32),
            pltpu.VMEM((8, tall, cols), BF16),
            pltpu.VMEM((rows, 256), BF16),
            pltpu.VMEM((2, rows, 128), F32),
            pltpu.SemaphoreType.DMA((8, 2, 2)),
            pltpu.SemaphoreType.DMA((cols // 256,)),
        ],
        cost_estimate=cost(tall * cols),
        compiler_params=pltpu.CompilerParams(vmem_limit_bytes=32 * MIB),
        name="main_cells",
    )(
        edge_values, inner, low, high, fall, left, right,
        across_taps(512, 256), down_taps(STEP), source, slope, flow,
    )


def out_shapes(rows, cols):
    return [
        jax.ShapeDtypeStruct((rows, cols), F32),
        jax.ShapeDtypeStruct((rows, cols), F32),
        jax.ShapeDtypeStruct((8, rows, cols), BF16),
    ]


def cost(cells_done):
    return pl.CostEstimate(
        flops=cells_done * 4000, bytes_accessed=cells_done * 24, transcendentals=cells_done * 2
    )


def unpack_left(value, q):
    return value if q == 3 else pltpu.roll(value, 96 - PAD * q, 1)


def unpack_right(value, q):
    return value if q == 0 else pltpu.roll(value, 128 - PAD * q, 1)


def ends_kernel(
    edge_ref, inner_ref, band_ref, first_ref, second_ref, near_ref, next_ref, across, down,
    relief_in, slope_in, flow_in, relief_hbm, slope_hbm, flow_hbm,
    relief, slope, flow, wide, band, low_ref, high_ref, sems,
):
    rows, cols = band_ref.shape
    lanes = cols // 128
    near = 2 * PAD
    tall = PAD + 16
    inverse = 1.0 / (tap_total() ** 2)
    packed = first_ref.shape[0]
    others = before_and_after(near_ref[...], next_ref[...], "gy")
    for e in range(2):
        here = slice(PAD, PAD + near) if e == 0 else slice(0, near)
        there = slice(0, PAD) if e == 0 else slice(near, near + PAD)
        other = others[e]
        top = e * tall
        own_rows = slice(rows - near, rows) if e else slice(0, near)
        pack_rows = slice(packed - near, packed) if e else slice(0, near)
        band[e, here, 128 : 128 + cols] = band_ref[own_rows, :]
        band[e, there, 128 : 128 + cols] = other[:, 0:cols].astype(BF16)
        left, right = before_and_after(first_ref[pack_rows, :], second_ref[pack_rows, :], "gx")
        far_left = unpack_left(left, 3 * e)
        far_right = unpack_right(right, 3 * e)
        left, right = before_and_after(
            other[:, cols : cols + 128], other[:, cols + 128 : cols + 256], "gx"
        )
        corner_left = unpack_left(left, 0 if e else 3)
        corner_right = unpack_right(right, 0 if e else 3)
        band[e, here, 0:128] = far_left.astype(BF16)
        band[e, there, 0:128] = corner_left.astype(BF16)
        band[e, here, 128 + cols :] = far_right.astype(BF16)
        band[e, there, 128 + cols :] = corner_right.astype(BF16)
        if e == 0:
            wide[0, top : top + 8, :] = corner_left[PAD - 8 : PAD]
            wide[0, top + 8 : top + 48, :] = far_left[0:40]
            wide[lanes + 1, top : top + 8, :] = corner_right[PAD - 8 : PAD]
            wide[lanes + 1, top + 8 : top + 48, :] = far_right[0:40]
        else:
            wide[0, top : top + 40, :] = far_left[near - 40 : near]
            wide[0, top + 40 : top + 48, :] = corner_left[0:8]
            wide[lanes + 1, top : top + 40, :] = far_right[near - 40 : near]
            wide[lanes + 1, top + 40 : top + 48, :] = corner_right[0:8]
        for j in range(lanes):
            part = other[:, j * 128 : (j + 1) * 128]
            own = edge_ref.at[int(j > 0)] if j in (0, lanes - 1) else inner_ref.at[j - 1]
            if e == 0:
                wide[j + 1, top : top + 8, :] = part[PAD - 8 : PAD]
                wide[j + 1, top + 8 : top + 48, :] = own[0:40, :]
            else:
                wide[j + 1, top : top + 40, :] = own[rows - 40 : rows, :]
                wide[j + 1, top + 40 : top + 48, :] = part[0:8]

    smooth = jnp.concatenate([dot(down[...], band[e]).astype(BF16) for e in range(2)], axis=0)
    for j in range(lanes // 2):
        value = dot(smooth[:, j * 256 : j * 256 + 512], across[...])
        for e in range(2):
            for h in range(2):
                at = j * 256 + h * 128
                centre = wide[j * 2 + h + 1, e * tall + 8 : e * tall + 8 + PAD, :]
                part = value[e * PAD : (e + 1) * PAD, h * 128 : h * 128 + 128]
                relief[e, :, at : at + 128] = centre - part * inverse
    for j in range(lanes):
        low, high = sideways(wide[j + 1], wide[j], wide[j + 2])
        low_ref[j] = low
        high_ref[j] = high

    def one_end(e, carry):
        for at in range(0, PAD, 16):
            top = pl.multiple_of(e * tall + 8 + at, 8)
            for j in range(lanes):
                value, parts = cells(
                    lambda d: wide[j + 1, pl.ds(top + d, 16), :],
                    lambda d: low_ref[j, pl.ds(top + d, 16), :],
                    lambda d: high_ref[j, pl.ds(top + d, 16), :],
                )
                place = (slice(at, at + 16), slice(j * 128, (j + 1) * 128))
                slope[(e,) + place] = value
                for n, part in enumerate(parts):
                    flow[(e, n) + place] = part
        place = pl.ds(pl.multiple_of(e * (rows - PAD), PAD), PAD)
        pltpu.make_async_copy(relief.at[e], relief_hbm.at[place], sems.at[e, 0]).start()
        pltpu.make_async_copy(slope.at[e], slope_hbm.at[place], sems.at[e, 1]).start()
        pltpu.make_async_copy(flow.at[e], flow_hbm.at[:, place], sems.at[e, 2]).start()
        return carry

    lax.fori_loop(0, 2, one_end, 0)
    for e in range(2):
        place = pl.ds(e * (rows - PAD), PAD)
        pltpu.make_async_copy(relief.at[e], relief_hbm.at[place], sems.at[e, 0]).wait()
        pltpu.make_async_copy(slope.at[e], slope_hbm.at[place], sems.at[e, 1]).wait()
        pltpu.make_async_copy(flow.at[e], flow_hbm.at[:, place], sems.at[e, 2]).wait()


def ends(edge_values, inner, band, left, right, up, down, outs):
    rows, cols = band.shape
    lanes = cols // 128
    return pl.pallas_call(
        ends_kernel,
        out_shape=out_shapes(rows, cols),
        in_specs=[VMEM] * 9 + [ANY] * 3,
        out_specs=[ANY] * 3,
        input_output_aliases={9: 0, 10: 1, 11: 2},
        scratch_shapes=[
            pltpu.VMEM((2, PAD, cols), F32),
            pltpu.VMEM((2, PAD, cols), F32),
            pltpu.VMEM((2, 8, PAD, cols), BF16),
            pltpu.VMEM((lanes + 2, 2 * (PAD + 16), 128), F32),
            pltpu.VMEM((2, 3 * PAD, cols + 256), BF16),
            pltpu.VMEM((lanes, 2 * (PAD + 16), 128), F32),
            pltpu.VMEM((lanes, 2 * (PAD + 16), 128), F32),
            pltpu.SemaphoreType.DMA((2, 3)),
        ],
        cost_estimate=cost(2 * PAD * cols),
        compiler_params=pltpu.CompilerParams(vmem_limit_bytes=16 * MIB),
        name="end_cells",
    )(
        edge_values, inner, band, left, right, up, down,
        across_taps(512, 256), down_taps(PAD), *outs,
    )


def swap(first, second, axis):
    devices = lax.axis_size(axis)
    received = []
    for start, value in enumerate((first, second)):
        pairs = [(i, i + 1) for i in range(start, devices - 1, 2)]
        received.append(lax.ppermute(value, axis, pairs + [(j, i) for i, j in pairs]))
    return received


def local(source_blocks, block_scale, block_list, block_count, row_weights, col_weights):
    block_list = block_list.T
    outgoing, source = gather(block_list, block_count, block_scale, source_blocks)
    edge = source_blocks.shape[1]
    arrived = lax.all_to_all(outgoing, "gy", split_axis=0, concat_axis=0, tiled=True)
    arrived = arrived.reshape(-1, edge, edge)
    weights = (row_weights, col_weights)
    edge_values, *messages = edges(source, arrived, *weights)
    beside = swap(*messages, "gx")
    inner, low, high, band, fall, strips, odd, *outs = middle(
        source, arrived, *weights, edge_values
    )
    messages = []
    for n in range(2):
        corners = [jnp.where(odd[:1] == n, side[-PAD:], side[:PAD]) for side in beside]
        messages.append(jnp.concatenate([strips[n], *corners], axis=1))
    ahead = swap(*messages, "gy")
    outs = main(edge_values, inner, low, high, fall, *beside, source, *outs)
    return tuple(ends(edge_values, inner, band, *beside, *ahead, outs))


def solution(mesh):
    in_specs = (
        P(("gx", "gy"), None, None),
        P(("gx", "gy")),
        P(),
        P(),
        P(("gx", "gy"), None, None),
        P(("gx", "gy"), None, None),
    )
    out_specs = (P("gy", "gx"), P("gy", "gx"), P(None, "gy", "gx"))
    return jax.shard_map(local, mesh=mesh, in_specs=in_specs, out_specs=out_specs, check_vma=False)
```

```python
import jax
import jax.numpy as jnp
import ml_dtypes
import numpy as np
from jax import lax
from jax.experimental import pallas as pl
from jax.experimental.pallas import tpu as pltpu
from jax.sharding import PartitionSpec as P

W = 6
CAP = 4
RIM = 24
PAD = 32
SIGMA = 10.0
FLAT = 0.05
DIAG = 0.5**0.5
F32 = jnp.float32
BF16 = jnp.bfloat16
MIB = 1 << 20
ZERO_AT = W * W

SMEM = pl.BlockSpec(memory_space=pltpu.SMEM)
VMEM = pl.BlockSpec(memory_space=pltpu.VMEM)
ANY = pl.BlockSpec(memory_space=pl.ANY)


def gather_kernel(
    list_hbm, count_hbm, scale_hbm, blocks_hbm, out_hbm, source_hbm,
    listed, counted, scale, blocks, found, table, staged,
    named, numbered, seen, source, sems, out_sems,
):
    holders = lax.axis_size("gy")
    first = lax.axis_index("gx") * holders
    held = blocks.shape[0]
    base = (first + lax.axis_index("gy")) * held
    slots = listed.shape[0]
    copies = [
        pltpu.make_async_copy(list_hbm, listed, sems.at[0]),
        pltpu.make_async_copy(count_hbm, counted, sems.at[1]),
        pltpu.make_async_copy(scale_hbm, scale, sems.at[2]),
        pltpu.make_async_copy(blocks_hbm, blocks, sems.at[3]),
        pltpu.make_async_copy(list_hbm, named, sems.at[5]),
        pltpu.make_async_copy(count_hbm, numbered, sems.at[6]),
    ]
    for copy in copies:
        copy.start()
    copies[0].wait()
    copies[1].wait()
    shape = found.shape
    row = lax.broadcasted_iota(jnp.int32, shape, 0)
    live = jnp.broadcast_to(counted[...], shape)
    rank = jnp.zeros(shape, jnp.int32)
    chosen = jnp.zeros(shape, jnp.int32)
    for k in range(slots):
        block = jnp.broadcast_to(listed[k : k + 1, :], shape) - base
        hit = (block >= 0) & (block < held) & (k < live)
        chosen = jnp.where(hit & (rank == row), block, chosen)
        rank = rank + hit.astype(jnp.int32)
    found[...] = jnp.where(row < CAP, chosen, rank)
    handed = pltpu.make_async_copy(found, table, sems.at[4])
    handed.start()
    copies[4].wait()
    copies[5].wait()
    tile = first + lax.axis_index("gy")
    count = numbered[0, tile]
    for h in range(out_hbm.shape[0]):
        seen[h] = 0
    for k in range(slots):
        block = jnp.clip(named[k, tile] - first * held, 0, out_hbm.shape[0] * held - 1)
        owner = lax.shift_right_logical(block, jnp.int32(held.bit_length() - 1))
        rank = seen[owner]
        source[0, k] = owner * CAP + jnp.minimum(rank, CAP - 1)
        seen[owner] = rank + (k < count).astype(jnp.int32)
    source[0, slots] = count
    told = pltpu.make_async_copy(source, source_hbm, sems.at[7])
    told.start()
    handed.wait()
    copies[2].wait()
    copies[3].wait()

    def one_tile(t, carry):
        @pl.when(table[CAP, first + t] > 0)
        def fill():
            for j in range(CAP):
                block = table[j, first + t]
                value = blocks[block].astype(F32) * scale[block]
                staged[t, j] = value.astype(BF16)
            pltpu.make_async_copy(staged.at[t], out_hbm.at[t], out_sems.at[t]).start()

        return carry

    lax.fori_loop(0, holders, one_tile, 0)

    def one_wait(t, carry):
        @pl.when(table[CAP, first + t] > 0)
        def drain():
            pltpu.make_async_copy(staged.at[t], out_hbm.at[t], out_sems.at[t]).wait()

        return carry

    lax.fori_loop(0, holders, one_wait, 0)
    told.wait()


def gather(block_list, block_count, block_scale, source_blocks):
    held, edge, _ = source_blocks.shape
    holders = lax.axis_size("gy")
    slots, tiles = block_list.shape
    return pl.pallas_call(
        gather_kernel,
        out_shape=[
            jax.ShapeDtypeStruct((holders, CAP, edge, edge), BF16),
            jax.ShapeDtypeStruct((1, tiles), jnp.int32),
        ],
        in_specs=[ANY] * 4,
        out_specs=[ANY] * 2,
        scratch_shapes=[
            pltpu.VMEM((slots, tiles), jnp.int32),
            pltpu.VMEM((1, tiles), jnp.int32),
            pltpu.SMEM((held,), F32),
            pltpu.VMEM((held, edge, edge), BF16),
            pltpu.VMEM((8, tiles), jnp.int32),
            pltpu.SMEM((8, tiles), jnp.int32),
            pltpu.VMEM((holders, CAP, edge, edge), BF16),
            pltpu.SMEM((slots, tiles), jnp.int32),
            pltpu.SMEM((1, tiles), jnp.int32),
            pltpu.SMEM((holders,), jnp.int32),
            pltpu.SMEM((1, tiles), jnp.int32),
            pltpu.SemaphoreType.DMA((8,)),
            pltpu.SemaphoreType.DMA((holders,)),
        ],
        compiler_params=pltpu.CompilerParams(vmem_limit_bytes=56 * MIB),
        name="gather_blocks",
    )(block_list, block_count.reshape(1, tiles), block_scale, source_blocks)


def is_even(axis):
    return lax.rem(lax.axis_index(axis), 2) == 0


def before_and_after(first, second, axis):
    even = is_even(axis)
    first, second = first.astype(F32), second.astype(F32)
    return jnp.where(even, second, first), jnp.where(even, first, second)


def first_products(windows, source_ref, arrived_ref, row_ref):
    live = source_ref[0, row_ref.shape[0]]
    values = [dot(row_ref[k], arrived_ref[source_ref[0, k]]) for k in windows]
    return [jnp.where(k < live, value, 0.0).astype(BF16) for k, value in zip(windows, values)]


def edges_kernel(
    source_ref, arrived_ref, row_ref, col_ref, edge_ref, first_ref, second_ref
):
    edge = row_ref.shape[1]
    for s in range(2):
        windows = [i * W + s * (W - 1) for i in range(W)]
        parts = first_products(windows, source_ref, arrived_ref, row_ref)
        values = [dot(part, col_ref[k]) for k, part in zip(windows, parts)]
        for i, value in enumerate(values):
            edge_ref[s, i * edge : (i + 1) * edge, :] = value
    rows = edge_ref.shape[1]
    chunk = rows // 4
    lane = lax.broadcasted_iota(jnp.int32, (chunk, 128), 1)
    left = jnp.zeros((chunk, 128), F32)
    right = jnp.zeros((chunk, 128), F32)
    for q in range(4):
        mine = (lane >= PAD * q) & (lane < PAD * (q + 1))
        part = edge_ref[0, q * chunk : (q + 1) * chunk, :]
        if q:
            part = pltpu.roll(part, PAD * q, 1)
        left = jnp.where(mine, part, left)
        part = edge_ref[1, q * chunk : (q + 1) * chunk, :]
        if q != 3:
            part = pltpu.roll(part, PAD * (q + 1), 1)
        right = jnp.where(mine, part, right)
    even = is_even("gx")
    first_ref[...] = jnp.where(even, right, left).astype(BF16)
    second_ref[...] = jnp.where(even, left, right).astype(BF16)


def edges(source, arrived, row_weights, col_weights):
    edge = row_weights.shape[1]
    side = W * edge
    shapes = [((2, side, edge), F32), ((side // 4, 128), BF16), ((side // 4, 128), BF16)]
    return pl.pallas_call(
        edges_kernel,
        out_shape=[jax.ShapeDtypeStruct(s, d) for s, d in shapes],
        in_specs=[SMEM, VMEM, VMEM, VMEM],
        out_specs=[VMEM] * len(shapes),
        cost_estimate=cost(side * 256),
        compiler_params=pltpu.CompilerParams(vmem_limit_bytes=16 * MIB),
        name="edge_windows",
    )(source, arrived, row_weights, col_weights)


def middle_kernel(
    source_ref, arrived_ref, row_ref, col_ref, edge_ref, down,
    inner_ref, low_ref, high_ref, band_ref, fall_ref, strips_ref, odd_ref,
):
    edge = row_ref.shape[1]
    rows = band_ref.shape[0]
    odd = lax.rem(lax.axis_index("gy"), 2)
    odd_ref[...] = jnp.full(odd_ref.shape, odd, jnp.int32)
    for s in range(2):
        band_ref[:, s * (W - 1) * edge : (s * (W - 1) + 1) * edge] = edge_ref[s].astype(BF16)


    def shifts(i):
        span = slice(i * edge, (i + 1) * edge)
        pieces = [edge_ref[0, span, :]]
        pieces += [inner_ref[j, span, :] for j in range(W - 2)] + [edge_ref[1, span, :]]
        lane = lax.broadcasted_iota(jnp.int32, pieces[0].shape, 1)
        lows = [pltpu.roll(piece, 1, 1) for piece in pieces]
        highs = [pltpu.roll(piece, 127, 1) for piece in pieces]
        for j in range(W):
            low_ref[j, span, :] = jnp.where(lane == 0, lows[j - 1], lows[j]) if j else lows[j]
            high_ref[j, span, :] = (
                jnp.where(lane == 127, highs[j + 1], highs[j]) if j < W - 1 else highs[j]
            )

    fallen = 0
    for t in range(W + 1):
        while fallen < rows - 2 * PAD and fallen + STEP + 2 * PAD <= t * edge:
            value = dot(down[...], band_ref[fallen : fallen + STEP + 2 * PAD, :])
            fall_ref[fallen : fallen + STEP, :] = value.astype(BF16)
            fallen += STEP
        windows = [t * W + j for j in range(1, W - 1)] if t < W else []
        parts = first_products(windows, source_ref, arrived_ref, row_ref)
        if t:
            shifts(t - 1)
        values = [dot(part, col_ref[k]) for k, part in zip(windows, parts)]
        span = slice(t * edge, (t + 1) * edge)
        for j, value in enumerate(values):
            inner_ref[j, span, :] = value
            band_ref[span, (j + 1) * edge : (j + 2) * edge] = value.astype(BF16)
    for n in range(2):
        at = pl.multiple_of(jnp.where(odd == n, rows - PAD, 0), PAD)
        strips_ref[n] = band_ref[pl.ds(at, PAD), :]


def middle(source, arrived, row_weights, col_weights, edge_values):
    edge = row_weights.shape[1]
    side = W * edge
    shapes = [
        ((W - 2, side, edge), F32),
        ((W, side, edge), F32),
        ((W, side, edge), F32),
        ((side, side), BF16),
        ((side - 2 * PAD, side), BF16),
        ((2, PAD, side), BF16),
        ((8, 128), jnp.int32),
    ]
    return pl.pallas_call(
        middle_kernel,
        out_shape=[jax.ShapeDtypeStruct(s, d) for s, d in shapes],
        in_specs=[SMEM] + [VMEM] * 5,
        out_specs=[VMEM] * len(shapes),
        cost_estimate=cost(side * side),
        compiler_params=pltpu.CompilerParams(vmem_limit_bytes=24 * MIB),
        name="middle_windows",
    )(source, arrived, row_weights, col_weights, edge_values, down_taps(STEP))


def tap(offset):
    value = np.exp(-(offset * offset).astype(np.float32) / np.float32(2.0 * SIGMA * SIGMA))
    return np.where(np.abs(offset) <= RIM, value, 0.0).astype(ml_dtypes.bfloat16)


def tap_total():
    return float(np.sum(tap(np.arange(-RIM, RIM + 1)).astype(np.float64)))


def across_taps(wide, out):
    return jnp.asarray(tap(np.arange(wide)[:, None] - np.arange(out)[None, :] - 128))


def down_taps(step):
    return jnp.asarray(tap(np.arange(step + 2 * PAD)[None, :] - np.arange(step)[:, None] - PAD))


def cells(mid, low, high):
    centre, cl, cr = [load(0).astype(BF16) for load in (mid, low, high)]
    uc, ul, ur = [load(-1).astype(BF16) for load in (mid, low, high)]
    dc, dl, dr = [load(1).astype(BF16) for load in (mid, low, high)]
    one = dr - ul
    two = ur - dl
    across = cr - cl
    along = dc - uc
    grad_x = (one + two) + (across + across)
    grad_y = (one - two) + (along + along)
    steep = grad_x * grad_x + grad_y * grad_y
    square = BF16(1.0) + steep * BF16(1.0 / 64.0)
    slope = (square * lax.rsqrt(square)).astype(F32)
    flows = []
    for value, diagonal in (
        (ul, True), (uc, False), (ur, True), (cl, False),
        (cr, False), (dl, True), (dc, False), (dr, True),
    ):
        drop = jnp.maximum(centre - value, 0)
        flows.append((drop * BF16(DIAG) if diagonal else drop) + BF16(FLAT))
    total = (
        ((flows[0] + flows[1]) + (flows[2] + flows[3]))
        + ((flows[4] + flows[5]) + (flows[6] + flows[7]))
    )
    share = pl.reciprocal(total.astype(F32), approx=True).astype(BF16)
    return slope, [flow * share for flow in flows]


def sideways(centre, before, after):
    lane = lax.broadcasted_iota(jnp.int32, centre.shape, 1)
    low = jnp.where(lane == 0, pltpu.roll(before, 1, 1), pltpu.roll(centre, 1, 1))
    high = jnp.where(lane == 127, pltpu.roll(after, 127, 1), pltpu.roll(centre, 127, 1))
    return low, high


def dot(a, b):
    return jnp.dot(a, b, preferred_element_type=F32)


STEP = 176


def main_kernel(
    edge_ref, inner_ref, low_ref, high_ref, fall_ref, first_ref, second_ref, across, down,
    zero_ref, relief_hbm, slope_hbm, flow_hbm, relief, slope, flow, far, patched, sems, relief_sems,
):
    rows, cols = low_ref.shape[1], relief.shape[1]
    lanes = cols // 128
    steps = (rows - 2 * PAD) // STEP
    chunk = rows // 4
    inverse = 1.0 / (tap_total() ** 2)
    lane = lax.broadcasted_iota(jnp.int32, (chunk, 128), 1)
    left, right = before_and_after(first_ref[...], second_ref[...], "gx")
    for q in range(4):
        span = slice(q * chunk, (q + 1) * chunk)
        value = unpack_left(left, q)
        far[span, 0:128] = value.astype(BF16)
        patched[0, span, :] = jnp.where(lane == 0, pltpu.roll(value, 1, 1), low_ref[0, span, :])
        value = unpack_right(right, q)
        far[span, 128:256] = value.astype(BF16)
        patched[1, span, :] = jnp.where(
            lane == 127, pltpu.roll(value, 127, 1), high_ref[lanes - 1, span, :]
        )

    marks = (0, 48, 112, 208, 304, 400, 496, 576, 640, 688, rows - 2 * PAD)
    pieces = tuple(zip(marks[:-1], marks[1:]))

    def copies(i):
        start, stop = pieces[i]
        span = slice(start, stop)
        place = pl.ds(PAD + start, stop - start)
        return (
            pltpu.make_async_copy(slope.at[span], slope_hbm.at[place], sems.at[i, 0]),
            pltpu.make_async_copy(flow.at[:, span], flow_hbm.at[:, place], sems.at[i, 1]),
        )

    def relief_copy(j):
        column = pl.ds(j * 256, 256)
        return pltpu.make_async_copy(
            relief.at[:, column], relief_hbm.at[pl.ds(PAD, rows - 2 * PAD), column], relief_sems.at[j]
        )

    def mid(j, span):
        if j in (0, lanes - 1):
            return edge_ref[int(j > 0), span, :]
        return inner_ref[j - 1, span, :]

    def low(j, span):
        return low_ref[j, span, :] if j else patched[0, span, :]

    def high(j, span):
        return high_ref[j, span, :] if j < lanes - 1 else patched[1, span, :]

    def smooth(j):
        at = j * 256
        if j == 0:
            wide = jnp.concatenate([sides[:, 0:128], fall_ref[:, 0:384]], axis=1)
        elif j == lanes // 2 - 1:
            wide = jnp.concatenate([fall_ref[:, at - 128 :], sides[:, 128:256]], axis=1)
        else:
            wide = fall_ref[:, at - 128 : at + 384]
        return dot(wide, across[...])

    def relieve(j, value):
        at = j * 256
        for h in range(2):
            centre = mid(j * 2 + h, slice(PAD, rows - PAD))
            relief[:, at + h * 128 : at + h * 128 + 128] = (
                centre - value[:, h * 128 : h * 128 + 128] * inverse
            )
        relief_copy(j).start()

    zero = jnp.minimum(zero_ref[0, ZERO_AT], 0)
    piece = 0
    for q in range((rows - 2 * PAD) // 16):
        at = q * 16
        if q == 3:
            sides = jnp.concatenate(
                [dot(down[...], far[i * STEP : (i + 1) * STEP + 2 * PAD, :]).astype(BF16) for i in range(steps)],
                axis=0,
            )
        if q in (3, 13, 23):
            smoothed = smooth(q // 10)
        if q in (8, 18, 28):
            relieve(q // 10, smoothed)
        for j in range(lanes):
            def load(piece):
                return lambda d: piece(j, pl.ds(at + PAD + (zero + d if d else 0), 16))

            value, parts = cells(load(mid), load(low), load(high))
            place = (slice(at, at + 16), slice(j * 128, (j + 1) * 128))
            slope[place] = value
            for n, part in enumerate(parts):
                flow[(n,) + place] = part
        if at + 16 == pieces[piece][1]:
            for copy in copies(piece):
                copy.start()
            piece += 1
    for j in range(lanes // 2):
        relief_copy(j).wait()
    for i in range(len(pieces)):
        for copy in copies(i):
            copy.wait()


def main(edge_values, inner, low, high, fall, left, right, source):
    lanes, rows, _ = low.shape
    cols = lanes * 128
    tall = rows - 2 * PAD
    return pl.pallas_call(
        main_kernel,
        out_shape=out_shapes(rows, cols),
        in_specs=[VMEM] * 9 + [SMEM],
        out_specs=[ANY] * 3,
        scratch_shapes=[
            pltpu.VMEM((tall, cols), F32),
            pltpu.VMEM((tall, cols), F32),
            pltpu.VMEM((8, tall, cols), BF16),
            pltpu.VMEM((rows, 256), BF16),
            pltpu.VMEM((2, rows, 128), F32),
            pltpu.SemaphoreType.DMA((10, 2)),
            pltpu.SemaphoreType.DMA((cols // 256,)),
        ],
        cost_estimate=cost(tall * cols),
        compiler_params=pltpu.CompilerParams(vmem_limit_bytes=32 * MIB),
        name="main_cells",
    )(
        edge_values, inner, low, high, fall, left, right,
        across_taps(512, 256), down_taps(STEP), source,
    )


def out_shapes(rows, cols):
    return [
        jax.ShapeDtypeStruct((rows, cols), F32),
        jax.ShapeDtypeStruct((rows, cols), F32),
        jax.ShapeDtypeStruct((8, rows, cols), BF16),
    ]


def cost(cells_done):
    return pl.CostEstimate(
        flops=cells_done * 4000, bytes_accessed=cells_done * 24, transcendentals=cells_done * 2
    )


def unpack_left(value, q):
    return value if q == 3 else pltpu.roll(value, 96 - PAD * q, 1)


def unpack_right(value, q):
    return value if q == 0 else pltpu.roll(value, 128 - PAD * q, 1)


def ends_kernel(
    edge_ref, inner_ref, band_ref, first_ref, second_ref, near_ref, next_ref, across, down,
    relief_in, slope_in, flow_in, relief_hbm, slope_hbm, flow_hbm,
    relief, slope, flow, wide, band, low_ref, high_ref, sems,
):
    rows, cols = band_ref.shape
    lanes = cols // 128
    near = 2 * PAD
    tall = PAD + 16
    inverse = 1.0 / (tap_total() ** 2)
    packed = first_ref.shape[0]
    others = before_and_after(near_ref[...], next_ref[...], "gy")
    for e in range(2):
        here = slice(PAD, PAD + near) if e == 0 else slice(0, near)
        there = slice(0, PAD) if e == 0 else slice(near, near + PAD)
        other = others[e]
        top = e * tall
        own_rows = slice(rows - near, rows) if e else slice(0, near)
        pack_rows = slice(packed - near, packed) if e else slice(0, near)
        band[e, here, 128 : 128 + cols] = band_ref[own_rows, :]
        band[e, there, 128 : 128 + cols] = other[:, 0:cols].astype(BF16)
        left, right = before_and_after(first_ref[pack_rows, :], second_ref[pack_rows, :], "gx")
        far_left = unpack_left(left, 3 * e)
        far_right = unpack_right(right, 3 * e)
        left, right = before_and_after(
            other[:, cols : cols + 128], other[:, cols + 128 : cols + 256], "gx"
        )
        corner_left = unpack_left(left, 0 if e else 3)
        corner_right = unpack_right(right, 0 if e else 3)
        band[e, here, 0:128] = far_left.astype(BF16)
        band[e, there, 0:128] = corner_left.astype(BF16)
        band[e, here, 128 + cols :] = far_right.astype(BF16)
        band[e, there, 128 + cols :] = corner_right.astype(BF16)
        if e == 0:
            wide[0, top : top + 8, :] = corner_left[PAD - 8 : PAD]
            wide[0, top + 8 : top + 48, :] = far_left[0:40]
            wide[lanes + 1, top : top + 8, :] = corner_right[PAD - 8 : PAD]
            wide[lanes + 1, top + 8 : top + 48, :] = far_right[0:40]
        else:
            wide[0, top : top + 40, :] = far_left[near - 40 : near]
            wide[0, top + 40 : top + 48, :] = corner_left[0:8]
            wide[lanes + 1, top : top + 40, :] = far_right[near - 40 : near]
            wide[lanes + 1, top + 40 : top + 48, :] = corner_right[0:8]
        for j in range(lanes):
            part = other[:, j * 128 : (j + 1) * 128]
            own = edge_ref.at[int(j > 0)] if j in (0, lanes - 1) else inner_ref.at[j - 1]
            if e == 0:
                wide[j + 1, top : top + 8, :] = part[PAD - 8 : PAD]
                wide[j + 1, top + 8 : top + 48, :] = own[0:40, :]
            else:
                wide[j + 1, top : top + 40, :] = own[rows - 40 : rows, :]
                wide[j + 1, top + 40 : top + 48, :] = part[0:8]

    smooth = jnp.concatenate([dot(down[...], band[e]).astype(BF16) for e in range(2)], axis=0)
    for j in range(lanes // 2):
        value = dot(smooth[:, j * 256 : j * 256 + 512], across[...])
        for e in range(2):
            for h in range(2):
                at = j * 256 + h * 128
                centre = wide[j * 2 + h + 1, e * tall + 8 : e * tall + 8 + PAD, :]
                part = value[e * PAD : (e + 1) * PAD, h * 128 : h * 128 + 128]
                relief[e, :, at : at + 128] = centre - part * inverse
    for j in range(lanes):
        low, high = sideways(wide[j + 1], wide[j], wide[j + 2])
        low_ref[j] = low
        high_ref[j] = high

    def one_end(e, carry):
        for at in range(0, PAD, 16):
            top = pl.multiple_of(e * tall + 8 + at, 8)
            for j in range(lanes):
                value, parts = cells(
                    lambda d: wide[j + 1, pl.ds(top + d, 16), :],
                    lambda d: low_ref[j, pl.ds(top + d, 16), :],
                    lambda d: high_ref[j, pl.ds(top + d, 16), :],
                )
                place = (slice(at, at + 16), slice(j * 128, (j + 1) * 128))
                slope[(e,) + place] = value
                for n, part in enumerate(parts):
                    flow[(e, n) + place] = part
        place = pl.ds(pl.multiple_of(e * (rows - PAD), PAD), PAD)
        pltpu.make_async_copy(relief.at[e], relief_hbm.at[place], sems.at[e, 0]).start()
        pltpu.make_async_copy(slope.at[e], slope_hbm.at[place], sems.at[e, 1]).start()
        pltpu.make_async_copy(flow.at[e], flow_hbm.at[:, place], sems.at[e, 2]).start()
        return carry

    lax.fori_loop(0, 2, one_end, 0)
    for e in range(2):
        place = pl.ds(e * (rows - PAD), PAD)
        pltpu.make_async_copy(relief.at[e], relief_hbm.at[place], sems.at[e, 0]).wait()
        pltpu.make_async_copy(slope.at[e], slope_hbm.at[place], sems.at[e, 1]).wait()
        pltpu.make_async_copy(flow.at[e], flow_hbm.at[:, place], sems.at[e, 2]).wait()


def ends(edge_values, inner, band, left, right, up, down, outs):
    rows, cols = band.shape
    lanes = cols // 128
    return pl.pallas_call(
        ends_kernel,
        out_shape=out_shapes(rows, cols),
        in_specs=[VMEM] * 9 + [ANY] * 3,
        out_specs=[ANY] * 3,
        input_output_aliases={9: 0, 10: 1, 11: 2},
        scratch_shapes=[
            pltpu.VMEM((2, PAD, cols), F32),
            pltpu.VMEM((2, PAD, cols), F32),
            pltpu.VMEM((2, 8, PAD, cols), BF16),
            pltpu.VMEM((lanes + 2, 2 * (PAD + 16), 128), F32),
            pltpu.VMEM((2, 3 * PAD, cols + 256), BF16),
            pltpu.VMEM((lanes, 2 * (PAD + 16), 128), F32),
            pltpu.VMEM((lanes, 2 * (PAD + 16), 128), F32),
            pltpu.SemaphoreType.DMA((2, 3)),
        ],
        cost_estimate=cost(2 * PAD * cols),
        compiler_params=pltpu.CompilerParams(vmem_limit_bytes=16 * MIB),
        name="end_cells",
    )(
        edge_values, inner, band, left, right, up, down,
        across_taps(512, 256), down_taps(PAD), *outs,
    )


def swap(first, second, axis):
    devices = lax.axis_size(axis)
    received = []
    for start, value in enumerate((first, second)):
        pairs = [(i, i + 1) for i in range(start, devices - 1, 2)]
        received.append(lax.ppermute(value, axis, pairs + [(j, i) for i, j in pairs]))
    return received


def local(source_blocks, block_scale, block_list, block_count, row_weights, col_weights):
    block_list = block_list.T
    outgoing, source = gather(block_list, block_count, block_scale, source_blocks)
    edge = source_blocks.shape[1]
    arrived = lax.all_to_all(outgoing, "gy", split_axis=0, concat_axis=0, tiled=True)
    arrived = arrived.reshape(-1, edge, edge)
    weights = (row_weights, col_weights)
    edge_values, *messages = edges(source, arrived, *weights)
    beside = swap(*messages, "gx")
    inner, low, high, band, fall, strips, odd = middle(source, arrived, *weights, edge_values)
    messages = []
    for n in range(2):
        corners = [jnp.where(odd[:1] == n, side[-PAD:], side[:PAD]) for side in beside]
        messages.append(jnp.concatenate([strips[n], *corners], axis=1))
    ahead = swap(*messages, "gy")
    outs = main(edge_values, inner, low, high, fall, *beside, source)
    return tuple(ends(edge_values, inner, band, *beside, *ahead, outs))


def solution(mesh):
    in_specs = (
        P(("gx", "gy"), None, None),
        P(("gx", "gy")),
        P(),
        P(),
        P(("gx", "gy"), None, None),
        P(("gx", "gy"), None, None),
    )
    out_specs = (P("gy", "gx"), P("gy", "gx"), P(None, "gy", "gx"))
    return jax.shard_map(local, mesh=mesh, in_specs=in_specs, out_specs=out_specs, check_vma=False)
```
